32 devices in a mesh: tile: 8 (over y, x, core), depth: 4 (over z).
Axes of the slice: x: 2, y: 2, z: 4, core: 2. Of those that a mesh axis runs over, the one named last changes fastest.
Arguments:
- estimate: float32 [8, 256, 1024], P('depth', 'tile'), may hold values from 0.25 to 4
- views: bfloat16 [8, 8, 256, 1024], P(None, 'depth', 'tile'), may hold values from 0.19921875 to 5
- kernel_x: float32 [8, 31], replicated, may hold values from 0.01 to 1
- kernel_y: float32 [8, 31], replicated, may hold values from 0.01 to 1
- kernel_z: float32 [8, 31], replicated, may hold values from 0.01 to 1
- offsets: int32 [8], replicated, may hold values from 16 to 96
Outputs:
- updated: float32 [8, 256, 1024], P('depth', 'tile')
The draws below stay inside these ranges and needn't reach their ends.
All inputs are finite; a program needn't handle non-finite values.
Results may differ from the reference program's by a relative error of at most 0.0007.
Values may be sent and summed in bfloat16 or wider, within the bound.
No kernel may reach another device: no remote copies, remote signals or barrier semaphores. Data moves between devices by JAX's collectives and lax.ppermute only.
A program may use at most 128 MiB of HBM per device.

```python
import math
import jax
import jax.numpy as jnp
from jax import lax

XT = 32
NY = 1024
VIEWS = 8
TAPS = 31
NZ = 8
NX = 256
VX = 160


def set_ends(result, own_key, least, top_value):
    longest = result.shape.index(max(result.shape))
    spots = []
    for shift in (0, 1):
        where = [jax.random.randint(jax.random.fold_in(own_key, axis), (), 0, length) for axis, length in enumerate(result.shape)]
        where[longest] = (where[longest] + shift) % result.shape[longest]
        spots.append(tuple(where))
    return result.at[spots[0]].set(least).at[spots[1]].set(top_value)


def levels(own_key, shape, cuts, least, high):
    gain, own = 1.0, jax.random.fold_in(own_key, 6)
    for dim, shards_of in cuts:
        heights = jnp.exp(jax.random.uniform(jax.random.fold_in(own, dim), (shards_of,), jnp.float32, least / len(cuts), high / len(cuts)))
        gain = gain * jnp.repeat(heights, shape[dim] // shards_of).reshape([-1 if axis == dim else 1 for axis in range(len(shape))])
    return gain


def setup_inputs(seed: int = 0) -> dict:
    arg_keys = jax.random.split(jax.random.key(seed), 7)
    return {
        "estimate": jnp.clip(jnp.exp(math.log(4.0) - 2.7725887 * jax.random.uniform(arg_keys[0], (NZ, NX, NY), jnp.float32) ** levels(arg_keys[0], (NZ, NX, NY), ((0, 4), (1, 8)), -0.2, 0.2)), 0.25, 4.0),
        "views": jnp.clip(jnp.exp(math.log(5.0) - 3.2227897 * jax.random.uniform(arg_keys[1], (VIEWS, NZ, NX, NY), jnp.float32) ** levels(arg_keys[1], (VIEWS, NZ, NX, NY), ((1, 4), (2, 8)), -0.2, 0.2)), 0.19921875, 5.0).astype(jnp.bfloat16),
        "kernel_x": jnp.clip(jnp.exp(jax.random.uniform(arg_keys[2], (VIEWS, TAPS), jnp.float32, math.log(0.01), math.log(1.0))), 0.01, 1.0),
        "kernel_y": jnp.clip(jnp.exp(jax.random.uniform(arg_keys[3], (VIEWS, TAPS), jnp.float32, math.log(0.01), math.log(1.0))), 0.01, 1.0),
        "kernel_z": jnp.clip(jnp.exp(jax.random.uniform(arg_keys[4], (VIEWS, TAPS), jnp.float32, math.log(0.01), math.log(1.0))), 0.01, 1.0),
        "offsets": set_ends(jax.random.randint(arg_keys[5], (VIEWS,), XT // 2, NX - VX + 1), jax.random.fold_in(arg_keys[5], 1), XT // 2, NX - VX).astype(jnp.int32),
    }


def normalize(kernel):
    return kernel / jnp.sum(kernel, axis=1, keepdims=True)


def convolve(values, kernel, axis):
    margin = kernel.shape[0] // 2
    length = values.shape[axis]
    widths = [(0, 0)] * values.ndim
    widths[axis] = (margin, margin)
    padded = jnp.pad(values, widths)
    summed = jnp.zeros_like(values)
    for tap_index in range(kernel.shape[0]):
        summed = summed + kernel[tap_index] * lax.slice_in_dim(padded, tap_index, tap_index + length, axis=axis)
    return summed


def reference(estimate, views, kernel_x, kernel_y, kernel_z, offsets):
    kernel_x = normalize(kernel_x)
    kernel_y = normalize(kernel_y)
    kernel_z = normalize(kernel_z)
    row_ids = jnp.arange(NX, dtype=jnp.int32)
    covered = ((row_ids[None, :] >= offsets[:, None]) & (row_ids[None, :] < offsets[:, None] + VX)).astype(jnp.float32)
    coverage = jnp.sum(covered, axis=0)

    def per_view(view_index, accumulated):
        blurred = convolve(estimate, kernel_x[view_index], 1)
        blurred = convolve(blurred, kernel_y[view_index], 2)
        blurred = convolve(blurred, kernel_z[view_index], 0)
        recorded = views[view_index].astype(jnp.float32)
        correction = covered[view_index][None, :, None] * (recorded / blurred - 1.0)
        backward = convolve(correction, kernel_z[view_index][::-1], 0)
        backward = convolve(backward, kernel_y[view_index][::-1], 2)
        backward = convolve(backward, kernel_x[view_index][::-1], 1)
        return accumulated + backward

    summed = lax.fori_loop(0, VIEWS, per_view, jnp.zeros_like(estimate))
    return estimate * (1.0 + summed / jnp.maximum(coverage, 1.0)[None, :, None])
```

```python
import functools
import jax
import jax.numpy as jnp
from jax import lax
from jax.experimental import pallas as pl
from jax.experimental.pallas import tpu as pltpu
from jax.sharding import PartitionSpec as P

F32, BF16 = jnp.float32, jnp.bfloat16
HALO = 16
LANES = 128
WIDE = 256
VMEM_LIMIT = 40 * 1024 * 1024


def normalized(ref):
    return ref[...] / jnp.sum(ref[...], axis=1, keepdims=True)


def select_taps(index, kernel):
    total = jnp.zeros((kernel.shape[0],) + index.shape[1:], F32)
    for tap in range(kernel.shape[1]):
        total = total + jnp.where(index == tap, kernel[:, tap : tap + 1], 0.0)
    return total


def slanted(row, rows):
    spread = jnp.broadcast_to(row, (rows, row.shape[1]))
    return pltpu.roll(spread, 0, 1, stride=1, stride_axis=0)


def matrices_kernel(planes, strip, depth_ref, kx_ref, ky_ref, kz_ref, w_ref, wt_ref, tf_ref, tb_ref):
    views, taps = kx_ref.shape
    margin = taps // 2
    extent = strip + 2 * HALO
    depth = w_ref.shape[1] // (planes * extent)
    kx, ky, kz = normalized(kx_ref), normalized(ky_ref), normalized(kz_ref)
    lane = lax.broadcasted_iota(jnp.int32, (1, LANES), 1)
    x_row = select_taps(lane % extent - (HALO - margin), kx)
    near = jnp.where(lane < LANES // 2, lane, lane - LANES)
    forward_row = select_taps(margin - near, ky)
    backward_row = select_taps(margin + near, ky)
    column = lax.broadcasted_iota(jnp.int32, (1, w_ref.shape[1]), 1) // extent
    device = depth_ref[0]
    source = device + column // planes
    source = jnp.where(source >= depth, source - depth, source)
    plane = source * planes + column % planes
    z_rows = [select_taps(plane - (device * planes + own) + margin, kz) for own in range(planes)]
    for view in range(views):
        x_block = slanted(x_row[view : view + 1], strip)
        x_block = jnp.concatenate([x_block] * (w_ref.shape[1] // LANES), axis=1)
        for own in range(planes):
            first = (view * planes + own) * strip
            block = x_block * z_rows[own][view : view + 1]
            w_ref[first : first + strip, :] = block.astype(BF16)
    wt_ref[...] = w_ref[...].astype(F32).T.astype(BF16)
    i = lax.broadcasted_iota(jnp.int32, (LANES, LANES), 0)
    j = lax.broadcasted_iota(jnp.int32, (LANES, LANES), 1)
    zeros = jnp.zeros((LANES, LANES), BF16)
    for view in range(views):
        for row, out in ((forward_row, tf_ref), (backward_row, tb_ref)):
            circle = slanted(row[view : view + 1], LANES)
            middle = jnp.where(jnp.abs(j - i) < LANES // 2, circle, 0.0).astype(BF16)
            earlier = jnp.where(i - j > LANES // 2, circle, 0.0).astype(BF16)
            later = jnp.where(j - i > LANES // 2, circle, 0.0).astype(BF16)
            grid = ((earlier, zeros), (middle, earlier), (later, middle), (zeros, later))
            for a, blocks in enumerate(grid):
                for b, block in enumerate(blocks):
                    out[view, a * LANES : (a + 1) * LANES, b * LANES : (b + 1) * LANES] = block


def write_coded(out_ref, where, values):
    pick = values.shape[-1] // 2 - LANES
    base = values[..., pick : pick + LANES].astype(BF16)
    wide = base.astype(F32)
    for first in range(0, values.shape[-1], LANES):
        part = values[..., first : first + LANES]
        part = base if first == pick else (part - wide).astype(BF16)
        out_ref[where + (slice(first, first + LANES),)] = part


def decoded(values, first):
    pick = values.shape[-1] // 2 - LANES
    base = values[..., pick : pick + LANES].astype(F32)
    if first == pick:
        return base
    return base + values[..., first : first + LANES].astype(F32)


def main_kernel(planes, strip, view_rows, place_ref, offsets_ref, *refs):
    (all_ref, before_ref, after_ref, views_ref, w_ref, wt_ref, tf_ref, tb_ref,
     core_ref, top_ref, bottom_ref, ext_ref, pad_ref, back_ref, deep_ref) = refs
    views = offsets_ref.shape[0]
    extent = strip + 2 * HALO
    columns = all_ref.shape[-1]
    group = planes * strip
    for p in range(all_ref.shape[0]):
        first = p * extent
        ext_ref[first : first + HALO, :] = before_ref[p]
        ext_ref[first + HALO : first + HALO + strip, :] = all_ref[p]
        ext_ref[first + HALO + strip : first + extent, :] = after_ref[p]
    for pad in (pad_ref, back_ref):
        pad[:, :LANES] = jnp.zeros((pad.shape[0], LANES), BF16)
        pad[:, LANES + columns :] = jnp.zeros((pad.shape[0], LANES), BF16)
    for first in range(0, columns, WIDE):
        block = jnp.dot(w_ref[...], ext_ref[:, first : first + WIDE], preferred_element_type=F32)
        pad_ref[:, LANES + first : LANES + first + WIDE] = block.astype(BF16)
    row = place_ref[0] + lax.broadcasted_iota(jnp.int32, (group, WIDE), 0) % strip
    starts = range(0, columns, WIDE)

    def windows(pad, rows):
        return jnp.concatenate([pad[rows, first : first + WIDE + 2 * LANES] for first in starts], axis=0)

    for view in range(views):
        rows = slice(view * group, (view + 1) * group)
        low = offsets_ref[view]
        inside = (row >= low) & (row < low + view_rows)
        blurred = jnp.dot(windows(pad_ref, rows), tf_ref[view], preferred_element_type=F32)
        for n, first in enumerate(starts):
            part = blurred[n * group : (n + 1) * group]
            seen = views_ref[rows, first : first + WIDE].astype(F32)
            correction = jnp.where(inside, seen / part - 1.0, 0.0)
            back_ref[rows, LANES + first : LANES + first + WIDE] = correction.astype(BF16)
        backward = jnp.dot(windows(back_ref, rows), tb_ref[view], preferred_element_type=F32)
        for n, first in enumerate(starts):
            deep_ref[rows, first : first + WIDE] = backward[n * group : (n + 1) * group].astype(BF16)
    for p in range(core_ref.shape[0]):
        part = jnp.dot(wt_ref[p * extent : (p + 1) * extent], deep_ref[...], preferred_element_type=F32)
        core_ref[p] = part[HALO : HALO + strip]
        write_coded(top_ref, (p, slice(None)), part[:HALO])
        write_coded(bottom_ref, (p, slice(None)), part[HALO + strip :])


def join_kernel(planes, core_ref, above_ref, below_ref, own_ref, *sends):
    strip = core_ref.shape[1]
    columns = core_ref.shape[2]
    for p in range(core_ref.shape[0]):
        above, below = above_ref[p], below_ref[p]
        parts = []
        for first in range(0, columns, LANES):
            lanes = slice(first, first + LANES)
            tail = core_ref[p, strip - HALO :, lanes] + decoded(below, first)
            head = core_ref[p, :HALO, lanes] + decoded(above, first)
            inner = [core_ref[p, HALO : strip - HALO, lanes]] if strip > 2 * HALO else []
            parts.append(jnp.concatenate([head, *inner, tail], axis=0))
        whole = jnp.concatenate(parts, axis=1)
        if p < planes:
            own_ref[p] = whole
        else:
            write_coded(sends[p // planes - 1], (p % planes, slice(None)), whole)


def update_kernel(view_rows, place_ref, offsets_ref, estimate_ref, own_ref, *refs):
    received, out_ref = refs[:-1], refs[-1]
    planes, strip, columns = estimate_ref.shape
    row = place_ref[0] + lax.broadcasted_iota(jnp.int32, (strip, LANES), 0)
    coverage = jnp.zeros((strip, LANES), F32)
    for view in range(offsets_ref.shape[0]):
        low = offsets_ref[view]
        coverage = coverage + jnp.where((row >= low) & (row < low + view_rows), 1.0, 0.0)
    scale = 1.0 / jnp.maximum(coverage, 1.0)
    for p in range(planes):
        for first in range(0, columns, LANES):
            lanes = slice(first, first + LANES)
            summed = own_ref[p, :, lanes]
            for ref in received:
                summed = summed + decoded(ref[p], first)
            out_ref[p, :, lanes] = estimate_ref[p, :, lanes] * (1.0 + summed * scale)


def call(body, outs, scalars, arrays, scratch=(), flops=0, moved=0):
    return pl.pallas_call(
        body,
        out_shape=outs,
        in_specs=[pl.BlockSpec(memory_space=pltpu.SMEM)] * scalars
        + [pl.BlockSpec(memory_space=pltpu.VMEM)] * arrays,
        out_specs=jax.tree.map(lambda _: pl.BlockSpec(memory_space=pltpu.VMEM), outs),
        scratch_shapes=list(scratch),
        compiler_params=pltpu.CompilerParams(vmem_limit_bytes=VMEM_LIMIT),
        cost_estimate=pl.CostEstimate(flops=flops, bytes_accessed=moved, transcendentals=0),
    )


def shards(estimate, views, kernel_x, kernel_y, kernel_z, offsets):
    shape = jax.ShapeDtypeStruct
    depth, tiles = lax.axis_size("depth"), lax.axis_size("tile")
    planes, strip, columns = estimate.shape
    count = views.shape[0]
    extent = strip + 2 * HALO
    rows = count * planes * strip
    deep = depth * planes
    inner = deep * extent
    view_rows = 5 * strip * tiles // 8
    place = (lax.axis_index("tile") * strip).astype(jnp.int32).reshape(1)
    device = lax.axis_index("depth").astype(jnp.int32).reshape(1)

    def turned(array, shift):
        return lax.ppermute(array, "depth", [(i, (i - shift) % depth) for i in range(depth)])

    up = [(i, i + 1) for i in range(tiles - 1)]
    down = [(j, i) for i, j in up]

    own = estimate.astype(BF16)
    chunks = [own] + [turned(own, shift) for shift in range(1, depth)]
    w, wt, tf, tb = call(
        functools.partial(matrices_kernel, planes, strip),
        (shape((rows, inner), BF16), shape((inner, rows), BF16))
        + (shape((count, WIDE + 2 * LANES, WIDE), BF16),) * 2,
        1, 3, flops=10**8, moved=5 * 2**20,
    )(device, kernel_x, kernel_y, kernel_z)
    gathered = jnp.concatenate(chunks, axis=0)
    before = lax.ppermute(gathered[:, strip - HALO :], "tile", up)
    after = lax.ppermute(gathered[:, :HALO], "tile", down)
    halo = shape((deep, HALO, columns), BF16)
    core, top, bottom = call(
        functools.partial(main_kernel, planes, strip, view_rows),
        (shape((deep, strip, columns), F32), halo, halo),
        2, 8,
        scratch=(
            pltpu.VMEM((inner, columns), BF16),
            pltpu.VMEM((rows, columns + 2 * LANES), BF16),
            pltpu.VMEM((rows, columns + 2 * LANES), BF16),
            pltpu.VMEM((rows, columns), BF16),
        ),
        flops=2 * 10**9, moved=10 * 2**20,
    )(place, offsets, gathered, before, after, views.reshape(rows, columns), w, wt, tf, tb)
    below = lax.ppermute(top, "tile", down)
    above = lax.ppermute(bottom, "tile", up)
    block = (planes, strip, columns)
    own_sum, *sends = call(
        functools.partial(join_kernel, planes),
        (shape(block, F32),) + (shape(block, BF16),) * (depth - 1),
        0, 3, flops=10**6, moved=3 * 2**20,
    )(core, above, below)
    received = [turned(send, depth - 1 - n) for n, send in enumerate(sends)]
    return call(
        functools.partial(update_kernel, view_rows),
        shape(block, F32),
        2, 2 + len(received), flops=10**6, moved=2**20,
    )(place, offsets, estimate, own_sum, *received)


def solution(mesh):
    in_specs = (P("depth", "tile", None), P(None, "depth", "tile", None), P(), P(), P(), P())
    out_specs = P("depth", "tile", None)
    return jax.shard_map(shards, mesh=mesh, in_specs=in_specs, out_specs=out_specs, check_vma=False)
```

```python
import functools
import jax
import jax.numpy as jnp
from jax import lax
from jax.experimental import pallas as pl
from jax.experimental.pallas import tpu as pltpu
from jax.sharding import PartitionSpec as P

F32, BF16 = jnp.float32, jnp.bfloat16
HALO = 16
LANES = 128
WIDE = 256
VMEM_LIMIT = 40 * 1024 * 1024


def normalized(ref):
    return ref[...] / jnp.sum(ref[...], axis=1, keepdims=True)


def select_taps(index, kernel):
    total = jnp.zeros((kernel.shape[0],) + index.shape[1:], F32)
    for tap in range(kernel.shape[1]):
        total = total + jnp.where(index == tap, kernel[:, tap : tap + 1], 0.0)
    return total


def slanted(row, rows):
    spread = jnp.broadcast_to(row, (rows, row.shape[1]))
    return pltpu.roll(spread, 0, 1, stride=1, stride_axis=0)


def matrices_kernel(planes, strip, order, device_ref, kx_ref, ky_ref, kz_ref, w_ref, tf_ref, tb_ref, *wt_refs):
    views, taps = kx_ref.shape
    margin = taps // 2
    extent = strip + 2 * HALO
    kx, ky, kz = normalized(kx_ref), normalized(ky_ref), normalized(kz_ref)
    lane = lax.broadcasted_iota(jnp.int32, (1, LANES), 1)
    x_row = select_taps(lane % extent - (HALO - margin), kx)
    near = jnp.where(lane < LANES // 2, lane, lane - LANES)
    forward_row = select_taps(margin - near, ky)
    backward_row = select_taps(margin + near, ky)
    column = lax.broadcasted_iota(jnp.int32, (1, w_ref.shape[1]), 1) // extent
    device, odd = device_ref[0], device_ref[1] == 1
    step = jnp.zeros_like(column)
    for n, shift in enumerate(order):
        step = jnp.where(column // planes == n, shift, step)
    plane = (device ^ step) * planes + column % planes
    spot = lax.broadcasted_iota(jnp.int32, (strip, LANES), 1) % extent
    swap_first = jnp.logical_and(spot < HALO, jnp.logical_not(odd))
    swap_last = jnp.logical_and(spot >= extent - HALO, jnp.logical_not(odd))
    z_rows = [select_taps(plane - (device * planes + own) + margin, kz) for own in range(planes)]
    for view in range(views):
        x_block = slanted(x_row[view : view + 1], strip)
        turn = extent - HALO
        x_block = jnp.where(
            swap_first,
            pltpu.roll(x_block, LANES - turn, 1),
            jnp.where(swap_last, pltpu.roll(x_block, turn, 1), x_block),
        )
        x_block = jnp.concatenate([x_block] * (w_ref.shape[1] // LANES), axis=1)
        for own in range(planes):
            first = (view * planes + own) * strip
            block = x_block * z_rows[own][view : view + 1]
            w_ref[first : first + strip, :] = block.astype(BF16)
    first = 0
    for wt_ref in wt_refs:
        last = first + wt_ref.shape[0]
        wt_ref[...] = w_ref[:, first:last].astype(F32).T.astype(BF16)
        first = last
    i = lax.broadcasted_iota(jnp.int32, (LANES, LANES), 0)
    j = lax.broadcasted_iota(jnp.int32, (LANES, LANES), 1)
    zeros = jnp.zeros((LANES, LANES), BF16)
    for view in range(views):
        for row, out in ((forward_row, tf_ref), (backward_row, tb_ref)):
            circle = slanted(row[view : view + 1], LANES)
            middle = jnp.where(jnp.abs(j - i) < LANES // 2, circle, 0.0).astype(BF16)
            earlier = jnp.where(i - j > LANES // 2, circle, 0.0).astype(BF16)
            later = jnp.where(j - i > LANES // 2, circle, 0.0).astype(BF16)
            grid = ((earlier, zeros), (middle, earlier), (later, middle), (zeros, later))
            for a, blocks in enumerate(grid):
                for b, block in enumerate(blocks):
                    out[view, a * LANES : (a + 1) * LANES, b * LANES : (b + 1) * LANES] = block


def write_coded(out_ref, where, values):
    pick = values.shape[-1] // 2 - LANES
    base = values[..., pick : pick + LANES].astype(BF16)
    wide = base.astype(F32)
    for first in range(0, values.shape[-1], LANES):
        part = values[..., first : first + LANES]
        part = base if first == pick else (part - wide).astype(BF16)
        out_ref[where + (slice(first, first + LANES),)] = part


def decoded(values, first):
    pick = values.shape[-1] // 2 - LANES
    base = values[..., pick : pick + LANES].astype(F32)
    if first == pick:
        return base
    return base + values[..., first : first + LANES].astype(F32)


def pack_kernel(device_ref, *refs):
    one_ref, two_ref = refs[-2:]
    planes, strip = refs[0].shape[:2]
    odd = device_ref[1]
    one = pl.multiple_of((1 - odd) * (strip - HALO), HALO)
    two = pl.multiple_of(odd * (strip - HALO), HALO)
    for p in range(one_ref.shape[0]):
        chunk = refs[p // planes]
        one_ref[p] = chunk[p % planes, pl.ds(one, HALO), :]
        two_ref[p] = chunk[p % planes, pl.ds(two, HALO), :]


def project(planes, extent, wt_ref, deep_ref, core_ref, first_ref, second_ref):
    for p in range(core_ref.shape[0]):
        part = jnp.dot(wt_ref[p * extent : (p + 1) * extent], deep_ref[...], preferred_element_type=F32)
        core_ref[p] = part[HALO : extent - HALO]
        write_coded(first_ref, (p, slice(None)), part[:HALO])
        write_coded(second_ref, (p, slice(None)), part[extent - HALO :])


def main_kernel(planes, strip, view_rows, sizes, place_ref, offsets_ref, *refs):
    groups = len(sizes)
    chunks, refs = refs[: sum(sizes)], refs[sum(sizes) :]
    halos, refs = refs[: 2 * groups], refs[2 * groups :]
    views_ref, w_ref, wt_ref, tf_ref, tb_ref = refs[:5]
    deep_ref, *outs = refs[5:-3]
    ext_ref, pad_ref, back_ref = refs[-3:]
    views = offsets_ref.shape[0]
    extent = strip + 2 * HALO
    columns = ext_ref.shape[-1]
    group = planes * strip
    where = [(g, p) for g, size in enumerate(sizes) for p in range(size * planes)]
    for n, (g, p) in enumerate(where):
        first = n * extent
        ext_ref[first : first + HALO, :] = halos[2 * g][p]
        ext_ref[first + HALO : first + HALO + strip, :] = chunks[n // planes][n % planes]
        ext_ref[first + HALO + strip : first + extent, :] = halos[2 * g + 1][p]
    for pad in (pad_ref, back_ref):
        pad[:, :LANES] = jnp.zeros((pad.shape[0], LANES), BF16)
        pad[:, LANES + columns :] = jnp.zeros((pad.shape[0], LANES), BF16)
    for first in range(0, columns, WIDE):
        block = jnp.dot(w_ref[...], ext_ref[:, first : first + WIDE], preferred_element_type=F32)
        pad_ref[:, LANES + first : LANES + first + WIDE] = block.astype(BF16)
    row = place_ref[0] + lax.broadcasted_iota(jnp.int32, (group, WIDE), 0) % strip
    starts = range(0, columns, WIDE)

    def windows(pad, rows):
        return jnp.concatenate([pad[rows, first : first + WIDE + 2 * LANES] for first in starts], axis=0)

    for view in range(views):
        rows = slice(view * group, (view + 1) * group)
        low = offsets_ref[view]
        inside = (row >= low) & (row < low + view_rows)
        blurred = jnp.dot(windows(pad_ref, rows), tf_ref[view], preferred_element_type=F32)
        for n, first in enumerate(starts):
            part = blurred[n * group : (n + 1) * group]
            seen = views_ref[rows, first : first + WIDE].astype(F32)
            correction = jnp.where(inside, seen / part - 1.0, 0.0)
            back_ref[rows, LANES + first : LANES + first + WIDE] = correction.astype(BF16)
        backward = jnp.dot(windows(back_ref, rows), tb_ref[view], preferred_element_type=F32)
        for n, first in enumerate(starts):
            deep_ref[rows, first : first + WIDE] = backward[n * group : (n + 1) * group].astype(BF16)
    project(planes, extent, wt_ref, deep_ref, *outs)


def join_kernel(planes, kept, device_ref, core_ref, first_ref, second_ref, *refs):
    strip = core_ref.shape[1]
    columns = core_ref.shape[2]
    odd = device_ref[1] == 1
    outs = refs[-(core_ref.shape[0] // planes) :]
    for p in range(core_ref.shape[0]):
        one, two = first_ref[p], second_ref[p]
        parts = []
        for first in range(0, columns, LANES):
            lanes = slice(first, first + LANES)
            inside, outside = decoded(one, first), decoded(two, first)
            head = core_ref[p, :HALO, lanes] + jnp.where(odd, inside, outside)
            tail = core_ref[p, strip - HALO :, lanes] + jnp.where(odd, outside, inside)
            middle = [core_ref[p, HALO : strip - HALO, lanes]] if strip > 2 * HALO else []
            parts.append(jnp.concatenate([head, *middle, tail], axis=0))
        whole = jnp.concatenate(parts, axis=1)
        out_ref = outs[p // planes]
        if p // planes == kept:
            out_ref[p % planes] = whole
        else:
            write_coded(out_ref, (p % planes, slice(None)), whole)


def update_kernel(view_rows, place_ref, offsets_ref, estimate_ref, own_ref, *refs):
    received, out_ref = refs[:-1], refs[-1]
    planes, strip, columns = estimate_ref.shape
    row = place_ref[0] + lax.broadcasted_iota(jnp.int32, (strip, LANES), 0)
    coverage = jnp.zeros((strip, LANES), F32)
    for view in range(offsets_ref.shape[0]):
        low = offsets_ref[view]
        coverage = coverage + jnp.where((row >= low) & (row < low + view_rows), 1.0, 0.0)
    scale = 1.0 / jnp.maximum(coverage, 1.0)
    for p in range(planes):
        for first in range(0, columns, LANES):
            lanes = slice(first, first + LANES)
            summed = own_ref[p, :, lanes]
            for ref in received:
                summed = summed + decoded(ref[p], first)
            out_ref[p, :, lanes] = estimate_ref[p, :, lanes] * (1.0 + summed * scale)


def call(body, outs, scalars, arrays, scratch=(), after=0, flops=0, moved=0):
    return pl.pallas_call(
        body,
        out_shape=outs,
        in_specs=[pl.BlockSpec(memory_space=pltpu.SMEM)] * scalars
        + [pl.BlockSpec(memory_space=pltpu.VMEM)] * arrays
        + [pl.BlockSpec(memory_space=pl.ANY)] * after,
        out_specs=jax.tree.map(lambda _: pl.BlockSpec(memory_space=pltpu.VMEM), outs),
        scratch_shapes=list(scratch),
        compiler_params=pltpu.CompilerParams(vmem_limit_bytes=VMEM_LIMIT),
        cost_estimate=pl.CostEstimate(flops=flops, bytes_accessed=moved, transcendentals=0),
    )


def shards(estimate, views, kernel_x, kernel_y, kernel_z, offsets):
    shape = jax.ShapeDtypeStruct
    depth, tiles = lax.axis_size("depth"), lax.axis_size("tile")
    planes, strip, columns = estimate.shape
    count = views.shape[0]
    extent = strip + 2 * HALO
    rows = count * planes * strip
    inner = depth * planes * extent
    view_rows = 5 * strip * tiles // 8
    tile = lax.axis_index("tile").astype(jnp.int32)
    odd = tile % 2
    place = (tile * strip).reshape(1)
    device = jnp.stack([lax.axis_index("depth").astype(jnp.int32), odd])
    groups = [list(range(depth // 2)), list(range(depth // 2, depth))]
    order = sum(groups, [])
    sizes = [len(group) for group in groups]

    def across(array, step):
        return lax.ppermute(array, "depth", [(i, i ^ step) for i in range(depth)])

    pairings = (
        [(i, i ^ 1) for i in range(tiles)],
        [(i, i - 1 + 2 * (i % 2)) for i in range(1, tiles - 1)],
    )

    def neighbours(first, second):
        second = lax.ppermute(second, "tile", pairings[1])
        return lax.ppermute(first, "tile", pairings[0]), second

    own = estimate.astype(BF16)
    chunks = {0: own}
    for step in reversed(order[1:]):
        chunks[step] = across(own, step)
    w, tf, tb, *wts = call(
        functools.partial(matrices_kernel, planes, strip, order),
        (shape((rows, inner), BF16),) + (shape((count, WIDE + 2 * LANES, WIDE), BF16),) * 2
        + tuple(shape((size * planes * extent, rows), BF16) for size in sizes),
        1, 3, flops=10**8, moved=5 * 2**20,
    )(device, kernel_x, kernel_y, kernel_z)
    halos, packed = [], []
    for group in groups:
        halo = shape((len(group) * planes, HALO, columns), BF16)
        packed = call(
            pack_kernel, (halo, halo), 1, len(group), after=len(packed), flops=10**5, moved=2**20
        )(device, *[chunks[step] for step in group], *packed)
        halos += neighbours(*packed)

    def outs_of(size):
        halo = shape((size * planes, HALO, columns), BF16)
        return (shape((size * planes, strip, columns), F32), halo, halo)

    deep = shape((rows, columns), BF16)
    deep, *far = call(
        functools.partial(main_kernel, planes, strip, view_rows, sizes),
        (deep,) + outs_of(sizes[1]),
        2, depth + len(halos) + 5,
        scratch=(
            pltpu.VMEM((inner, columns), BF16),
            pltpu.VMEM((rows, columns + 2 * LANES), BF16),
            pltpu.VMEM((rows, columns + 2 * LANES), BF16),
        ),
        flops=2 * 10**9, moved=10 * 2**20,
    )(place, offsets, *[chunks[step] for step in order], *halos, views.reshape(rows, columns), w, wts[1], tf, tb)
    far[1:] = neighbours(*far[1:])
    near = call(
        functools.partial(project, planes, extent),
        outs_of(sizes[0]), 0, 2, flops=3 * 10**8, moved=3 * 2**20,
    )(wts[0], deep)
    near = [near[0], *neighbours(*near[1:])]
    block = (planes, strip, columns)
    far_sums = call(
        functools.partial(join_kernel, planes, None),
        (shape(block, BF16),) * sizes[1],
        1, 3, flops=10**6, moved=3 * 2**20,
    )(device, *far)
    received = [across(total, step) for step, total in zip(groups[1], far_sums)]
    own_sum, *near_sums = call(
        functools.partial(join_kernel, planes, 0),
        (shape(block, F32),) + (shape(block, BF16),) * (sizes[0] - 1),
        1, 3, after=1, flops=10**6, moved=3 * 2**20,
    )(device, *near, far_sums[0])
    received += [across(total, step) for step, total in zip(groups[0][1:], near_sums)]
    return call(
        functools.partial(update_kernel, view_rows),
        shape(block, F32),
        2, 1 + depth, flops=10**6, moved=2**20,
    )(place, offsets, estimate, own_sum, *received)


def solution(mesh):
    in_specs = (P("depth", "tile", None), P(None, "depth", "tile", None), P(), P(), P(), P())
    out_specs = P("depth", "tile", None)
    return jax.shard_map(shards, mesh=mesh, in_specs=in_specs, out_specs=out_specs, check_vma=False)
```

```python
import functools
import jax
import jax.numpy as jnp
from jax import lax
from jax.experimental import pallas as pl
from jax.experimental.pallas import tpu as pltpu
from jax.sharding import PartitionSpec as P

F32, BF16 = jnp.float32, jnp.bfloat16
HALO = 16
LANES = 128
WIDE = 256
VMEM_LIMIT = 40 * 1024 * 1024


def normalized(ref):
    return ref[...] / jnp.sum(ref[...], axis=1, keepdims=True)


def select_taps(index, kernel):
    total = jnp.zeros((kernel.shape[0],) + index.shape[1:], F32)
    for tap in range(kernel.shape[1]):
        total = total + jnp.where(index == tap, kernel[:, tap : tap + 1], 0.0)
    return total


def slanted(row, rows):
    spread = jnp.broadcast_to(row, (rows, row.shape[1]))
    return pltpu.roll(spread, 0, 1, stride=1, stride_axis=0)


def matrices_kernel(planes, strip, depth_ref, kx_ref, ky_ref, kz_ref, w_ref, wt_ref, tf_ref, tb_ref):
    views, taps = kx_ref.shape
    margin = taps // 2
    extent = strip + 2 * HALO
    depth = w_ref.shape[1] // (planes * extent)
    kx, ky, kz = normalized(kx_ref), normalized(ky_ref), normalized(kz_ref)
    lane = lax.broadcasted_iota(jnp.int32, (1, LANES), 1)
    x_row = select_taps(lane % extent - (HALO - margin), kx)
    near = jnp.where(lane < LANES // 2, lane, lane - LANES)
    forward_row = select_taps(margin - near, ky)
    backward_row = select_taps(margin + near, ky)
    column = lax.broadcasted_iota(jnp.int32, (1, w_ref.shape[1]), 1) // extent
    device = depth_ref[0]
    source = device + column // planes
    source = jnp.where(source >= depth, source - depth, source)
    plane = source * planes + column % planes
    z_rows = [select_taps(plane - (device * planes + own) + margin, kz) for own in range(planes)]
    for view in range(views):
        x_block = slanted(x_row[view : view + 1], strip)
        x_block = jnp.concatenate([x_block] * (w_ref.shape[1] // LANES), axis=1)
        for own in range(planes):
            first = (view * planes + own) * strip
            block = x_block * z_rows[own][view : view + 1]
            w_ref[first : first + strip, :] = block.astype(BF16)
    wt_ref[...] = w_ref[...].astype(F32).T.astype(BF16)
    i = lax.broadcasted_iota(jnp.int32, (LANES, LANES), 0)
    j = lax.broadcasted_iota(jnp.int32, (LANES, LANES), 1)
    zeros = jnp.zeros((LANES, LANES), BF16)
    for view in range(views):
        for row, out in ((forward_row, tf_ref), (backward_row, tb_ref)):
            circle = slanted(row[view : view + 1], LANES)
            middle = jnp.where(jnp.abs(j - i) < LANES // 2, circle, 0.0).astype(BF16)
            earlier = jnp.where(i - j > LANES // 2, circle, 0.0).astype(BF16)
            later = jnp.where(j - i > LANES // 2, circle, 0.0).astype(BF16)
            grid = ((earlier, zeros), (middle, earlier), (later, middle), (zeros, later))
            for a, blocks in enumerate(grid):
                for b, block in enumerate(blocks):
                    out[view, a * LANES : (a + 1) * LANES, b * LANES : (b + 1) * LANES] = block


def write_coded(out_ref, where, values):
    pick = values.shape[-1] // 2 - LANES
    base = values[..., pick : pick + LANES].astype(BF16)
    wide = base.astype(F32)
    for first in range(0, values.shape[-1], LANES):
        part = values[..., first : first + LANES]
        part = base if first == pick else (part - wide).astype(BF16)
        out_ref[where + (slice(first, first + LANES),)] = part


def decoded(values, first):
    pick = values.shape[-1] // 2 - LANES
    base = values[..., pick : pick + LANES].astype(F32)
    if first == pick:
        return base
    return base + values[..., first : first + LANES].astype(F32)


def main_kernel(planes, strip, view_rows, place_ref, device_ref, offsets_ref, *refs):
    (all_ref, before_ref, after_ref, views_ref, w_ref, wt_ref, tf_ref, tb_ref,
     core_ref, top_ref, bottom_ref, ext_ref, pad_ref, back_ref, deep_ref) = refs
    views = offsets_ref.shape[0]
    extent = strip + 2 * HALO
    columns = all_ref.shape[-1]
    group = planes * strip
    depth = all_ref.shape[0] // planes
    for p in range(all_ref.shape[0]):
        first = p * extent
        source = device_ref[0] + p // planes
        plane = jnp.where(source >= depth, source - depth, source) * planes + p % planes
        ext_ref[first : first + HALO, :] = before_ref[plane]
        ext_ref[first + HALO : first + HALO + strip, :] = all_ref[plane]
        ext_ref[first + HALO + strip : first + extent, :] = after_ref[plane]
    for pad in (pad_ref, back_ref):
        pad[:, :LANES] = jnp.zeros((pad.shape[0], LANES), BF16)
        pad[:, LANES + columns :] = jnp.zeros((pad.shape[0], LANES), BF16)
    for first in range(0, columns, WIDE):
        block = jnp.dot(w_ref[...], ext_ref[:, first : first + WIDE], preferred_element_type=F32)
        pad_ref[:, LANES + first : LANES + first + WIDE] = block.astype(BF16)
    row = place_ref[0] + lax.broadcasted_iota(jnp.int32, (group, WIDE), 0) % strip
    starts = range(0, columns, WIDE)

    def windows(pad, rows):
        return jnp.concatenate([pad[rows, first : first + WIDE + 2 * LANES] for first in starts], axis=0)

    for view in range(views):
        rows = slice(view * group, (view + 1) * group)
        low = offsets_ref[view]
        inside = (row >= low) & (row < low + view_rows)
        blurred = jnp.dot(windows(pad_ref, rows), tf_ref[view], preferred_element_type=F32)
        for n, first in enumerate(starts):
            part = blurred[n * group : (n + 1) * group]
            seen = views_ref[rows, first : first + WIDE].astype(F32)
            correction = jnp.where(inside, seen / part - 1.0, 0.0)
            back_ref[rows, LANES + first : LANES + first + WIDE] = correction.astype(BF16)
        backward = jnp.dot(windows(back_ref, rows), tb_ref[view], preferred_element_type=F32)
        for n, first in enumerate(starts):
            deep_ref[rows, first : first + WIDE] = backward[n * group : (n + 1) * group].astype(BF16)
    for p in range(core_ref.shape[0]):
        part = jnp.dot(wt_ref[p * extent : (p + 1) * extent], deep_ref[...], preferred_element_type=F32)
        core_ref[p] = part[HALO : HALO + strip]
        write_coded(top_ref, (p, slice(None)), part[:HALO])
        write_coded(bottom_ref, (p, slice(None)), part[HALO + strip :])


def join_kernel(planes, core_ref, above_ref, below_ref, own_ref, *sends):
    strip = core_ref.shape[1]
    columns = core_ref.shape[2]
    for p in range(core_ref.shape[0]):
        above, below = above_ref[p], below_ref[p]
        parts = []
        for first in range(0, columns, LANES):
            lanes = slice(first, first + LANES)
            tail = core_ref[p, strip - HALO :, lanes] + decoded(below, first)
            head = core_ref[p, :HALO, lanes] + decoded(above, first)
            inner = [core_ref[p, HALO : strip - HALO, lanes]] if strip > 2 * HALO else []
            parts.append(jnp.concatenate([head, *inner, tail], axis=0))
        whole = jnp.concatenate(parts, axis=1)
        if p < planes:
            own_ref[p] = whole
        else:
            write_coded(sends[p // planes - 1], (p % planes, slice(None)), whole)


def update_kernel(view_rows, place_ref, offsets_ref, estimate_ref, own_ref, *refs):
    received, out_ref = refs[:-1], refs[-1]
    planes, strip, columns = estimate_ref.shape
    row = place_ref[0] + lax.broadcasted_iota(jnp.int32, (strip, LANES), 0)
    coverage = jnp.zeros((strip, LANES), F32)
    for view in range(offsets_ref.shape[0]):
        low = offsets_ref[view]
        coverage = coverage + jnp.where((row >= low) & (row < low + view_rows), 1.0, 0.0)
    scale = 1.0 / jnp.maximum(coverage, 1.0)
    for p in range(planes):
        for first in range(0, columns, LANES):
            lanes = slice(first, first + LANES)
            summed = own_ref[p, :, lanes]
            for ref in received:
                summed = summed + decoded(ref[p], first)
            out_ref[p, :, lanes] = estimate_ref[p, :, lanes] * (1.0 + summed * scale)


def call(body, outs, scalars, arrays, scratch=(), flops=0, moved=0):
    return pl.pallas_call(
        body,
        out_shape=outs,
        in_specs=[pl.BlockSpec(memory_space=pltpu.SMEM)] * scalars
        + [pl.BlockSpec(memory_space=pltpu.VMEM)] * arrays,
        out_specs=jax.tree.map(lambda _: pl.BlockSpec(memory_space=pltpu.VMEM), outs),
        scratch_shapes=list(scratch),
        compiler_params=pltpu.CompilerParams(vmem_limit_bytes=VMEM_LIMIT),
        cost_estimate=pl.CostEstimate(flops=flops, bytes_accessed=moved, transcendentals=0),
    )


def shards(estimate, views, kernel_x, kernel_y, kernel_z, offsets):
    shape = jax.ShapeDtypeStruct
    depth, tiles = lax.axis_size("depth"), lax.axis_size("tile")
    planes, strip, columns = estimate.shape
    count = views.shape[0]
    extent = strip + 2 * HALO
    rows = count * planes * strip
    deep = depth * planes
    inner = deep * extent
    view_rows = 5 * strip * tiles // 8
    place = (lax.axis_index("tile") * strip).astype(jnp.int32).reshape(1)
    device = lax.axis_index("depth").astype(jnp.int32).reshape(1)

    def turned(array, shift):
        return lax.ppermute(array, "depth", [(i, (i - shift) % depth) for i in range(depth)])

    up = [(i, i + 1) for i in range(tiles - 1)]
    down = [(j, i) for i, j in up]

    own = estimate.astype(BF16)
    gathered = lax.all_gather(own, "depth", axis=0, tiled=True)
    w, wt, tf, tb = call(
        functools.partial(matrices_kernel, planes, strip),
        (shape((rows, inner), BF16), shape((inner, rows), BF16))
        + (shape((count, WIDE + 2 * LANES, WIDE), BF16),) * 2,
        1, 3, flops=10**8, moved=5 * 2**20,
    )(device, kernel_x, kernel_y, kernel_z)
    before = lax.ppermute(gathered[:, strip - HALO :], "tile", up)
    after = lax.ppermute(gathered[:, :HALO], "tile", down)
    halo = shape((deep, HALO, columns), BF16)
    core, top, bottom = call(
        functools.partial(main_kernel, planes, strip, view_rows),
        (shape((deep, strip, columns), F32), halo, halo),
        3, 8,
        scratch=(
            pltpu.VMEM((inner, columns), BF16),
            pltpu.VMEM((rows, columns + 2 * LANES), BF16),
            pltpu.VMEM((rows, columns + 2 * LANES), BF16),
            pltpu.VMEM((rows, columns), BF16),
        ),
        flops=2 * 10**9, moved=10 * 2**20,
    )(place, device, offsets, gathered, before, after, views.reshape(rows, columns), w, wt, tf, tb)
    below = lax.ppermute(top, "tile", down)
    above = lax.ppermute(bottom, "tile", up)
    block = (planes, strip, columns)
    own_sum, *sends = call(
        functools.partial(join_kernel, planes),
        (shape(block, F32),) + (shape(block, BF16),) * (depth - 1),
        0, 3, flops=10**6, moved=3 * 2**20,
    )(core, above, below)
    received = [turned(send, depth - 1 - n) for n, send in enumerate(sends)]
    return call(
        functools.partial(update_kernel, view_rows),
        shape(block, F32),
        2, 2 + len(received), flops=10**6, moved=2**20,
    )(place, offsets, estimate, own_sum, *received)


def solution(mesh):
    in_specs = (P("depth", "tile", None), P(None, "depth", "tile", None), P(), P(), P(), P())
    out_specs = P("depth", "tile", None)
    return jax.shard_map(shards, mesh=mesh, in_specs=in_specs, out_specs=out_specs, check_vma=False)
```

```python
import functools
import jax
import jax.numpy as jnp
from jax import lax
from jax.experimental import pallas as pl
from jax.experimental.pallas import tpu as pltpu
from jax.sharding import PartitionSpec as P

F32, BF16 = jnp.float32, jnp.bfloat16
HALO = 16
LANES = 128
WIDE = 256
VMEM_LIMIT = 40 * 1024 * 1024


def normalized(ref):
    return ref[...] / jnp.sum(ref[...], axis=1, keepdims=True)


def select_taps(index, kernel):
    total = jnp.zeros((kernel.shape[0],) + index.shape[1:], F32)
    for tap in range(kernel.shape[1]):
        total = total + jnp.where(index == tap, kernel[:, tap : tap + 1], 0.0)
    return total


def slanted(row, rows):
    spread = jnp.broadcast_to(row, (rows, row.shape[1]))
    return pltpu.roll(spread, 0, 1, stride=1, stride_axis=0)


def matrices_kernel(planes, strip, device_ref, kx_ref, ky_ref, kz_ref, w_ref, wt_ref, tf_ref, tb_ref):
    views, taps = kx_ref.shape
    margin = taps // 2
    extent = strip + 2 * HALO
    kx, ky, kz = normalized(kx_ref), normalized(ky_ref), normalized(kz_ref)
    lane = lax.broadcasted_iota(jnp.int32, (1, LANES), 1)
    x_row = select_taps(lane % extent - (HALO - margin), kx)
    near = jnp.where(lane < LANES // 2, lane, lane - LANES)
    forward_row = select_taps(margin - near, ky)
    backward_row = select_taps(margin + near, ky)
    column = lax.broadcasted_iota(jnp.int32, (1, w_ref.shape[1]), 1) // extent
    device, odd = device_ref[0], device_ref[1] == 1
    plane = (device ^ (column // planes)) * planes + column % planes
    spot = lax.broadcasted_iota(jnp.int32, (strip, LANES), 1) % extent
    swap_first = jnp.logical_and(spot < HALO, jnp.logical_not(odd))
    swap_last = jnp.logical_and(spot >= extent - HALO, jnp.logical_not(odd))
    z_rows = [select_taps(plane - (device * planes + own) + margin, kz) for own in range(planes)]
    for view in range(views):
        x_block = slanted(x_row[view : view + 1], strip)
        turn = extent - HALO
        x_block = jnp.where(
            swap_first,
            pltpu.roll(x_block, LANES - turn, 1),
            jnp.where(swap_last, pltpu.roll(x_block, turn, 1), x_block),
        )
        x_block = jnp.concatenate([x_block] * (w_ref.shape[1] // LANES), axis=1)
        for own in range(planes):
            first = (view * planes + own) * strip
            block = x_block * z_rows[own][view : view + 1]
            w_ref[first : first + strip, :] = block.astype(BF16)
    wt_ref[...] = w_ref[...].astype(F32).T.astype(BF16)
    i = lax.broadcasted_iota(jnp.int32, (LANES, LANES), 0)
    j = lax.broadcasted_iota(jnp.int32, (LANES, LANES), 1)
    zeros = jnp.zeros((LANES, LANES), BF16)
    for view in range(views):
        for row, out in ((forward_row, tf_ref), (backward_row, tb_ref)):
            circle = slanted(row[view : view + 1], LANES)
            middle = jnp.where(jnp.abs(j - i) < LANES // 2, circle, 0.0).astype(BF16)
            earlier = jnp.where(i - j > LANES // 2, circle, 0.0).astype(BF16)
            later = jnp.where(j - i > LANES // 2, circle, 0.0).astype(BF16)
            grid = ((earlier, zeros), (middle, earlier), (later, middle), (zeros, later))
            for a, blocks in enumerate(grid):
                for b, block in enumerate(blocks):
                    out[view, a * LANES : (a + 1) * LANES, b * LANES : (b + 1) * LANES] = block


def write_coded(out_ref, where, values):
    pick = values.shape[-1] // 2 - LANES
    base = values[..., pick : pick + LANES].astype(BF16)
    wide = base.astype(F32)
    for first in range(0, values.shape[-1], LANES):
        part = values[..., first : first + LANES]
        part = base if first == pick else (part - wide).astype(BF16)
        out_ref[where + (slice(first, first + LANES),)] = part


def decoded(values, first):
    pick = values.shape[-1] // 2 - LANES
    base = values[..., pick : pick + LANES].astype(F32)
    if first == pick:
        return base
    return base + values[..., first : first + LANES].astype(F32)


def main_kernel(planes, strip, view_rows, depth, place_ref, offsets_ref, *refs):
    chunks, outer, refs = refs[:depth], refs[depth : 2 * depth], refs[2 * depth :]
    inner_ref, views_ref, w_ref, wt_ref, tf_ref, tb_ref, core_ref, back1_ref = refs[:8]
    back2, (ext_ref, pad_ref, back_ref, deep_ref) = refs[8:-4], refs[-4:]
    views = offsets_ref.shape[0]
    extent = strip + 2 * HALO
    columns = ext_ref.shape[-1]
    group = planes * strip
    for p in range(depth * planes):
        first = p * extent
        ext_ref[first : first + HALO, :] = inner_ref[p]
        ext_ref[first + HALO : first + HALO + strip, :] = chunks[p // planes][p % planes]
        ext_ref[first + HALO + strip : first + extent, :] = outer[p // planes][p % planes]
    for pad in (pad_ref, back_ref):
        pad[:, :LANES] = jnp.zeros((pad.shape[0], LANES), BF16)
        pad[:, LANES + columns :] = jnp.zeros((pad.shape[0], LANES), BF16)
    for first in range(0, columns, WIDE):
        block = jnp.dot(w_ref[...], ext_ref[:, first : first + WIDE], preferred_element_type=F32)
        pad_ref[:, LANES + first : LANES + first + WIDE] = block.astype(BF16)
    row = place_ref[0] + lax.broadcasted_iota(jnp.int32, (group, WIDE), 0) % strip
    starts = range(0, columns, WIDE)

    def windows(pad, rows):
        return jnp.concatenate([pad[rows, first : first + WIDE + 2 * LANES] for first in starts], axis=0)

    for view in range(views):
        rows = slice(view * group, (view + 1) * group)
        low = offsets_ref[view]
        inside = (row >= low) & (row < low + view_rows)
        blurred = jnp.dot(windows(pad_ref, rows), tf_ref[view], preferred_element_type=F32)
        for n, first in enumerate(starts):
            part = blurred[n * group : (n + 1) * group]
            seen = views_ref[rows, first : first + WIDE].astype(F32)
            correction = jnp.where(inside, seen / part - 1.0, 0.0)
            back_ref[rows, LANES + first : LANES + first + WIDE] = correction.astype(BF16)
        backward = jnp.dot(windows(back_ref, rows), tb_ref[view], preferred_element_type=F32)
        for n, first in enumerate(starts):
            deep_ref[rows, first : first + WIDE] = backward[n * group : (n + 1) * group].astype(BF16)
    for p in range(core_ref.shape[0]):
        part = jnp.dot(wt_ref[p * extent : (p + 1) * extent], deep_ref[...], preferred_element_type=F32)
        core_ref[p] = part[HALO : extent - HALO]
        write_coded(back1_ref, (p, slice(None)), part[:HALO])
        write_coded(back2[p // planes], (p % planes, slice(None)), part[extent - HALO :])


def join_kernel(planes, device_ref, core_ref, inner_ref, own_ref, *sends):
    strip = core_ref.shape[1]
    columns = core_ref.shape[2]
    odd = device_ref[1] == 1
    for p in range(core_ref.shape[0]):
        inner = inner_ref[p]
        parts = []
        for first in range(0, columns, LANES):
            lanes = slice(first, first + LANES)
            added = decoded(inner, first)
            head = core_ref[p, :HALO, lanes] + jnp.where(odd, added, 0.0)
            tail = core_ref[p, strip - HALO :, lanes] + jnp.where(odd, 0.0, added)
            middle = [core_ref[p, HALO : strip - HALO, lanes]] if strip > 2 * HALO else []
            parts.append(jnp.concatenate([head, *middle, tail], axis=0))
        whole = jnp.concatenate(parts, axis=1)
        if p < planes:
            own_ref[p] = whole
        else:
            write_coded(sends[p // planes - 1], (p % planes, slice(None)), whole)


def update_kernel(view_rows, place_ref, device_ref, offsets_ref, estimate_ref, own_ref, *refs):
    received, out_ref = refs[:-1], refs[-1]
    near = len(received) // 2
    received, outer = received[:near], received[near:]
    planes, strip, columns = estimate_ref.shape
    odd = device_ref[1] == 1
    row = place_ref[0] + lax.broadcasted_iota(jnp.int32, (strip, LANES), 0)
    coverage = jnp.zeros((strip, LANES), F32)
    for view in range(offsets_ref.shape[0]):
        low = offsets_ref[view]
        coverage = coverage + jnp.where((row >= low) & (row < low + view_rows), 1.0, 0.0)
    scale = 1.0 / jnp.maximum(coverage, 1.0)
    for p in range(planes):
        for first in range(0, columns, LANES):
            lanes = slice(first, first + LANES)
            summed = own_ref[p, :, lanes]
            for ref in received:
                summed = summed + decoded(ref[p], first)
            edge = decoded(outer[0][p], first)
            for ref in outer[1:]:
                edge = edge + decoded(ref[p], first)
            head = summed[:HALO] + jnp.where(odd, 0.0, edge)
            tail = summed[strip - HALO :] + jnp.where(odd, edge, 0.0)
            middle = [summed[HALO : strip - HALO]] if strip > 2 * HALO else []
            summed = jnp.concatenate([head, *middle, tail], axis=0)
            out_ref[p, :, lanes] = estimate_ref[p, :, lanes] * (1.0 + summed * scale)


def call(body, outs, scalars, arrays, scratch=(), flops=0, moved=0):
    return pl.pallas_call(
        body,
        out_shape=outs,
        in_specs=[pl.BlockSpec(memory_space=pltpu.SMEM)] * scalars
        + [pl.BlockSpec(memory_space=pltpu.VMEM)] * arrays,
        out_specs=jax.tree.map(lambda _: pl.BlockSpec(memory_space=pltpu.VMEM), outs),
        scratch_shapes=list(scratch),
        compiler_params=pltpu.CompilerParams(vmem_limit_bytes=VMEM_LIMIT),
        cost_estimate=pl.CostEstimate(flops=flops, bytes_accessed=moved, transcendentals=0),
    )


def shards(estimate, views, kernel_x, kernel_y, kernel_z, offsets):
    shape = jax.ShapeDtypeStruct
    depth, tiles = lax.axis_size("depth"), lax.axis_size("tile")
    planes, strip, columns = estimate.shape
    count = views.shape[0]
    extent = strip + 2 * HALO
    rows = count * planes * strip
    inner = depth * planes * extent
    view_rows = 5 * strip * tiles // 8
    tile = lax.axis_index("tile").astype(jnp.int32)
    odd = tile % 2
    place = (tile * strip).reshape(1)
    device = jnp.stack([lax.axis_index("depth").astype(jnp.int32), odd])
    steps = range(depth)

    def across(array, step):
        return lax.ppermute(array, "depth", [(i, i ^ step) for i in range(depth)])

    def beside(array, step):
        pairs = [(i, i - 1 + 2 * (i % 2)) for i in range(1, tiles - 1)]
        pairs = [(i * depth + d, j * depth + (d ^ step)) for i, j in pairs for d in range(depth)]
        return lax.ppermute(array, ("tile", "depth"), pairs)

    def within(array):
        return lax.ppermute(array, "tile", [(i, i ^ 1) for i in range(tiles)])

    def early_or_late(array, early):
        return jnp.where(odd == early, array[:, :HALO], array[:, strip - HALO :])

    own = estimate.astype(BF16)
    edge = early_or_late(own, 0)
    chunks = [own] + [across(own, step) for step in steps[1:]]
    outer = [beside(edge, step) for step in steps]
    chunks, outer = lax.optimization_barrier((chunks, outer))
    w, wt, tf, tb = call(
        functools.partial(matrices_kernel, planes, strip),
        (shape((rows, inner), BF16), shape((inner, rows), BF16))
        + (shape((count, WIDE + 2 * LANES, WIDE), BF16),) * 2,
        1, 3, flops=10**8, moved=5 * 2**20,
    )(device, kernel_x, kernel_y, kernel_z)
    inside = within(early_or_late(jnp.concatenate(chunks, axis=0), 1))
    halo = shape((planes, HALO, columns), BF16)
    core, back1, *back2 = call(
        functools.partial(main_kernel, planes, strip, view_rows, depth),
        (shape((depth * planes, strip, columns), F32), shape((depth * planes, HALO, columns), BF16))
        + (halo,) * depth,
        2, 2 * depth + 6,
        scratch=(
            pltpu.VMEM((inner, columns), BF16),
            pltpu.VMEM((rows, columns + 2 * LANES), BF16),
            pltpu.VMEM((rows, columns + 2 * LANES), BF16),
            pltpu.VMEM((rows, columns), BF16),
        ),
        flops=2 * 10**9, moved=10 * 2**20,
    )(place, offsets, *chunks, *outer, inside, views.reshape(rows, columns), w, wt, tf, tb)
    block = (planes, strip, columns)
    own_sum, *sends = call(
        functools.partial(join_kernel, planes),
        (shape(block, F32),) + (shape(block, BF16),) * (depth - 1),
        1, 2, flops=10**6, moved=3 * 2**20,
    )(device, core, within(back1))
    received = [across(send, step) for send, step in zip(sends, steps[1:])]
    edges = [beside(send, step) for send, step in zip(back2, steps)]
    return call(
        functools.partial(update_kernel, view_rows),
        shape(block, F32),
        3, 1 + 2 * depth, flops=10**6, moved=2**20,
    )(place, device, offsets, estimate, own_sum, *received, *edges[::-1])


def solution(mesh):
    in_specs = (P("depth", "tile", None), P(None, "depth", "tile", None), P(), P(), P(), P())
    out_specs = P("depth", "tile", None)
    return jax.shard_map(shards, mesh=mesh, in_specs=in_specs, out_specs=out_specs, check_vma=False)
```

```python
import functools
import jax
import jax.numpy as jnp
from jax import lax
from jax.experimental import pallas as pl
from jax.experimental.pallas import tpu as pltpu
from jax.sharding import PartitionSpec as P

F32, BF16 = jnp.float32, jnp.bfloat16
HALO = 16
LANES = 128
WIDE = 256
VMEM_LIMIT = 40 * 1024 * 1024


def normalized(ref):
    return ref[...] / jnp.sum(ref[...], axis=1, keepdims=True)


def select_taps(index, kernel):
    total = jnp.zeros((kernel.shape[0],) + index.shape[1:], F32)
    for tap in range(kernel.shape[1]):
        total = total + jnp.where(index == tap, kernel[:, tap : tap + 1], 0.0)
    return total


def slanted(row, rows):
    spread = jnp.broadcast_to(row, (rows, row.shape[1]))
    return pltpu.roll(spread, 0, 1, stride=1, stride_axis=0)


def matrices_kernel(planes, strip, device_ref, kx_ref, ky_ref, kz_ref, w_ref, wt_ref, tf_ref, tb_ref):
    views, taps = kx_ref.shape
    margin = taps // 2
    extent = strip + 2 * HALO
    kx, ky, kz = normalized(kx_ref), normalized(ky_ref), normalized(kz_ref)
    lane = lax.broadcasted_iota(jnp.int32, (1, LANES), 1)
    x_row = select_taps(lane % extent - (HALO - margin), kx)
    near = jnp.where(lane < LANES // 2, lane, lane - LANES)
    forward_row = select_taps(margin - near, ky)
    backward_row = select_taps(margin + near, ky)
    column = lax.broadcasted_iota(jnp.int32, (1, w_ref.shape[1]), 1) // extent
    device, odd = device_ref[0], device_ref[1] == 1
    plane = (device ^ (column // planes)) * planes + column % planes
    spot = lax.broadcasted_iota(jnp.int32, (strip, LANES), 1) % extent
    z_rows = [select_taps(plane - (device * planes + own) + margin, kz) for own in range(planes)]
    for view in range(views):
        x_block = slanted(x_row[view : view + 1], strip)
        turned = x_block
        for quarter in range(extent // HALO):
            shift = extent - (2 * quarter + 1) * HALO
            moved = pltpu.roll(x_block, (LANES - shift) % LANES, 1)
            here = jnp.logical_and(spot // HALO == quarter, jnp.logical_not(odd))
            turned = jnp.where(here, moved, turned)
        x_block = turned
        x_block = jnp.concatenate([x_block] * (w_ref.shape[1] // LANES), axis=1)
        for own in range(planes):
            first = (view * planes + own) * strip
            block = x_block * z_rows[own][view : view + 1]
            w_ref[first : first + strip, :] = block.astype(BF16)
    wt_ref[...] = w_ref[...].astype(F32).T.astype(BF16)
    i = lax.broadcasted_iota(jnp.int32, (LANES, LANES), 0)
    j = lax.broadcasted_iota(jnp.int32, (LANES, LANES), 1)
    zeros = jnp.zeros((LANES, LANES), BF16)
    for view in range(views):
        for row, out in ((forward_row, tf_ref), (backward_row, tb_ref)):
            circle = slanted(row[view : view + 1], LANES)
            middle = jnp.where(jnp.abs(j - i) < LANES // 2, circle, 0.0).astype(BF16)
            earlier = jnp.where(i - j > LANES // 2, circle, 0.0).astype(BF16)
            later = jnp.where(j - i > LANES // 2, circle, 0.0).astype(BF16)
            grid = ((earlier, zeros), (middle, earlier), (later, middle), (zeros, later))
            for a, blocks in enumerate(grid):
                for b, block in enumerate(blocks):
                    out[view, a * LANES : (a + 1) * LANES, b * LANES : (b + 1) * LANES] = block


def write_coded(out_ref, where, values):
    pick = values.shape[-1] // 2 - LANES
    base = values[..., pick : pick + LANES].astype(BF16)
    wide = base.astype(F32)
    for first in range(0, values.shape[-1], LANES):
        part = values[..., first : first + LANES]
        part = base if first == pick else (part - wide).astype(BF16)
        out_ref[where + (slice(first, first + LANES),)] = part


def decoded(values, first):
    pick = values.shape[-1] // 2 - LANES
    base = values[..., pick : pick + LANES].astype(F32)
    if first == pick:
        return base
    return base + values[..., first : first + LANES].astype(F32)


def main_kernel(planes, view_rows, place_ref, offsets_ref, *refs):
    quarters, (views_ref, w_ref, wt_ref, tf_ref, tb_ref) = refs[:4], refs[4:9]
    cores, backs, (ext_ref, pad_ref, back_ref, deep_ref) = refs[9:11], refs[11:13], refs[13:]
    views = offsets_ref.shape[0]
    count = quarters[0].shape[0]
    extent = ext_ref.shape[0] // count
    strip = extent - 2 * HALO
    columns = ext_ref.shape[-1]
    group = planes * strip
    for p in range(count):
        for n, ref in enumerate(quarters[::-1]):
            ext_ref[p * extent + n * HALO : p * extent + (n + 1) * HALO, :] = ref[p]
    for pad in (pad_ref, back_ref):
        pad[:, :LANES] = jnp.zeros((pad.shape[0], LANES), BF16)
        pad[:, LANES + columns :] = jnp.zeros((pad.shape[0], LANES), BF16)
    for first in range(0, columns, WIDE):
        block = jnp.dot(w_ref[...], ext_ref[:, first : first + WIDE], preferred_element_type=F32)
        pad_ref[:, LANES + first : LANES + first + WIDE] = block.astype(BF16)
    row = place_ref[0] + lax.broadcasted_iota(jnp.int32, (group, WIDE), 0) % strip
    starts = range(0, columns, WIDE)

    def windows(pad, rows):
        return jnp.concatenate([pad[rows, first : first + WIDE + 2 * LANES] for first in starts], axis=0)

    for view in range(views):
        rows = slice(view * group, (view + 1) * group)
        low = offsets_ref[view]
        inside = (row >= low) & (row < low + view_rows)
        blurred = jnp.dot(windows(pad_ref, rows), tf_ref[view], preferred_element_type=F32)
        for n, first in enumerate(starts):
            part = blurred[n * group : (n + 1) * group]
            seen = views_ref[rows, first : first + WIDE].astype(F32)
            correction = jnp.where(inside, seen / part - 1.0, 0.0)
            back_ref[rows, LANES + first : LANES + first + WIDE] = correction.astype(BF16)
        backward = jnp.dot(windows(back_ref, rows), tb_ref[view], preferred_element_type=F32)
        for n, first in enumerate(starts):
            deep_ref[rows, first : first + WIDE] = backward[n * group : (n + 1) * group].astype(BF16)
    for p in range(count):
        part = jnp.dot(wt_ref[p * extent : (p + 1) * extent], deep_ref[...], preferred_element_type=F32)
        write_coded(backs[0], (p, slice(None)), part[:HALO])
        cores[0][p] = part[HALO : 2 * HALO]
        cores[1][p] = part[2 * HALO : 3 * HALO]
        write_coded(backs[1], (p, slice(None)), part[3 * HALO :])


def join_kernel(planes, core_ref, other_ref, own_ref, *sends):
    columns = core_ref.shape[2]
    for p in range(core_ref.shape[0]):
        other = other_ref[p]
        parts = []
        for first in range(0, columns, LANES):
            parts.append(core_ref[p, :, first : first + LANES] + decoded(other, first))
        whole = jnp.concatenate(parts, axis=1)
        if p < planes:
            own_ref[p] = whole
        else:
            write_coded(sends[p // planes - 1], (p % planes, slice(None)), whole)


def update_kernel(view_rows, place_ref, device_ref, offsets_ref, estimate_ref, *refs):
    parts, out_ref = refs[:-1], refs[-1]
    planes, strip, columns = estimate_ref.shape
    odd = device_ref[1]
    for half, start in ((0, (1 - odd) * HALO), (1, odd * HALO)):
        mine = parts[half * (len(parts) // 2) : (half + 1) * (len(parts) // 2)]
        row = place_ref[0] + start + lax.broadcasted_iota(jnp.int32, (HALO, LANES), 0)
        coverage = jnp.zeros((HALO, LANES), F32)
        for view in range(offsets_ref.shape[0]):
            low = offsets_ref[view]
            coverage = coverage + jnp.where((row >= low) & (row < low + view_rows), 1.0, 0.0)
        scale = 1.0 / jnp.maximum(coverage, 1.0)
        rows = pl.ds(pl.multiple_of(start, HALO), HALO)
        for p in range(planes):
            for first in range(0, columns, LANES):
                lanes = slice(first, first + LANES)
                summed = mine[0][p, :, lanes]
                for ref in mine[1:]:
                    summed = summed + decoded(ref[p], first)
                out_ref[p, rows, lanes] = estimate_ref[p, rows, lanes] * (1.0 + summed * scale)


def call(body, outs, scalars, arrays, scratch=(), flops=0, moved=0):
    return pl.pallas_call(
        body,
        out_shape=outs,
        in_specs=[pl.BlockSpec(memory_space=pltpu.SMEM)] * scalars
        + [pl.BlockSpec(memory_space=pltpu.VMEM)] * arrays,
        out_specs=jax.tree.map(lambda _: pl.BlockSpec(memory_space=pltpu.VMEM), outs),
        scratch_shapes=list(scratch),
        compiler_params=pltpu.CompilerParams(vmem_limit_bytes=VMEM_LIMIT),
        cost_estimate=pl.CostEstimate(flops=flops, bytes_accessed=moved, transcendentals=0),
    )


def shards(estimate, views, kernel_x, kernel_y, kernel_z, offsets):
    shape = jax.ShapeDtypeStruct
    depth, tiles = lax.axis_size("depth"), lax.axis_size("tile")
    planes, strip, columns = estimate.shape
    count = views.shape[0]
    extent = strip + 2 * HALO
    rows = count * planes * strip
    span = depth * planes * extent
    view_rows = 5 * strip * tiles // 8
    tile = lax.axis_index("tile").astype(jnp.int32)
    odd = tile % 2
    place = (tile * strip).reshape(1)
    device = jnp.stack([lax.axis_index("depth").astype(jnp.int32), odd])
    assert strip == 2 * HALO and tiles % 2 == 0

    def across(array, step):
        return lax.ppermute(array, "depth", [(i, i ^ step) for i in range(depth)])

    def beside(array):
        return lax.ppermute(array, "tile", [(i, i - 1 + 2 * (i % 2)) for i in range(1, tiles - 1)])

    def within(array):
        return lax.ppermute(array, "tile", [(i, i ^ 1) for i in range(tiles)])

    own = estimate.astype(BF16)
    early, late = own[:, :HALO], own[:, HALO:]
    outer_own, inner_own = jnp.where(odd == 1, late, early), jnp.where(odd == 1, early, late)
    outer = jnp.concatenate([outer_own] + [across(outer_own, step) for step in range(1, depth)], axis=0)
    other_chip = beside(outer)
    inner = jnp.concatenate([inner_own] + [across(inner_own, step) for step in range(1, depth)], axis=0)
    other_core = within(inner)
    w, wt, tf, tb = call(
        functools.partial(matrices_kernel, planes, strip),
        (shape((rows, span), BF16), shape((span, rows), BF16))
        + (shape((count, WIDE + 2 * LANES, WIDE), BF16),) * 2,
        1, 3, flops=10**8, moved=5 * 2**20,
    )(device, kernel_x, kernel_y, kernel_z)
    halves = (depth * planes, HALO, columns)
    inner, outer, to_core, to_chip = call(
        functools.partial(main_kernel, planes, view_rows),
        (shape(halves, F32),) * 2 + (shape(halves, BF16),) * 2,
        2, 9,
        scratch=(
            pltpu.VMEM((span, columns), BF16),
            pltpu.VMEM((rows, columns + 2 * LANES), BF16),
            pltpu.VMEM((rows, columns + 2 * LANES), BF16),
            pltpu.VMEM((rows, columns), BF16),
        ),
        flops=2 * 10**9, moved=10 * 2**20,
    )(place, offsets, other_chip, outer, inner, other_core, views.reshape(rows, columns), w, wt, tf, tb)
    block = (planes, HALO, columns)
    sums = []
    for core, other in ((inner, within(to_core)), (outer, beside(to_chip))):
        own_sum, *sends = call(
            functools.partial(join_kernel, planes),
            (shape(block, F32),) + (shape(block, BF16),) * (depth - 1),
            0, 2, flops=10**6, moved=3 * 2**20,
        )(core, other)
        sums += [own_sum] + [across(send, step + 1) for step, send in enumerate(sends)]
    return call(
        functools.partial(update_kernel, view_rows),
        shape(estimate.shape, F32),
        3, 1 + 2 * depth, flops=10**6, moved=2**20,
    )(place, device, offsets, estimate, *sums)


def solution(mesh):
    in_specs = (P("depth", "tile", None), P(None, "depth", "tile", None), P(), P(), P(), P())
    out_specs = P("depth", "tile", None)
    return jax.shard_map(shards, mesh=mesh, in_specs=in_specs, out_specs=out_specs, check_vma=False)
```

```python
import functools
import jax
import jax.numpy as jnp
from jax import lax
from jax.experimental import pallas as pl
from jax.experimental.pallas import tpu as pltpu
from jax.sharding import PartitionSpec as P

F32, BF16 = jnp.float32, jnp.bfloat16
HALO = 16
LANES = 128
WIDE = 256
VMEM_LIMIT = 40 * 1024 * 1024


def select_taps(index, kernel):
    total = jnp.zeros((kernel.shape[0],) + index.shape[1:], F32)
    for tap in range(kernel.shape[1]):
        total = total + jnp.where(index == tap, kernel[:, tap : tap + 1], 0.0)
    return total


def slanted(row, rows):
    spread = jnp.broadcast_to(row, (rows, row.shape[1]))
    return pltpu.roll(spread, 0, 1, stride=1, stride_axis=0)


def matrices_kernel(planes, strip, device_ref, kernels_ref, w_ref, wt_ref, tf_ref, tb_ref):
    views, taps = kernels_ref.shape[1:]
    margin = taps // 2
    extent = strip + 2 * HALO
    kx, ky, kz = [kernels_ref[n] / jnp.sum(kernels_ref[n], axis=1, keepdims=True) for n in range(3)]
    lane = lax.broadcasted_iota(jnp.int32, (1, LANES), 1)
    x_row = select_taps(lane % extent - (HALO - margin), kx)
    near = jnp.where(lane < LANES // 2, lane, lane - LANES)
    forward_row = select_taps(margin - near, ky)
    backward_row = select_taps(margin + near, ky)
    column = lax.broadcasted_iota(jnp.int32, (1, w_ref.shape[1]), 1) // extent
    device, odd = device_ref[0], device_ref[1] == 1
    plane = (device ^ (column // planes)) * planes + column % planes
    spot = lax.broadcasted_iota(jnp.int32, (strip, LANES), 1) % extent
    z_rows = [select_taps(plane - (device * planes + own) + margin, kz) for own in range(planes)]
    for view in range(views):
        x_block = slanted(x_row[view : view + 1], strip)
        turned = x_block
        for quarter in range(extent // HALO):
            shift = extent - (2 * quarter + 1) * HALO
            moved = pltpu.roll(x_block, (LANES - shift) % LANES, 1)
            here = jnp.logical_and(spot // HALO == quarter, jnp.logical_not(odd))
            turned = jnp.where(here, moved, turned)
        x_block = turned
        x_block = jnp.concatenate([x_block] * (w_ref.shape[1] // LANES), axis=1)
        for own in range(planes):
            first = (view * planes + own) * strip
            block = x_block * z_rows[own][view : view + 1]
            w_ref[first : first + strip, :] = block.astype(BF16)
    wt_ref[...] = w_ref[...].astype(F32).T.astype(BF16)
    i = lax.broadcasted_iota(jnp.int32, (LANES, LANES), 0)
    j = lax.broadcasted_iota(jnp.int32, (LANES, LANES), 1)
    zeros = jnp.zeros((LANES, LANES), BF16)
    for view in range(views):
        for row, out in ((forward_row, tf_ref), (backward_row, tb_ref)):
            circle = slanted(row[view : view + 1], LANES)
            middle = jnp.where(jnp.abs(j - i) < LANES // 2, circle, 0.0).astype(BF16)
            earlier = jnp.where(i - j > LANES // 2, circle, 0.0).astype(BF16)
            later = jnp.where(j - i > LANES // 2, circle, 0.0).astype(BF16)
            grid = ((earlier, zeros), (middle, earlier), (later, middle), (zeros, later))
            for a, blocks in enumerate(grid):
                for b, block in enumerate(blocks):
                    out[view, a * LANES : (a + 1) * LANES, b * LANES : (b + 1) * LANES] = block


def write_coded(out_ref, where, values):
    pick = values.shape[-1] // 2 - LANES
    base = values[..., pick : pick + LANES].astype(BF16)
    wide = base.astype(F32)
    for first in range(0, values.shape[-1], LANES):
        part = values[..., first : first + LANES]
        part = base if first == pick else (part - wide).astype(BF16)
        out_ref[where + (slice(first, first + LANES),)] = part


def decoded(values, first):
    pick = values.shape[-1] // 2 - LANES
    base = values[..., pick : pick + LANES].astype(F32)
    if first == pick:
        return base
    return base + values[..., first : first + LANES].astype(F32)


def main_kernel(planes, view_rows, place_ref, device_ref, offsets_ref, *refs):
    quarters, (views_ref, w_ref, wt_ref, tf_ref, tb_ref) = refs[:4], refs[4:9]
    cores, backs, (ext_ref, pad_ref, back_ref, deep_ref) = refs[9:11], refs[11:13], refs[13:]
    views = offsets_ref.shape[0]
    count = quarters[0].shape[0]
    extent = ext_ref.shape[0] // count
    strip = extent - 2 * HALO
    columns = ext_ref.shape[-1]
    group = planes * strip
    for p in range(count):
        for n, ref in enumerate(quarters[::-1]):
            ext_ref[p * extent + n * HALO : p * extent + (n + 1) * HALO, :] = ref[p]

    @pl.when(device_ref[2] == 0)
    def _():
        for p in range(count):
            ext_ref[(p + 1) * extent - HALO : (p + 1) * extent, :] = jnp.zeros((HALO, columns), BF16)

    for pad in (pad_ref, back_ref):
        pad[:, :LANES] = jnp.zeros((pad.shape[0], LANES), BF16)
        pad[:, LANES + columns :] = jnp.zeros((pad.shape[0], LANES), BF16)
    for first in range(0, columns, WIDE):
        block = jnp.dot(w_ref[...], ext_ref[:, first : first + WIDE], preferred_element_type=F32)
        pad_ref[:, LANES + first : LANES + first + WIDE] = block.astype(BF16)
    row = place_ref[0] + lax.broadcasted_iota(jnp.int32, (group, WIDE), 0) % strip
    starts = range(0, columns, WIDE)

    def windows(pad, rows):
        return jnp.concatenate([pad[rows, first : first + WIDE + 2 * LANES] for first in starts], axis=0)

    for view in range(views):
        rows = slice(view * group, (view + 1) * group)
        low = offsets_ref[view]
        inside = (row >= low) & (row < low + view_rows)
        blurred = jnp.dot(windows(pad_ref, rows), tf_ref[view], preferred_element_type=F32)
        for n, first in enumerate(starts):
            part = blurred[n * group : (n + 1) * group]
            seen = views_ref[rows, first : first + WIDE].astype(F32)
            correction = jnp.where(inside, seen / part - 1.0, 0.0)
            back_ref[rows, LANES + first : LANES + first + WIDE] = correction.astype(BF16)
        backward = jnp.dot(windows(back_ref, rows), tb_ref[view], preferred_element_type=F32)
        for n, first in enumerate(starts):
            deep_ref[rows, first : first + WIDE] = backward[n * group : (n + 1) * group].astype(BF16)
    for p in range(count):
        part = jnp.dot(wt_ref[p * extent : (p + 1) * extent], deep_ref[...], preferred_element_type=F32)
        write_coded(backs[0], (p, slice(None)), part[:HALO])
        cores[0][p] = part[HALO : 2 * HALO]
        cores[1][p] = part[2 * HALO : 3 * HALO]
        write_coded(backs[1], (p, slice(None)), part[3 * HALO :])


def join_kernel(planes, flag, device_ref, core_ref, other_ref, own_ref, *sends):
    columns = core_ref.shape[2]
    counts = device_ref[flag] != 0
    for p in range(core_ref.shape[0]):
        other = other_ref[p]
        parts = []
        for first in range(0, columns, LANES):
            parts.append(core_ref[p, :, first : first + LANES] + jnp.where(counts, decoded(other, first), 0.0))
        whole = jnp.concatenate(parts, axis=1)
        if p < planes:
            own_ref[p] = whole
        else:
            write_coded(sends[p // planes - 1], (p % planes, slice(None)), whole)


def update_kernel(view_rows, place_ref, device_ref, offsets_ref, estimate_ref, *refs):
    parts, out_ref = refs[:-1], refs[-1]
    planes, strip, columns = estimate_ref.shape
    odd = device_ref[1]
    for half, start in ((0, (1 - odd) * HALO), (1, odd * HALO)):
        mine = parts[half * (len(parts) // 2) : (half + 1) * (len(parts) // 2)]
        row = place_ref[0] + start + lax.broadcasted_iota(jnp.int32, (HALO, LANES), 0)
        coverage = jnp.zeros((HALO, LANES), F32)
        for view in range(offsets_ref.shape[0]):
            low = offsets_ref[view]
            coverage = coverage + jnp.where((row >= low) & (row < low + view_rows), 1.0, 0.0)
        scale = 1.0 / jnp.maximum(coverage, 1.0)
        rows = pl.ds(pl.multiple_of(start, HALO), HALO)
        for p in range(planes):
            for first in range(0, columns, LANES):
                lanes = slice(first, first + LANES)
                summed = mine[0][p, :, lanes]
                for ref in mine[1:]:
                    summed = summed + decoded(ref[p], first)
                out_ref[p, rows, lanes] = estimate_ref[p, rows, lanes] * (1.0 + summed * scale)


def call(body, outs, scalars, arrays, scratch=(), flops=0, moved=0):
    return pl.pallas_call(
        body,
        out_shape=outs,
        in_specs=[pl.BlockSpec(memory_space=pltpu.SMEM)] * scalars
        + [pl.BlockSpec(memory_space=pltpu.VMEM)] * arrays,
        out_specs=jax.tree.map(lambda _: pl.BlockSpec(memory_space=pltpu.VMEM), outs),
        scratch_shapes=list(scratch),
        compiler_params=pltpu.CompilerParams(vmem_limit_bytes=VMEM_LIMIT),
        cost_estimate=pl.CostEstimate(flops=flops, bytes_accessed=moved, transcendentals=0),
    )


def shards(estimate, views, kernel_x, kernel_y, kernel_z, offsets):
    shape = jax.ShapeDtypeStruct
    depth, tiles = lax.axis_size("depth"), lax.axis_size("tile")
    planes, strip, columns = estimate.shape
    count = views.shape[0]
    extent = strip + 2 * HALO
    rows = count * planes * strip
    span = depth * planes * extent
    view_rows = 5 * strip * tiles // 8
    tile = lax.axis_index("tile").astype(jnp.int32)
    odd = tile % 2
    place = (tile * strip).reshape(1)
    has_chip = ((tile > 0) & (tile < tiles - 1)).astype(jnp.int32)
    block_index = lax.axis_index("depth").astype(jnp.int32)
    device = jnp.stack([block_index, odd, has_chip, jnp.ones_like(odd)])
    assert strip == 2 * HALO and tiles % 2 == 0

    def across(array, step):
        return lax.ppermute(array, "depth", [(i, i ^ step) for i in range(depth)])

    def beside(array):
        return lax.ppermute(array, "tile", [(i, (i - 1 + 2 * (i % 2)) % tiles) for i in range(tiles)])

    def within(array):
        return lax.ppermute(array, "tile", [(i, i ^ 1) for i in range(tiles)])

    own = estimate.astype(BF16)
    early, late = own[:, :HALO], own[:, HALO:]
    outer_own, inner_own = jnp.where(odd == 1, late, early), jnp.where(odd == 1, early, late)
    outer = jnp.concatenate([outer_own] + [across(outer_own, step) for step in range(1, depth)], axis=0)
    other_chip = beside(outer)
    inner = jnp.concatenate([inner_own] + [across(inner_own, step) for step in range(1, depth)], axis=0)
    other_core = within(inner)
    w, wt, tf, tb = call(
        functools.partial(matrices_kernel, planes, strip),
        (shape((rows, span), BF16), shape((span, rows), BF16))
        + (shape((count, WIDE + 2 * LANES, WIDE), BF16),) * 2,
        1, 1, flops=10**8, moved=5 * 2**20,
    )(device, jnp.stack([kernel_x, kernel_y, kernel_z]))
    halves = (depth * planes, HALO, columns)
    inner, outer, to_core, to_chip = call(
        functools.partial(main_kernel, planes, view_rows),
        (shape(halves, F32),) * 2 + (shape(halves, BF16),) * 2,
        3, 9,
        scratch=(
            pltpu.VMEM((span, columns), BF16),
            pltpu.VMEM((rows, columns + 2 * LANES), BF16),
            pltpu.VMEM((rows, columns + 2 * LANES), BF16),
            pltpu.VMEM((rows, columns), BF16),
        ),
        flops=2 * 10**9, moved=10 * 2**20,
    )(place, device, offsets, other_chip, outer, inner, other_core, views.reshape(rows, columns), w, wt, tf, tb)
    block = (planes, HALO, columns)
    sums = []
    for flag, core, other in ((3, inner, within(to_core)), (2, outer, beside(to_chip))):
        own_sum, *sends = call(
            functools.partial(join_kernel, planes, flag),
            (shape(block, F32),) + (shape(block, BF16),) * (depth - 1),
            1, 2, flops=10**6, moved=3 * 2**20,
        )(device, core, other)
        sums += [own_sum] + [across(send, step + 1) for step, send in enumerate(sends)]
    return call(
        functools.partial(update_kernel, view_rows),
        shape(estimate.shape, F32),
        3, 1 + 2 * depth, flops=10**6, moved=2**20,
    )(place, device, offsets, estimate, *sums)


def solution(mesh):
    in_specs = (P("depth", "tile", None), P(None, "depth", "tile", None), P(), P(), P(), P())
    out_specs = P("depth", "tile", None)
    return jax.shard_map(shards, mesh=mesh, in_specs=in_specs, out_specs=out_specs, check_vma=False)
```

```python
import functools
import jax
import jax.numpy as jnp
from jax import lax
from jax.experimental import pallas as pl
from jax.experimental.pallas import tpu as pltpu
from jax.sharding import PartitionSpec as P

F32, BF16 = jnp.float32, jnp.bfloat16
HALO = 16
LANES = 128
WIDE = 256
INFO = 4
VMEM_LIMIT = 40 * 1024 * 1024


def select_taps(index, kernel):
    total = jnp.zeros((kernel.shape[0],) + index.shape[1:], F32)
    for tap in range(kernel.shape[1]):
        total = total + jnp.where(index == tap, kernel[:, tap : tap + 1], 0.0)
    return total


def slanted(row, rows):
    spread = jnp.broadcast_to(row, (rows, row.shape[1]))
    return pltpu.roll(spread, 0, 1, stride=1, stride_axis=0)


def matrices_kernel(planes, strip, device_ref, kernels_ref, w_ref, wt_ref, tf_ref, tb_ref):
    views, taps = kernels_ref.shape[1:]
    margin = taps // 2
    extent = strip + 2 * HALO
    kx, ky, kz = [kernels_ref[n] / jnp.sum(kernels_ref[n], axis=1, keepdims=True) for n in range(3)]
    lane = lax.broadcasted_iota(jnp.int32, (1, LANES), 1)
    x_row = select_taps(lane % extent - (HALO - margin), kx)
    near = jnp.where(lane < LANES // 2, lane, lane - LANES)
    forward_row = select_taps(margin - near, ky)
    backward_row = select_taps(margin + near, ky)
    column = lax.broadcasted_iota(jnp.int32, (1, w_ref.shape[1]), 1) // extent
    device, odd = device_ref[0], device_ref[1] == 1
    plane = (device ^ (column // planes)) * planes + column % planes
    spot = lax.broadcasted_iota(jnp.int32, (strip, LANES), 1) % extent
    z_rows = [select_taps(plane - (device * planes + own) + margin, kz) for own in range(planes)]
    for view in range(views):
        x_block = slanted(x_row[view : view + 1], strip)
        turned = x_block
        for quarter in range(extent // HALO):
            shift = extent - (2 * quarter + 1) * HALO
            moved = pltpu.roll(x_block, (LANES - shift) % LANES, 1)
            here = jnp.logical_and(spot // HALO == quarter, jnp.logical_not(odd))
            turned = jnp.where(here, moved, turned)
        x_block = turned
        x_block = jnp.concatenate([x_block] * (w_ref.shape[1] // LANES), axis=1)
        for own in range(planes):
            first = (view * planes + own) * strip
            block = x_block * z_rows[own][view : view + 1]
            w_ref[first : first + strip, :] = block.astype(BF16)
    wt_ref[...] = w_ref[...].astype(F32).T.astype(BF16)
    i = lax.broadcasted_iota(jnp.int32, (LANES, LANES), 0)
    j = lax.broadcasted_iota(jnp.int32, (LANES, LANES), 1)
    zeros = jnp.zeros((LANES, LANES), BF16)
    for view in range(views):
        for row, out in ((forward_row, tf_ref), (backward_row, tb_ref)):
            circle = slanted(row[view : view + 1], LANES)
            middle = jnp.where(jnp.abs(j - i) < LANES // 2, circle, 0.0).astype(BF16)
            earlier = jnp.where(i - j > LANES // 2, circle, 0.0).astype(BF16)
            later = jnp.where(j - i > LANES // 2, circle, 0.0).astype(BF16)
            grid = ((earlier, zeros), (middle, earlier), (later, middle), (zeros, later))
            for a, blocks in enumerate(grid):
                for b, block in enumerate(blocks):
                    out[view, a * LANES : (a + 1) * LANES, b * LANES : (b + 1) * LANES] = block


def write_coded(out_ref, where, values):
    pick = values.shape[-1] // 2 - LANES
    base = values[..., pick : pick + LANES].astype(BF16)
    wide = base.astype(F32)
    for first in range(0, values.shape[-1], LANES):
        part = values[..., first : first + LANES]
        part = base if first == pick else (part - wide).astype(BF16)
        out_ref[where + (slice(first, first + LANES),)] = part


def decoded(values, first):
    pick = values.shape[-1] // 2 - LANES
    base = values[..., pick : pick + LANES].astype(F32)
    if first == pick:
        return base
    return base + values[..., first : first + LANES].astype(F32)


def main_kernel(planes, view_rows, info_ref, *refs):
    quarters, (views_ref, w_ref, wt_ref, tf_ref, tb_ref) = refs[:4], refs[4:9]
    cores, backs, (scale_ref, odd_ref) = refs[9:11], refs[11:13], refs[13:15]
    ext_ref, pad_ref, back_ref, deep_ref = refs[15:]
    views = info_ref.shape[0] - INFO
    count = quarters[0].shape[0]
    extent = ext_ref.shape[0] // count
    strip = extent - 2 * HALO
    columns = ext_ref.shape[-1]
    group = planes * strip
    for p in range(count):
        for n, ref in enumerate(quarters[::-1]):
            ext_ref[p * extent + n * HALO : p * extent + (n + 1) * HALO, :] = ref[p]

    @pl.when(info_ref[2] == 0)
    def _():
        for p in range(count):
            ext_ref[(p + 1) * extent - HALO : (p + 1) * extent, :] = jnp.zeros((HALO, columns), BF16)

    for pad in (pad_ref, back_ref):
        pad[:, :LANES] = jnp.zeros((pad.shape[0], LANES), BF16)
        pad[:, LANES + columns :] = jnp.zeros((pad.shape[0], LANES), BF16)
    for first in range(0, columns, WIDE):
        block = jnp.dot(w_ref[...], ext_ref[:, first : first + WIDE], preferred_element_type=F32)
        pad_ref[:, LANES + first : LANES + first + WIDE] = block.astype(BF16)
    row = info_ref[3] + lax.broadcasted_iota(jnp.int32, (group, WIDE), 0) % strip
    coverage = jnp.zeros((strip, LANES), F32)
    starts = range(0, columns, WIDE)

    def windows(pad, rows):
        return jnp.concatenate([pad[rows, first : first + WIDE + 2 * LANES] for first in starts], axis=0)

    for view in range(views):
        rows = slice(view * group, (view + 1) * group)
        low = info_ref[INFO + view]
        inside = (row >= low) & (row < low + view_rows)
        coverage = coverage + jnp.where(inside[:strip, :LANES], 1.0, 0.0)
        blurred = jnp.dot(windows(pad_ref, rows), tf_ref[view], preferred_element_type=F32)
        for n, first in enumerate(starts):
            part = blurred[n * group : (n + 1) * group]
            seen = views_ref[rows, first : first + WIDE].astype(F32)
            correction = jnp.where(inside, seen / part - 1.0, 0.0)
            back_ref[rows, LANES + first : LANES + first + WIDE] = correction.astype(BF16)
        backward = jnp.dot(windows(back_ref, rows), tb_ref[view], preferred_element_type=F32)
        for n, first in enumerate(starts):
            deep_ref[rows, first : first + WIDE] = backward[n * group : (n + 1) * group].astype(BF16)
    for p in range(count):
        part = jnp.dot(wt_ref[p * extent : (p + 1) * extent], deep_ref[...], preferred_element_type=F32)
        write_coded(backs[0], (p, slice(None)), part[:HALO])
        cores[0][p] = part[HALO : 2 * HALO]
        cores[1][p] = part[2 * HALO : 3 * HALO]
        write_coded(backs[1], (p, slice(None)), part[3 * HALO :])
    scale_ref[...] = 1.0 / jnp.maximum(coverage, 1.0)
    odd_ref[...] = jnp.full(odd_ref.shape, info_ref[1], jnp.int32)

    @pl.when(info_ref[2] == 0)
    def _():
        backs[1][...] = jnp.zeros(backs[1].shape, BF16)


def join_kernel(planes, core_ref, other_ref, own_ref, *sends):
    columns = core_ref.shape[2]
    for p in range(core_ref.shape[0]):
        other = other_ref[p]
        parts = []
        for first in range(0, columns, LANES):
            parts.append(core_ref[p, :, first : first + LANES] + decoded(other, first))
        whole = jnp.concatenate(parts, axis=1)
        if p < planes:
            own_ref[p] = whole
        else:
            write_coded(sends[p // planes - 1], (p % planes, slice(None)), whole)


def update_kernel(estimate_ref, scale_ref, odd_ref, *refs):
    parts, out_ref = refs[:-1], refs[-1]
    planes, strip, columns = estimate_ref.shape
    half = len(parts) // 2
    odd = odd_ref[...] == 1
    for p in range(planes):
        for first in range(0, columns, LANES):
            lanes = slice(first, first + LANES)
            sums = []
            for own_ref, *others in (parts[:half], parts[half:]):
                total = own_ref[p, :, lanes]
                for ref in others:
                    total = total + decoded(ref[p], first)
                sums.append(total)
            inner, outer = sums
            for rows, total in (
                (slice(0, HALO), jnp.where(odd, inner, outer)),
                (slice(HALO, strip), jnp.where(odd, outer, inner)),
            ):
                out_ref[p, rows, lanes] = estimate_ref[p, rows, lanes] * (1.0 + total * scale_ref[rows, :])


def call(body, outs, scalars, arrays, scratch=(), flops=0, moved=0):
    return pl.pallas_call(
        body,
        out_shape=outs,
        in_specs=[pl.BlockSpec(memory_space=pltpu.SMEM)] * scalars
        + [pl.BlockSpec(memory_space=pltpu.VMEM)] * arrays,
        out_specs=jax.tree.map(lambda _: pl.BlockSpec(memory_space=pltpu.VMEM), outs),
        scratch_shapes=list(scratch),
        compiler_params=pltpu.CompilerParams(vmem_limit_bytes=VMEM_LIMIT),
        cost_estimate=pl.CostEstimate(flops=flops, bytes_accessed=moved, transcendentals=0),
    )


def shards(estimate, views, kernel_x, kernel_y, kernel_z, offsets):
    shape = jax.ShapeDtypeStruct
    depth, tiles = lax.axis_size("depth"), lax.axis_size("tile")
    planes, strip, columns = estimate.shape
    count = views.shape[0]
    extent = strip + 2 * HALO
    rows = count * planes * strip
    span = depth * planes * extent
    view_rows = 5 * strip * tiles // 8
    tile = lax.axis_index("tile").astype(jnp.int32)
    odd = tile % 2
    has_chip = ((tile > 0) & (tile < tiles - 1)).astype(jnp.int32)
    block_index = lax.axis_index("depth").astype(jnp.int32)
    info = jnp.concatenate([jnp.stack([block_index, odd, has_chip, tile * strip]), offsets])
    assert strip == 2 * HALO and tiles % 2 == 0

    def across(array, step):
        return lax.ppermute(array, "depth", [(i, i ^ step) for i in range(depth)])

    def beside(array):
        pairs = [(i, i - 1 + 2 * (i % 2)) for i in range(1, tiles - 1)]
        return lax.ppermute(array, "tile", [(0, 0), *pairs, (tiles - 1, tiles - 1)])

    def within(array):
        return lax.ppermute(array, "tile", [(i, i ^ 1) for i in range(tiles)])

    own = estimate.astype(BF16)
    early, late = own[:, :HALO], own[:, HALO:]
    outer_own, inner_own = jnp.where(odd == 1, late, early), jnp.where(odd == 1, early, late)
    outer = jnp.concatenate([outer_own] + [across(outer_own, step) for step in range(1, depth)], axis=0)
    other_chip = beside(outer)
    inner = jnp.concatenate([inner_own] + [across(inner_own, step) for step in range(1, depth)], axis=0)
    other_core = within(inner)
    w, wt, tf, tb = call(
        functools.partial(matrices_kernel, planes, strip),
        (shape((rows, span), BF16), shape((span, rows), BF16))
        + (shape((count, WIDE + 2 * LANES, WIDE), BF16),) * 2,
        1, 1, flops=10**8, moved=5 * 2**20,
    )(info, jnp.stack([kernel_x, kernel_y, kernel_z]))
    halves = (depth * planes, HALO, columns)
    inner, outer, to_core, to_chip, scale, odd_rows = call(
        functools.partial(main_kernel, planes, view_rows),
        (shape(halves, F32),) * 2 + (shape(halves, BF16),) * 2
        + (shape((strip, LANES), F32), shape((HALO, LANES), jnp.int32)),
        1, 9,
        scratch=(
            pltpu.VMEM((span, columns), BF16),
            pltpu.VMEM((rows, columns + 2 * LANES), BF16),
            pltpu.VMEM((rows, columns + 2 * LANES), BF16),
            pltpu.VMEM((rows, columns), BF16),
        ),
        flops=2 * 10**9, moved=10 * 2**20,
    )(info, other_chip, outer, inner, other_core, views.reshape(rows, columns), w, wt, tf, tb)
    block = (planes, HALO, columns)
    sums = []
    for core, other in ((inner, within(to_core)), (outer, beside(to_chip))):
        own_sum, *sends = call(
            functools.partial(join_kernel, planes),
            (shape(block, F32),) + (shape(block, BF16),) * (depth - 1),
            0, 2, flops=10**6, moved=3 * 2**20,
        )(core, other)
        sums += [own_sum] + [across(send, step + 1) for step, send in enumerate(sends)]
    return call(
        update_kernel,
        shape(estimate.shape, F32),
        0, 3 + 2 * depth, flops=10**6, moved=2**20,
    )(estimate, scale, odd_rows, *sums)


def solution(mesh):
    in_specs = (P("depth", "tile", None), P(None, "depth", "tile", None), P(), P(), P(), P())
    out_specs = P("depth", "tile", None)
    return jax.shard_map(shards, mesh=mesh, in_specs=in_specs, out_specs=out_specs, check_vma=False)
```

```python
import functools
import jax
import jax.numpy as jnp
from jax import lax
from jax.experimental import pallas as pl
from jax.experimental.pallas import tpu as pltpu
from jax.sharding import PartitionSpec as P

F32, BF16 = jnp.float32, jnp.bfloat16
HALO = 16
LANES = 128
WIDE = 256
INFO = 4
VMEM_LIMIT = 40 * 1024 * 1024


def select_taps(index, kernel):
    total = jnp.zeros((kernel.shape[0],) + index.shape[1:], F32)
    for tap in range(kernel.shape[1]):
        total = total + jnp.where(index == tap, kernel[:, tap : tap + 1], 0.0)
    return total


def slanted(row, rows):
    spread = jnp.broadcast_to(row, (rows, row.shape[1]))
    return pltpu.roll(spread, 0, 1, stride=1, stride_axis=0)


def matrices_kernel(planes, strip, device_ref, kernels_ref, w_ref, wt_ref, tf_ref, tb_ref):
    views, taps = kernels_ref.shape[1:]
    margin = taps // 2
    extent = strip + 2 * HALO
    kx, ky, kz = [kernels_ref[n] / jnp.sum(kernels_ref[n], axis=1, keepdims=True) for n in range(3)]
    lane = lax.broadcasted_iota(jnp.int32, (1, LANES), 1)
    x_row = select_taps(lane % extent - (HALO - margin), kx)
    near = jnp.where(lane < LANES // 2, lane, lane - LANES)
    forward_row = select_taps(margin - near, ky)
    backward_row = select_taps(margin + near, ky)
    column = lax.broadcasted_iota(jnp.int32, (1, w_ref.shape[1]), 1) // extent
    device, odd = device_ref[0], device_ref[1] == 1
    plane = (device ^ (column // planes)) * planes + column % planes
    spot = lax.broadcasted_iota(jnp.int32, (strip, LANES), 1) % extent
    z_rows = [select_taps(plane - (device * planes + own) + margin, kz) for own in range(planes)]
    for view in range(views):
        x_block = slanted(x_row[view : view + 1], strip)
        turned = x_block
        for quarter in range(extent // HALO):
            shift = extent - (2 * quarter + 1) * HALO
            moved = pltpu.roll(x_block, (LANES - shift) % LANES, 1)
            here = jnp.logical_and(spot // HALO == quarter, jnp.logical_not(odd))
            turned = jnp.where(here, moved, turned)
        x_block = turned
        x_block = jnp.concatenate([x_block] * (w_ref.shape[1] // LANES), axis=1)
        for own in range(planes):
            first = (view * planes + own) * strip
            block = x_block * z_rows[own][view : view + 1]
            w_ref[first : first + strip, :] = block.astype(BF16)
    wt_ref[...] = w_ref[...].astype(F32).T.astype(BF16)
    i = lax.broadcasted_iota(jnp.int32, (LANES, LANES), 0)
    j = lax.broadcasted_iota(jnp.int32, (LANES, LANES), 1)
    zeros = jnp.zeros((LANES, LANES), BF16)
    for view in range(views):
        for row, out in ((forward_row, tf_ref), (backward_row, tb_ref)):
            circle = slanted(row[view : view + 1], LANES)
            middle = jnp.where(jnp.abs(j - i) < LANES // 2, circle, 0.0).astype(BF16)
            earlier = jnp.where(i - j > LANES // 2, circle, 0.0).astype(BF16)
            later = jnp.where(j - i > LANES // 2, circle, 0.0).astype(BF16)
            grid = ((earlier, zeros), (middle, earlier), (later, middle), (zeros, later))
            for a, blocks in enumerate(grid):
                for b, block in enumerate(blocks):
                    out[view, a * LANES : (a + 1) * LANES, b * LANES : (b + 1) * LANES] = block


def write_coded(out_ref, where, values):
    pick = values.shape[-1] // 2 - LANES
    base = values[..., pick : pick + LANES].astype(BF16)
    wide = base.astype(F32)
    for first in range(0, values.shape[-1], LANES):
        part = values[..., first : first + LANES]
        part = base if first == pick else (part - wide).astype(BF16)
        out_ref[where + (slice(first, first + LANES),)] = part


def decoded(values, first):
    pick = values.shape[-1] // 2 - LANES
    base = values[..., pick : pick + LANES].astype(F32)
    if first == pick:
        return base
    return base + values[..., first : first + LANES].astype(F32)


def main_kernel(planes, view_rows, info_ref, *refs):
    quarters, (views_ref, w_ref, wt_ref, tf_ref, tb_ref) = refs[:4], refs[4:9]
    core_ref, inner_ref, *outer_refs, scale_ref, odd_ref = refs[9:17]
    ext_ref, pad_ref, back_ref, deep_ref = refs[17:]
    views = info_ref.shape[0] - INFO
    count = quarters[0].shape[0]
    extent = ext_ref.shape[0] // count
    strip = extent - 2 * HALO
    columns = ext_ref.shape[-1]
    group = planes * strip
    for p in range(count):
        for n, ref in enumerate(quarters[::-1]):
            ext_ref[p * extent + n * HALO : p * extent + (n + 1) * HALO, :] = ref[p]

    @pl.when(info_ref[2] == 0)
    def _():
        for p in range(count):
            ext_ref[(p + 1) * extent - HALO : (p + 1) * extent, :] = jnp.zeros((HALO, columns), BF16)

    for pad in (pad_ref, back_ref):
        pad[:, :LANES] = jnp.zeros((pad.shape[0], LANES), BF16)
        pad[:, LANES + columns :] = jnp.zeros((pad.shape[0], LANES), BF16)
    for first in range(0, columns, WIDE):
        block = jnp.dot(w_ref[...], ext_ref[:, first : first + WIDE], preferred_element_type=F32)
        pad_ref[:, LANES + first : LANES + first + WIDE] = block.astype(BF16)
    row = info_ref[3] + lax.broadcasted_iota(jnp.int32, (group, WIDE), 0) % strip
    coverage = jnp.zeros((strip, LANES), F32)
    starts = range(0, columns, WIDE)

    def windows(pad, rows):
        return jnp.concatenate([pad[rows, first : first + WIDE + 2 * LANES] for first in starts], axis=0)

    for view in range(views):
        rows = slice(view * group, (view + 1) * group)
        low = info_ref[INFO + view]
        inside = (row >= low) & (row < low + view_rows)
        coverage = coverage + jnp.where(inside[:strip, :LANES], 1.0, 0.0)
        blurred = jnp.dot(windows(pad_ref, rows), tf_ref[view], preferred_element_type=F32)
        for n, first in enumerate(starts):
            part = blurred[n * group : (n + 1) * group]
            seen = views_ref[rows, first : first + WIDE].astype(F32)
            correction = jnp.where(inside, seen / part - 1.0, 0.0)
            back_ref[rows, LANES + first : LANES + first + WIDE] = correction.astype(BF16)
        backward = jnp.dot(windows(back_ref, rows), tb_ref[view], preferred_element_type=F32)
        for n, first in enumerate(starts):
            deep_ref[rows, first : first + WIDE] = backward[n * group : (n + 1) * group].astype(BF16)
    for p in range(count):
        part = jnp.dot(wt_ref[p * extent : (p + 1) * extent], deep_ref[...], preferred_element_type=F32)
        write_coded(inner_ref, (p, slice(None)), part[:HALO])
        core_ref[p] = part[HALO : 2 * HALO]
        outer_refs[p // (count // 2)][p % (count // 2)] = part[2 * HALO : 3 * HALO]
        write_coded(outer_refs[2 + p // (count // 2)], (p % (count // 2), slice(None)), part[3 * HALO :])
    scale_ref[...] = 1.0 / jnp.maximum(coverage, 1.0)
    odd_ref[...] = jnp.full(odd_ref.shape, info_ref[1], jnp.int32)

    @pl.when(info_ref[2] == 0)
    def _():
        for ref in outer_refs[2:]:
            ref[...] = jnp.zeros(ref.shape, BF16)


def join_kernel(planes, kept, core_ref, other_ref, *outs):
    columns = core_ref.shape[2]
    for p in range(core_ref.shape[0]):
        other = other_ref[p]
        parts = []
        for first in range(0, columns, LANES):
            parts.append(core_ref[p, :, first : first + LANES] + decoded(other, first))
        whole = jnp.concatenate(parts, axis=1)
        if p < kept:
            outs[0][p] = whole
        else:
            write_coded(outs[p // planes], (p % planes, slice(None)), whole)


def update_kernel(estimate_ref, scale_ref, odd_ref, *refs):
    parts, out_ref = refs[:-1], refs[-1]
    planes, strip, columns = estimate_ref.shape
    half = len(parts) // 2
    odd = odd_ref[...] == 1
    for p in range(planes):
        for first in range(0, columns, LANES):
            lanes = slice(first, first + LANES)
            sums = []
            for own_ref, *others in (parts[:half], parts[half:]):
                total = own_ref[p, :, lanes]
                for ref in others:
                    total = total + decoded(ref[p], first)
                sums.append(total)
            inner, outer = sums
            for rows, total in (
                (slice(0, HALO), jnp.where(odd, inner, outer)),
                (slice(HALO, strip), jnp.where(odd, outer, inner)),
            ):
                out_ref[p, rows, lanes] = estimate_ref[p, rows, lanes] * (1.0 + total * scale_ref[rows, :])


def call(body, outs, scalars, arrays, scratch=(), flops=0, moved=0):
    return pl.pallas_call(
        body,
        out_shape=outs,
        in_specs=[pl.BlockSpec(memory_space=pltpu.SMEM)] * scalars
        + [pl.BlockSpec(memory_space=pltpu.VMEM)] * arrays,
        out_specs=jax.tree.map(lambda _: pl.BlockSpec(memory_space=pltpu.VMEM), outs),
        scratch_shapes=list(scratch),
        compiler_params=pltpu.CompilerParams(vmem_limit_bytes=VMEM_LIMIT),
        cost_estimate=pl.CostEstimate(flops=flops, bytes_accessed=moved, transcendentals=0),
    )


def shards(estimate, views, kernel_x, kernel_y, kernel_z, offsets):
    shape = jax.ShapeDtypeStruct
    depth, tiles = lax.axis_size("depth"), lax.axis_size("tile")
    planes, strip, columns = estimate.shape
    count = views.shape[0]
    extent = strip + 2 * HALO
    rows = count * planes * strip
    span = depth * planes * extent
    view_rows = 5 * strip * tiles // 8
    tile = lax.axis_index("tile").astype(jnp.int32)
    odd = tile % 2
    has_chip = ((tile > 0) & (tile < tiles - 1)).astype(jnp.int32)
    block_index = lax.axis_index("depth").astype(jnp.int32)
    info = jnp.concatenate([jnp.stack([block_index, odd, has_chip, tile * strip]), offsets])
    assert strip == 2 * HALO and tiles % 2 == 0

    def across(array, step):
        return lax.ppermute(array, "depth", [(i, i ^ step) for i in range(depth)])

    def beside(array):
        pairs = []
        for d in range(depth):
            pairs += [(i * depth + d, (i - 1 + 2 * (i % 2)) * depth + d) for i in range(1, tiles - 1)]
            pairs += [(i * depth + d, i * depth + (d ^ 1)) for i in (0, tiles - 1)]
        return lax.ppermute(array, ("tile", "depth"), pairs)

    def within(array):
        return lax.ppermute(array, "tile", [(i, i ^ 1) for i in range(tiles)])

    own = estimate.astype(BF16)
    early, late = own[:, :HALO], own[:, HALO:]
    outer_own, inner_own = jnp.where(odd == 1, late, early), jnp.where(odd == 1, early, late)
    outer = jnp.concatenate([outer_own] + [across(outer_own, step) for step in range(1, depth)], axis=0)
    other_chip = beside(outer)
    inner = jnp.concatenate([inner_own] + [across(inner_own, step) for step in range(1, depth)], axis=0)
    other_core = within(inner)
    w, wt, tf, tb = call(
        functools.partial(matrices_kernel, planes, strip),
        (shape((rows, span), BF16), shape((span, rows), BF16))
        + (shape((count, WIDE + 2 * LANES, WIDE), BF16),) * 2,
        1, 1, flops=10**8, moved=5 * 2**20,
    )(info, jnp.stack([kernel_x, kernel_y, kernel_z]))
    halves = (depth * planes, HALO, columns)
    quarter = (depth * planes // 2, HALO, columns)
    core, to_core, near, far, near_edge, far_edge, scale, odd_rows = call(
        functools.partial(main_kernel, planes, view_rows),
        (shape(halves, F32), shape(halves, BF16)) + (shape(quarter, F32),) * 2 + (shape(quarter, BF16),) * 2
        + (shape((strip, LANES), F32), shape((HALO, LANES), jnp.int32)),
        1, 9,
        scratch=(
            pltpu.VMEM((span, columns), BF16),
            pltpu.VMEM((rows, columns + 2 * LANES), BF16),
            pltpu.VMEM((rows, columns + 2 * LANES), BF16),
            pltpu.VMEM((rows, columns), BF16),
        ),
        flops=2 * 10**9, moved=10 * 2**20,
    )(info, other_chip, outer, inner, other_core, views.reshape(rows, columns), w, wt, tf, tb)
    block = (planes, HALO, columns)

    def joined(core, other, first, earlier=()):
        core, _ = lax.optimization_barrier((core, earlier))
        steps = range(first, first + core.shape[0] // planes)
        totals = call(
            functools.partial(join_kernel, planes, planes if first == 0 else 0),
            tuple(shape(block, BF16 if step else F32) for step in steps),
            0, 2, flops=10**6, moved=3 * 2**20,
        )(core, other)
        return totals, [across(total, step) if step else total for step, total in zip(steps, totals)]

    far_edge = beside(far_edge)
    totals, sums = joined(core, within(to_core), 0)
    totals, far = joined(far, far_edge, depth // 2, totals)
    sums += joined(near, beside(near_edge), 0, [totals, sums[2:]])[1] + far
    return call(
        update_kernel,
        shape(estimate.shape, F32),
        0, 3 + 2 * depth, flops=10**6, moved=2**20,
    )(estimate, scale, odd_rows, *sums)


def solution(mesh):
    in_specs = (P("depth", "tile", None), P(None, "depth", "tile", None), P(), P(), P(), P())
    out_specs = P("depth", "tile", None)
    return jax.shard_map(shards, mesh=mesh, in_specs=in_specs, out_specs=out_specs, check_vma=False)
```

```python
import functools
import jax
import jax.numpy as jnp
from jax import lax
from jax.experimental import pallas as pl
from jax.experimental.pallas import tpu as pltpu
from jax.sharding import PartitionSpec as P

F32, BF16 = jnp.float32, jnp.bfloat16
HALO = 16
LANES = 128
WIDE = 256
INFO = 4
VMEM_LIMIT = 40 * 1024 * 1024


def select_taps(index, kernel):
    total = jnp.zeros((kernel.shape[0],) + index.shape[1:], F32)
    for tap in range(kernel.shape[1]):
        total = total + jnp.where(index == tap, kernel[:, tap : tap + 1], 0.0)
    return total


def slanted(row, rows):
    spread = jnp.broadcast_to(row, (rows, row.shape[1]))
    return pltpu.roll(spread, 0, 1, stride=1, stride_axis=0)


def matrices_kernel(planes, strip, device_ref, kernels_ref, w_ref, wt_ref, tf_ref, tb_ref):
    views, taps = kernels_ref.shape[1:]
    margin = taps // 2
    extent = strip + 2 * HALO
    kx, ky, kz = [kernels_ref[n] / jnp.sum(kernels_ref[n], axis=1, keepdims=True) for n in range(3)]
    lane = lax.broadcasted_iota(jnp.int32, (1, LANES), 1)
    x_row = select_taps(lane % extent - (HALO - margin), kx)
    near = jnp.where(lane < LANES // 2, lane, lane - LANES)
    forward_row = select_taps(margin - near, ky)
    backward_row = select_taps(margin + near, ky)
    column = lax.broadcasted_iota(jnp.int32, (1, w_ref.shape[1]), 1) // extent
    device, odd = device_ref[0], device_ref[1] == 1
    plane = (device ^ (column // planes)) * planes + column % planes
    spot = lax.broadcasted_iota(jnp.int32, (strip, LANES), 1) % extent
    z_rows = [select_taps(plane - (device * planes + own) + margin, kz) for own in range(planes)]
    for view in range(views):
        x_block = slanted(x_row[view : view + 1], strip)
        turned = x_block
        for quarter in range(extent // HALO):
            shift = extent - (2 * quarter + 1) * HALO
            moved = pltpu.roll(x_block, (LANES - shift) % LANES, 1)
            here = jnp.logical_and(spot // HALO == quarter, jnp.logical_not(odd))
            turned = jnp.where(here, moved, turned)
        x_block = turned
        x_block = jnp.concatenate([x_block] * (w_ref.shape[1] // LANES), axis=1)
        for own in range(planes):
            first = (view * planes + own) * strip
            block = x_block * z_rows[own][view : view + 1]
            w_ref[first : first + strip, :] = block.astype(BF16)
    wt_ref[...] = w_ref[...].astype(F32).T.astype(BF16)
    i = lax.broadcasted_iota(jnp.int32, (LANES, LANES), 0)
    j = lax.broadcasted_iota(jnp.int32, (LANES, LANES), 1)
    zeros = jnp.zeros((LANES, LANES), BF16)
    for view in range(views):
        for row, out in ((forward_row, tf_ref), (backward_row, tb_ref)):
            circle = slanted(row[view : view + 1], LANES)
            middle = jnp.where(jnp.abs(j - i) < LANES // 2, circle, 0.0).astype(BF16)
            earlier = jnp.where(i - j > LANES // 2, circle, 0.0).astype(BF16)
            later = jnp.where(j - i > LANES // 2, circle, 0.0).astype(BF16)
            grid = ((earlier, zeros), (middle, earlier), (later, middle), (zeros, later))
            for a, blocks in enumerate(grid):
                for b, block in enumerate(blocks):
                    out[view, a * LANES : (a + 1) * LANES, b * LANES : (b + 1) * LANES] = block


def write_coded(out_ref, where, values):
    pick = values.shape[-1] // 2 - LANES
    base = values[..., pick : pick + LANES].astype(BF16)
    wide = base.astype(F32)
    for first in range(0, values.shape[-1], LANES):
        part = values[..., first : first + LANES]
        part = base if first == pick else (part - wide).astype(BF16)
        out_ref[where + (slice(first, first + LANES),)] = part


def decoded(values, first):
    pick = values.shape[-1] // 2 - LANES
    base = values[..., pick : pick + LANES].astype(F32)
    if first == pick:
        return base
    return base + values[..., first : first + LANES].astype(F32)


def main_kernel(planes, view_rows, info_ref, *refs):
    quarters, (views_ref, w_ref, wt_ref, tf_ref, tb_ref) = refs[:4], refs[4:9]
    core_ref, inner_ref, *outer_refs, scale_ref, odd_ref = refs[9:17]
    ext_ref, pad_ref, back_ref, deep_ref = refs[17:]
    views = info_ref.shape[0] - INFO
    count = quarters[0].shape[0]
    extent = ext_ref.shape[0] // count
    strip = extent - 2 * HALO
    columns = ext_ref.shape[-1]
    group = planes * strip
    for p in range(count):
        for n, ref in enumerate(quarters[::-1]):
            ext_ref[p * extent + n * HALO : p * extent + (n + 1) * HALO, :] = ref[p]

    @pl.when(info_ref[2] == 0)
    def _():
        for p in range(count):
            ext_ref[(p + 1) * extent - HALO : (p + 1) * extent, :] = jnp.zeros((HALO, columns), BF16)

    for pad in (pad_ref, back_ref):
        pad[:, :LANES] = jnp.zeros((pad.shape[0], LANES), BF16)
        pad[:, LANES + columns :] = jnp.zeros((pad.shape[0], LANES), BF16)
    for first in range(0, columns, WIDE):
        block = jnp.dot(w_ref[...], ext_ref[:, first : first + WIDE], preferred_element_type=F32)
        pad_ref[:, LANES + first : LANES + first + WIDE] = block.astype(BF16)
    row = info_ref[3] + lax.broadcasted_iota(jnp.int32, (group, WIDE), 0) % strip
    coverage = jnp.zeros((strip, LANES), F32)
    starts = range(0, columns, WIDE)

    def windows(pad, rows):
        return jnp.concatenate([pad[rows, first : first + WIDE + 2 * LANES] for first in starts], axis=0)

    for view in range(views):
        rows = slice(view * group, (view + 1) * group)
        low = info_ref[INFO + view]
        inside = (row >= low) & (row < low + view_rows)
        coverage = coverage + jnp.where(inside[:strip, :LANES], 1.0, 0.0)
        blurred = jnp.dot(windows(pad_ref, rows), tf_ref[view], preferred_element_type=F32)
        for n, first in enumerate(starts):
            part = blurred[n * group : (n + 1) * group]
            seen = views_ref[rows, first : first + WIDE].astype(F32)
            inverse = pl.reciprocal(part, approx=True)
            inverse = inverse * (2.0 - part * inverse)
            correction = jnp.where(inside, seen * inverse - 1.0, 0.0)
            back_ref[rows, LANES + first : LANES + first + WIDE] = correction.astype(BF16)
        backward = jnp.dot(windows(back_ref, rows), tb_ref[view], preferred_element_type=F32)
        for n, first in enumerate(starts):
            deep_ref[rows, first : first + WIDE] = backward[n * group : (n + 1) * group].astype(BF16)
    for p in range(count):
        part = jnp.dot(wt_ref[p * extent : (p + 1) * extent], deep_ref[...], preferred_element_type=F32)
        write_coded(inner_ref, (p, slice(None)), part[:HALO])
        core_ref[p] = part[HALO : 2 * HALO]
        outer_refs[p // (count // 2)][p % (count // 2)] = part[2 * HALO : 3 * HALO]
        write_coded(outer_refs[2 + p // (count // 2)], (p % (count // 2), slice(None)), part[3 * HALO :])
    scale_ref[...] = 1.0 / jnp.maximum(coverage, 1.0)
    odd_ref[...] = jnp.full(odd_ref.shape, info_ref[1], jnp.int32)

    @pl.when(info_ref[2] == 0)
    def _():
        for ref in outer_refs[2:]:
            ref[...] = jnp.zeros(ref.shape, BF16)


def join_kernel(planes, kept, core_ref, other_ref, *outs):
    columns = core_ref.shape[2]
    for p in range(core_ref.shape[0]):
        other = other_ref[p]
        parts = []
        for first in range(0, columns, LANES):
            parts.append(core_ref[p, :, first : first + LANES] + decoded(other, first))
        whole = jnp.concatenate(parts, axis=1)
        if p < kept:
            outs[0][p] = whole
        else:
            write_coded(outs[p // planes], (p % planes, slice(None)), whole)


def update_kernel(estimate_ref, scale_ref, odd_ref, *refs):
    parts, out_ref = refs[:-1], refs[-1]
    planes, strip, columns = estimate_ref.shape
    half = len(parts) // 2
    odd = odd_ref[...] == 1
    for p in range(planes):
        for first in range(0, columns, LANES):
            lanes = slice(first, first + LANES)
            sums = []
            for own_ref, *others in (parts[:half], parts[half:]):
                total = own_ref[p, :, lanes]
                for ref in others:
                    total = total + decoded(ref[p], first)
                sums.append(total)
            inner, outer = sums
            for rows, total in (
                (slice(0, HALO), jnp.where(odd, inner, outer)),
                (slice(HALO, strip), jnp.where(odd, outer, inner)),
            ):
                out_ref[p, rows, lanes] = estimate_ref[p, rows, lanes] * (1.0 + total * scale_ref[rows, :])


def call(body, outs, scalars, arrays, scratch=(), flops=0, moved=0):
    return pl.pallas_call(
        body,
        out_shape=outs,
        in_specs=[pl.BlockSpec(memory_space=pltpu.SMEM)] * scalars
        + [pl.BlockSpec(memory_space=pltpu.VMEM)] * arrays,
        out_specs=jax.tree.map(lambda _: pl.BlockSpec(memory_space=pltpu.VMEM), outs),
        scratch_shapes=list(scratch),
        compiler_params=pltpu.CompilerParams(vmem_limit_bytes=VMEM_LIMIT),
        cost_estimate=pl.CostEstimate(flops=flops, bytes_accessed=moved, transcendentals=0),
    )


def shards(estimate, views, kernel_x, kernel_y, kernel_z, offsets):
    shape = jax.ShapeDtypeStruct
    depth, tiles = lax.axis_size("depth"), lax.axis_size("tile")
    planes, strip, columns = estimate.shape
    count = views.shape[0]
    extent = strip + 2 * HALO
    rows = count * planes * strip
    span = depth * planes * extent
    view_rows = 5 * strip * tiles // 8
    tile = lax.axis_index("tile").astype(jnp.int32)
    odd = tile % 2
    has_chip = ((tile > 0) & (tile < tiles - 1)).astype(jnp.int32)
    block_index = lax.axis_index("depth").astype(jnp.int32)
    info = jnp.concatenate([jnp.stack([block_index, odd, has_chip, tile * strip]), offsets])
    assert strip == 2 * HALO and tiles % 2 == 0

    def across(array, step):
        return lax.ppermute(array, "depth", [(i, i ^ step) for i in range(depth)])

    def beside(array, along_depth):
        pairs = []
        for d in range(depth):
            for i in range(tiles):
                j, e = (i - 1 + 2 * (i % 2)) % tiles, d
                if along_depth and i in (0, tiles - 1):
                    j, e = i, d ^ 1
                pairs.append((i * depth + d, j * depth + e))
        return lax.ppermute(array, ("tile", "depth"), pairs)

    def within(array):
        return lax.ppermute(array, "tile", [(i, i ^ 1) for i in range(tiles)])

    own = estimate.astype(BF16)
    early, late = own[:, :HALO], own[:, HALO:]
    outer_own, inner_own = jnp.where(odd == 1, late, early), jnp.where(odd == 1, early, late)
    outer = [outer_own] + [across(outer_own, step) for step in range(1, depth)]
    inner_own, _ = lax.optimization_barrier((inner_own, outer[-1]))
    outer = jnp.concatenate(outer, axis=0)
    other_chip = beside(outer, True)
    inner = jnp.concatenate([inner_own] + [across(inner_own, step) for step in range(1, depth)], axis=0)
    other_core = within(inner)
    w, wt, tf, tb = call(
        functools.partial(matrices_kernel, planes, strip),
        (shape((rows, span), BF16), shape((span, rows), BF16))
        + (shape((count, WIDE + 2 * LANES, WIDE), BF16),) * 2,
        1, 1, flops=10**8, moved=5 * 2**20,
    )(info, jnp.stack([kernel_x, kernel_y, kernel_z]))
    halves = (depth * planes, HALO, columns)
    quarter = (depth * planes // 2, HALO, columns)
    core, to_core, near, far, near_edge, far_edge, scale, odd_rows = call(
        functools.partial(main_kernel, planes, view_rows),
        (shape(halves, F32), shape(halves, BF16)) + (shape(quarter, F32),) * 2 + (shape(quarter, BF16),) * 2
        + (shape((strip, LANES), F32), shape((HALO, LANES), jnp.int32)),
        1, 9,
        scratch=(
            pltpu.VMEM((span, columns), BF16),
            pltpu.VMEM((rows, columns + 2 * LANES), BF16),
            pltpu.VMEM((rows, columns + 2 * LANES), BF16),
            pltpu.VMEM((rows, columns), BF16),
        ),
        flops=2 * 10**9, moved=10 * 2**20,
    )(info, other_chip, outer, inner, other_core, views.reshape(rows, columns), w, wt, tf, tb)
    block = (planes, HALO, columns)

    def joined(core, other, first, earlier=()):
        core, _ = lax.optimization_barrier((core, earlier))
        steps = range(first, first + core.shape[0] // planes)
        totals = call(
            functools.partial(join_kernel, planes, planes if first == 0 else 0),
            tuple(shape(block, BF16 if step else F32) for step in steps),
            0, 2, flops=10**6, moved=3 * 2**20,
        )(core, other)
        return totals, [across(total, step) if step else total for step, total in zip(steps, totals)]

    far_edge = beside(far_edge, False)
    totals, sums = joined(core, within(to_core), 0)
    totals, far = joined(far, far_edge, depth // 2, totals)
    sums += joined(near, beside(near_edge, False), 0, [totals, sums[2:]])[1] + far
    return call(
        update_kernel,
        shape(estimate.shape, F32),
        0, 3 + 2 * depth, flops=10**6, moved=2**20,
    )(estimate, scale, odd_rows, *sums)


def solution(mesh):
    in_specs = (P("depth", "tile", None), P(None, "depth", "tile", None), P(), P(), P(), P())
    out_specs = P("depth", "tile", None)
    return jax.shard_map(shards, mesh=mesh, in_specs=in_specs, out_specs=out_specs, check_vma=False)
```

```python
import functools
import jax
import jax.numpy as jnp
from jax import lax
from jax.experimental import pallas as pl
from jax.experimental.pallas import tpu as pltpu
from jax.sharding import PartitionSpec as P

F32, BF16 = jnp.float32, jnp.bfloat16
HALO = 16
LANES = 128
WIDE = 256
INFO = 4
VMEM_LIMIT = 40 * 1024 * 1024


def select_taps(index, kernel):
    total = jnp.zeros((kernel.shape[0],) + index.shape[1:], F32)
    for tap in range(kernel.shape[1]):
        total = total + jnp.where(index == tap, kernel[:, tap : tap + 1], 0.0)
    return total


def slanted(row, rows):
    spread = jnp.broadcast_to(row, (rows, row.shape[1]))
    return pltpu.roll(spread, 0, 1, stride=1, stride_axis=0)


def matrices_kernel(planes, strip, device_ref, kernels_ref, w_ref, wt_ref, tf_ref, tb_ref):
    views, taps = kernels_ref.shape[1:]
    margin = taps // 2
    extent = strip + 2 * HALO
    kx, ky, kz = [kernels_ref[n] / jnp.sum(kernels_ref[n], axis=1, keepdims=True) for n in range(3)]
    lane = lax.broadcasted_iota(jnp.int32, (1, LANES), 1)
    x_row = select_taps(lane % extent - (HALO - margin), kx)
    near = jnp.where(lane < LANES // 2, lane, lane - LANES)
    forward_row = select_taps(margin - near, ky)
    backward_row = select_taps(margin + near, ky)
    column = lax.broadcasted_iota(jnp.int32, (1, w_ref.shape[1]), 1) // extent
    device, odd = device_ref[0], device_ref[1] == 1
    plane = (device ^ (column // planes)) * planes + column % planes
    spot = lax.broadcasted_iota(jnp.int32, (strip, LANES), 1) % extent
    z_rows = [select_taps(plane - (device * planes + own) + margin, kz) for own in range(planes)]
    for view in range(views):
        x_block = slanted(x_row[view : view + 1], strip)
        turned = x_block
        for quarter in range(extent // HALO):
            shift = extent - (2 * quarter + 1) * HALO
            moved = pltpu.roll(x_block, (LANES - shift) % LANES, 1)
            here = jnp.logical_and(spot // HALO == quarter, jnp.logical_not(odd))
            turned = jnp.where(here, moved, turned)
        x_block = turned
        x_block = jnp.concatenate([x_block] * (w_ref.shape[1] // LANES), axis=1)
        for own in range(planes):
            first = (view * planes + own) * strip
            block = x_block * z_rows[own][view : view + 1]
            w_ref[first : first + strip, :] = block.astype(BF16)
    wt_ref[...] = w_ref[...].astype(F32).T.astype(BF16)
    i = lax.broadcasted_iota(jnp.int32, (LANES, LANES), 0)
    j = lax.broadcasted_iota(jnp.int32, (LANES, LANES), 1)
    zeros = jnp.zeros((LANES, LANES), BF16)
    for view in range(views):
        for row, out in ((forward_row, tf_ref), (backward_row, tb_ref)):
            circle = slanted(row[view : view + 1], LANES)
            middle = jnp.where(jnp.abs(j - i) < LANES // 2, circle, 0.0).astype(BF16)
            earlier = jnp.where(i - j > LANES // 2, circle, 0.0).astype(BF16)
            later = jnp.where(j - i > LANES // 2, circle, 0.0).astype(BF16)
            grid = ((earlier, zeros), (middle, earlier), (later, middle), (zeros, later))
            for a, blocks in enumerate(grid):
                for b, block in enumerate(blocks):
                    out[view, a * LANES : (a + 1) * LANES, b * LANES : (b + 1) * LANES] = block


def write_coded(out_ref, where, values):
    pick = values.shape[-1] // 2 - LANES
    base = values[..., pick : pick + LANES].astype(BF16)
    wide = base.astype(F32)
    for first in range(0, values.shape[-1], LANES):
        part = values[..., first : first + LANES]
        part = base if first == pick else (part - wide).astype(BF16)
        out_ref[where + (slice(first, first + LANES),)] = part


def decoded(values, first):
    pick = values.shape[-1] // 2 - LANES
    base = values[..., pick : pick + LANES].astype(F32)
    if first == pick:
        return base
    return base + values[..., first : first + LANES].astype(F32)


def main_kernel(planes, view_rows, info_ref, *refs):
    quarters, (views_ref, w_ref, wt_ref, tf_ref, tb_ref) = refs[:4], refs[4:9]
    core_ref, inner_ref, *outer_refs, scale_ref, odd_ref = refs[9:17]
    ext_ref, pad_ref, back_ref, deep_ref = refs[17:]
    views = info_ref.shape[0] - INFO
    count = quarters[0].shape[0]
    extent = ext_ref.shape[0] // count
    strip = extent - 2 * HALO
    columns = ext_ref.shape[-1]
    group = planes * strip
    for p in range(count):
        for n, ref in enumerate(quarters[::-1]):
            ext_ref[p * extent + n * HALO : p * extent + (n + 1) * HALO, :] = ref[p]

    @pl.when(info_ref[2] == 0)
    def _():
        for p in range(count):
            ext_ref[(p + 1) * extent - HALO : (p + 1) * extent, :] = jnp.zeros((HALO, columns), BF16)

    for pad in (pad_ref, back_ref):
        pad[:, :LANES] = jnp.zeros((pad.shape[0], LANES), BF16)
        pad[:, LANES + columns :] = jnp.zeros((pad.shape[0], LANES), BF16)
    for first in range(0, columns, WIDE):
        block = jnp.dot(w_ref[...], ext_ref[:, first : first + WIDE], preferred_element_type=F32)
        pad_ref[:, LANES + first : LANES + first + WIDE] = block.astype(BF16)
    row = info_ref[3] + lax.broadcasted_iota(jnp.int32, (group, WIDE), 0) % strip
    coverage = jnp.zeros((strip, LANES), F32)
    starts = range(0, columns, WIDE)

    def windows(pad, rows):
        return jnp.concatenate([pad[rows, first : first + WIDE + 2 * LANES] for first in starts], axis=0)

    for view in range(views):
        rows = slice(view * group, (view + 1) * group)
        low = info_ref[INFO + view]
        inside = (row >= low) & (row < low + view_rows)
        coverage = coverage + jnp.where(inside[:strip, :LANES], 1.0, 0.0)
        blurred = jnp.dot(windows(pad_ref, rows), tf_ref[view], preferred_element_type=F32)
        for n, first in enumerate(starts):
            part = blurred[n * group : (n + 1) * group]
            seen = views_ref[rows, first : first + WIDE].astype(F32)
            inverse = pl.reciprocal(part, approx=True)
            inverse = inverse * (2.0 - part * inverse)
            correction = jnp.where(inside, seen * inverse - 1.0, 0.0)
            back_ref[rows, LANES + first : LANES + first + WIDE] = correction.astype(BF16)
        backward = jnp.dot(windows(back_ref, rows), tb_ref[view], preferred_element_type=F32)
        for n, first in enumerate(starts):
            deep_ref[rows, first : first + WIDE] = backward[n * group : (n + 1) * group].astype(BF16)
    for p in range(count):
        part = jnp.dot(wt_ref[p * extent : (p + 1) * extent], deep_ref[...], preferred_element_type=F32)
        write_coded(inner_ref, (p, slice(None)), part[:HALO])
        core_ref[p] = part[HALO : 2 * HALO]
        outer_refs[p // (count // 2)][p % (count // 2)] = part[2 * HALO : 3 * HALO]
        write_coded(outer_refs[2 + p // (count // 2)], (p % (count // 2), slice(None)), part[3 * HALO :])
    scale_ref[...] = 1.0 / jnp.maximum(coverage, 1.0)
    odd_ref[...] = jnp.full(odd_ref.shape, info_ref[1], jnp.int32)

    @pl.when(info_ref[2] == 0)
    def _():
        for ref in outer_refs[2:]:
            ref[...] = jnp.zeros(ref.shape, BF16)


def join_kernel(planes, kept, core_ref, other_ref, *outs):
    columns = core_ref.shape[2]
    for p in range(core_ref.shape[0]):
        other = other_ref[p]
        parts = []
        for first in range(0, columns, LANES):
            parts.append(core_ref[p, :, first : first + LANES] + decoded(other, first))
        whole = jnp.concatenate(parts, axis=1)
        if p < kept:
            outs[0][p] = whole
        else:
            write_coded(outs[p // planes], (p % planes, slice(None)), whole)


def update_kernel(estimate_ref, scale_ref, odd_ref, *refs):
    parts, out_ref = refs[:-1], refs[-1]
    planes, strip, columns = estimate_ref.shape
    half = len(parts) // 2
    odd = odd_ref[...] == 1
    for p in range(planes):
        for first in range(0, columns, LANES):
            lanes = slice(first, first + LANES)
            sums = []
            for own_ref, *others in (parts[:half], parts[half:]):
                total = own_ref[p, :, lanes]
                for ref in others:
                    total = total + decoded(ref[p], first)
                sums.append(total)
            inner, outer = sums
            for rows, total in (
                (slice(0, HALO), jnp.where(odd, inner, outer)),
                (slice(HALO, strip), jnp.where(odd, outer, inner)),
            ):
                out_ref[p, rows, lanes] = estimate_ref[p, rows, lanes] * (1.0 + total * scale_ref[rows, :])


def call(body, outs, scalars, arrays, scratch=(), flops=0, moved=0):
    return pl.pallas_call(
        body,
        out_shape=outs,
        in_specs=[pl.BlockSpec(memory_space=pltpu.SMEM)] * scalars
        + [pl.BlockSpec(memory_space=pltpu.VMEM)] * arrays,
        out_specs=jax.tree.map(lambda _: pl.BlockSpec(memory_space=pltpu.VMEM), outs),
        scratch_shapes=list(scratch),
        compiler_params=pltpu.CompilerParams(vmem_limit_bytes=VMEM_LIMIT),
        cost_estimate=pl.CostEstimate(flops=flops, bytes_accessed=moved, transcendentals=0),
    )


def shards(estimate, views, kernel_x, kernel_y, kernel_z, offsets):
    shape = jax.ShapeDtypeStruct
    depth, tiles = lax.axis_size("depth"), lax.axis_size("tile")
    planes, strip, columns = estimate.shape
    count = views.shape[0]
    extent = strip + 2 * HALO
    rows = count * planes * strip
    span = depth * planes * extent
    view_rows = 5 * strip * tiles // 8
    tile = lax.axis_index("tile").astype(jnp.int32)
    odd = tile % 2
    has_chip = ((tile > 0) & (tile < tiles - 1)).astype(jnp.int32)
    block_index = lax.axis_index("depth").astype(jnp.int32)
    info = jnp.concatenate([jnp.stack([block_index, odd, has_chip, tile * strip]), offsets])
    assert strip == 2 * HALO and tiles % 2 == 0

    def across(array, step):
        return lax.ppermute(array, "depth", [(i, i ^ step) for i in range(depth)])

    def beside(array, along_depth):
        pairs = []
        for d in range(depth):
            for i in range(tiles):
                j, e = (i - 1 + 2 * (i % 2)) % tiles, d
                if along_depth and i in (0, tiles - 1):
                    j, e = i, d ^ 1
                pairs.append((i * depth + d, j * depth + e))
        return lax.ppermute(array, ("tile", "depth"), pairs)

    def within(array):
        return lax.ppermute(array, "tile", [(i, i ^ 1) for i in range(tiles)])

    own = estimate.astype(BF16)
    early, late = own[:, :HALO], own[:, HALO:]
    outer_own, inner_own = jnp.where(odd == 1, late, early), jnp.where(odd == 1, early, late)
    outer = [outer_own] + [across(outer_own, step) for step in range(1, depth)]
    inner_own, _ = lax.optimization_barrier((inner_own, outer[-1]))
    outer = jnp.concatenate(outer, axis=0)
    other_chip = beside(outer, True)
    kernels, _ = lax.optimization_barrier((jnp.stack([kernel_x, kernel_y, kernel_z]), outer))
    w, wt, tf, tb = call(
        functools.partial(matrices_kernel, planes, strip),
        (shape((rows, span), BF16), shape((span, rows), BF16))
        + (shape((count, WIDE + 2 * LANES, WIDE), BF16),) * 2,
        1, 1, flops=10**8, moved=5 * 2**20,
    )(info, kernels)
    inner = [inner_own] + [across(inner_own, step) for step in range(1, depth)]
    inner, _ = lax.optimization_barrier((inner, w))
    inner = jnp.concatenate(inner, axis=0)
    other_core = within(inner)
    halves = (depth * planes, HALO, columns)
    quarter = (depth * planes // 2, HALO, columns)
    core, to_core, near, far, near_edge, far_edge, scale, odd_rows = call(
        functools.partial(main_kernel, planes, view_rows),
        (shape(halves, F32), shape(halves, BF16)) + (shape(quarter, F32),) * 2 + (shape(quarter, BF16),) * 2
        + (shape((strip, LANES), F32), shape((HALO, LANES), jnp.int32)),
        1, 9,
        scratch=(
            pltpu.VMEM((span, columns), BF16),
            pltpu.VMEM((rows, columns + 2 * LANES), BF16),
            pltpu.VMEM((rows, columns + 2 * LANES), BF16),
            pltpu.VMEM((rows, columns), BF16),
        ),
        flops=2 * 10**9, moved=10 * 2**20,
    )(info, other_chip, outer, inner, other_core, views.reshape(rows, columns), w, wt, tf, tb)
    block = (planes, HALO, columns)

    def joined(core, other, first, earlier=()):
        core, _ = lax.optimization_barrier((core, earlier))
        steps = range(first, first + core.shape[0] // planes)
        totals = call(
            functools.partial(join_kernel, planes, planes if first == 0 else 0),
            tuple(shape(block, BF16 if step else F32) for step in steps),
            0, 2, flops=10**6, moved=3 * 2**20,
        )(core, other)
        return totals, [across(total, step) if step else total for step, total in zip(steps, totals)]

    far_edge = beside(far_edge, False)
    totals, sums = joined(core, within(to_core), 0)
    totals, far = joined(far, far_edge, depth // 2, [totals, sums[1]])
    sums += joined(near, beside(near_edge, False), 0, [totals, sums[2:]])[1] + far
    return call(
        update_kernel,
        shape(estimate.shape, F32),
        0, 3 + 2 * depth, flops=10**6, moved=2**20,
    )(estimate, scale, odd_rows, *sums)


def solution(mesh):
    in_specs = (P("depth", "tile", None), P(None, "depth", "tile", None), P(), P(), P(), P())
    out_specs = P("depth", "tile", None)
    return jax.shard_map(shards, mesh=mesh, in_specs=in_specs, out_specs=out_specs, check_vma=False)
```

```python
import functools
import jax
import jax.numpy as jnp
from jax import lax
from jax.experimental import pallas as pl
from jax.experimental.pallas import tpu as pltpu
from jax.sharding import PartitionSpec as P

F32, BF16 = jnp.float32, jnp.bfloat16
HALO = 16
LANES = 128
WIDE = 256
INFO = 4
VMEM_LIMIT = 40 * 1024 * 1024


def select_taps(index, kernel):
    total = jnp.zeros((kernel.shape[0],) + index.shape[1:], F32)
    for tap in range(kernel.shape[1]):
        total = total + jnp.where(index == tap, kernel[:, tap : tap + 1], 0.0)
    return total


def slanted(row, rows):
    spread = jnp.broadcast_to(row, (rows, row.shape[1]))
    return pltpu.roll(spread, 0, 1, stride=1, stride_axis=0)


def matrices_kernel(planes, strip, device_ref, kernels_ref, w_ref, wt_ref, tf_ref, tb_ref):
    views, taps = kernels_ref.shape[1:]
    margin = taps // 2
    extent = strip + 2 * HALO
    kx, ky, kz = [kernels_ref[n] / jnp.sum(kernels_ref[n], axis=1, keepdims=True) for n in range(3)]
    lane = lax.broadcasted_iota(jnp.int32, (1, LANES), 1)
    x_row = select_taps(lane % extent - (HALO - margin), kx)
    near = jnp.where(lane < LANES // 2, lane, lane - LANES)
    forward_row = select_taps(margin - near, ky)
    backward_row = select_taps(margin + near, ky)
    column = lax.broadcasted_iota(jnp.int32, (1, w_ref.shape[1]), 1) // extent
    device, odd = device_ref[0], device_ref[1] == 1
    plane = (device ^ (column // planes)) * planes + column % planes
    spot = lax.broadcasted_iota(jnp.int32, (strip, LANES), 1) % extent
    z_rows = [select_taps(plane - (device * planes + own) + margin, kz) for own in range(planes)]
    for view in range(views):
        x_block = slanted(x_row[view : view + 1], strip)
        turned = x_block
        for quarter in range(extent // HALO):
            shift = extent - (2 * quarter + 1) * HALO
            moved = pltpu.roll(x_block, (LANES - shift) % LANES, 1)
            here = jnp.logical_and(spot // HALO == quarter, jnp.logical_not(odd))
            turned = jnp.where(here, moved, turned)
        x_block = turned
        x_block = jnp.concatenate([x_block] * (w_ref.shape[1] // LANES), axis=1)
        for own in range(planes):
            first = (view * planes + own) * strip
            block = x_block * z_rows[own][view : view + 1]
            w_ref[first : first + strip, :] = block.astype(BF16)
    wt_ref[...] = w_ref[...].astype(F32).T.astype(BF16)
    i = lax.broadcasted_iota(jnp.int32, (LANES, LANES), 0)
    j = lax.broadcasted_iota(jnp.int32, (LANES, LANES), 1)
    zeros = jnp.zeros((LANES, LANES), BF16)
    for view in range(views):
        for row, out in ((forward_row, tf_ref), (backward_row, tb_ref)):
            circle = slanted(row[view : view + 1], LANES)
            middle = jnp.where(jnp.abs(j - i) < LANES // 2, circle, 0.0).astype(BF16)
            earlier = jnp.where(i - j > LANES // 2, circle, 0.0).astype(BF16)
            later = jnp.where(j - i > LANES // 2, circle, 0.0).astype(BF16)
            grid = ((earlier, zeros), (middle, earlier), (later, middle), (zeros, later))
            for a, blocks in enumerate(grid):
                for b, block in enumerate(blocks):
                    out[view, a * LANES : (a + 1) * LANES, b * LANES : (b + 1) * LANES] = block


def write_coded(out_ref, where, values):
    pick = values.shape[-1] // 2 - LANES
    base = values[..., pick : pick + LANES].astype(BF16)
    wide = base.astype(F32)
    for first in range(0, values.shape[-1], LANES):
        part = values[..., first : first + LANES]
        part = base if first == pick else (part - wide).astype(BF16)
        out_ref[where + (slice(first, first + LANES),)] = part


def decoded(values, first):
    pick = values.shape[-1] // 2 - LANES
    base = values[..., pick : pick + LANES].astype(F32)
    if first == pick:
        return base
    return base + values[..., first : first + LANES].astype(F32)


def main_kernel(planes, view_rows, info_ref, *refs):
    quarters, (views_ref, w_ref, wt_ref, tf_ref, tb_ref) = refs[:4], refs[4:9]
    core_ref, inner_ref, *outer_refs, scale_ref, odd_ref = refs[9:17]
    ext_ref, pad_ref, back_ref, deep_ref = refs[17:]
    views = info_ref.shape[0] - INFO
    count = quarters[0].shape[0]
    extent = ext_ref.shape[0] // count
    strip = extent - 2 * HALO
    columns = ext_ref.shape[-1]
    group = planes * strip
    for p in range(count):
        for n, ref in enumerate(quarters[::-1]):
            ext_ref[p * extent + n * HALO : p * extent + (n + 1) * HALO, :] = ref[p]

    @pl.when(info_ref[2] == 0)
    def _():
        for p in range(count):
            ext_ref[(p + 1) * extent - HALO : (p + 1) * extent, :] = jnp.zeros((HALO, columns), BF16)

    for pad in (pad_ref, back_ref):
        pad[:, :LANES] = jnp.zeros((pad.shape[0], LANES), BF16)
        pad[:, LANES + columns :] = jnp.zeros((pad.shape[0], LANES), BF16)
    for first in range(0, columns, WIDE):
        block = jnp.dot(w_ref[...], ext_ref[:, first : first + WIDE], preferred_element_type=F32)
        pad_ref[:, LANES + first : LANES + first + WIDE] = block.astype(BF16)
    row = info_ref[3] + lax.broadcasted_iota(jnp.int32, (group, WIDE), 0) % strip
    coverage = jnp.zeros((strip, LANES), F32)
    starts = range(0, columns, WIDE)

    def windows(pad, rows):
        return jnp.concatenate([pad[rows, first : first + WIDE + 2 * LANES] for first in starts], axis=0)

    for view in range(views):
        rows = slice(view * group, (view + 1) * group)
        low = info_ref[INFO + view]
        inside = (row >= low) & (row < low + view_rows)
        coverage = coverage + jnp.where(inside[:strip, :LANES], 1.0, 0.0)
        blurred = jnp.dot(windows(pad_ref, rows), tf_ref[view], preferred_element_type=F32)
        for n, first in enumerate(starts):
            part = blurred[n * group : (n + 1) * group]
            seen = views_ref[rows, first : first + WIDE].astype(F32)
            inverse = pl.reciprocal(part, approx=True)
            inverse = inverse * (2.0 - part * inverse)
            correction = jnp.where(inside, seen * inverse - 1.0, 0.0)
            back_ref[rows, LANES + first : LANES + first + WIDE] = correction.astype(BF16)
        backward = jnp.dot(windows(back_ref, rows), tb_ref[view], preferred_element_type=F32)
        for n, first in enumerate(starts):
            deep_ref[rows, first : first + WIDE] = backward[n * group : (n + 1) * group].astype(BF16)
    for p in range(count):
        part = jnp.dot(wt_ref[p * extent : (p + 1) * extent], deep_ref[...], preferred_element_type=F32)
        write_coded(inner_ref, (p, slice(None)), part[:HALO])
        core_ref[p] = part[HALO : 2 * HALO]
        outer_refs[p // (count // 2)][p % (count // 2)] = part[2 * HALO : 3 * HALO]
        write_coded(outer_refs[2 + p // (count // 2)], (p % (count // 2), slice(None)), part[3 * HALO :])
    scale_ref[...] = 1.0 / jnp.maximum(coverage, 1.0)
    odd_ref[...] = jnp.full(odd_ref.shape, info_ref[1], jnp.int32)

    @pl.when(info_ref[2] == 0)
    def _():
        for ref in outer_refs[2:]:
            ref[...] = jnp.zeros(ref.shape, BF16)


def join_kernel(planes, kept, core_ref, other_ref, *outs):
    columns = core_ref.shape[2]
    for p in range(core_ref.shape[0]):
        other = other_ref[p]
        parts = []
        for first in range(0, columns, LANES):
            parts.append(core_ref[p, :, first : first + LANES] + decoded(other, first))
        whole = jnp.concatenate(parts, axis=1)
        if p < kept:
            outs[0][p] = whole
        else:
            write_coded(outs[p // planes], (p % planes, slice(None)), whole)


def update_kernel(estimate_ref, scale_ref, odd_ref, *refs):
    parts, out_ref = refs[:-1], refs[-1]
    planes, strip, columns = estimate_ref.shape
    half = len(parts) // 2
    odd = odd_ref[...] == 1
    for p in range(planes):
        for first in range(0, columns, LANES):
            lanes = slice(first, first + LANES)
            sums = []
            for own_ref, *others in (parts[:half], parts[half:]):
                total = own_ref[p, :, lanes]
                for ref in others:
                    total = total + decoded(ref[p], first)
                sums.append(total)
            inner, outer = sums
            for rows, total in (
                (slice(0, HALO), jnp.where(odd, inner, outer)),
                (slice(HALO, strip), jnp.where(odd, outer, inner)),
            ):
                out_ref[p, rows, lanes] = estimate_ref[p, rows, lanes] * (1.0 + total * scale_ref[rows, :])


def call(body, outs, scalars, arrays, scratch=(), flops=0, moved=0):
    return pl.pallas_call(
        body,
        out_shape=outs,
        in_specs=[pl.BlockSpec(memory_space=pltpu.SMEM)] * scalars
        + [pl.BlockSpec(memory_space=pltpu.VMEM)] * arrays,
        out_specs=jax.tree.map(lambda _: pl.BlockSpec(memory_space=pltpu.VMEM), outs),
        scratch_shapes=list(scratch),
        compiler_params=pltpu.CompilerParams(vmem_limit_bytes=VMEM_LIMIT),
        cost_estimate=pl.CostEstimate(flops=flops, bytes_accessed=moved, transcendentals=0),
    )


def shards(estimate, views, kernel_x, kernel_y, kernel_z, offsets):
    shape = jax.ShapeDtypeStruct
    depth, tiles = lax.axis_size("depth"), lax.axis_size("tile")
    planes, strip, columns = estimate.shape
    count = views.shape[0]
    extent = strip + 2 * HALO
    rows = count * planes * strip
    span = depth * planes * extent
    view_rows = 5 * strip * tiles // 8
    tile = lax.axis_index("tile").astype(jnp.int32)
    odd = tile % 2
    has_chip = ((tile > 0) & (tile < tiles - 1)).astype(jnp.int32)
    block_index = lax.axis_index("depth").astype(jnp.int32)
    info = jnp.concatenate([jnp.stack([block_index, odd, has_chip, tile * strip]), offsets])
    assert strip == 2 * HALO and tiles % 2 == 0

    def across(array, step):
        return lax.ppermute(array, "depth", [(i, i ^ step) for i in range(depth)])

    def beside(array, along_depth):
        pairs = []
        for d in range(depth):
            for i in range(tiles):
                j, e = (i - 1 + 2 * (i % 2)) % tiles, d
                if along_depth and i in (0, tiles - 1):
                    j, e = i, d ^ 1
                pairs.append((i * depth + d, j * depth + e))
        return lax.ppermute(array, ("tile", "depth"), pairs)

    def within(array):
        return lax.ppermute(array, "tile", [(i, i ^ 1) for i in range(tiles)])

    own = estimate.astype(BF16)
    early, late = own[:, :HALO], own[:, HALO:]
    outer_own, inner_own = jnp.where(odd == 1, late, early), jnp.where(odd == 1, early, late)
    outer = [outer_own] + [across(outer_own, step) for step in range(1, depth)]
    inner_own, _ = lax.optimization_barrier((inner_own, outer[-1]))
    outer = jnp.concatenate(outer, axis=0)
    other_chip = beside(outer, True)
    kernels, _ = lax.optimization_barrier((jnp.stack([kernel_x, kernel_y, kernel_z]), outer))
    w, wt, tf, tb = call(
        functools.partial(matrices_kernel, planes, strip),
        (shape((rows, span), BF16), shape((span, rows), BF16))
        + (shape((count, WIDE + 2 * LANES, WIDE), BF16),) * 2,
        1, 1, flops=10**8, moved=5 * 2**20,
    )(info, kernels)
    inner = [inner_own] + [across(inner_own, step) for step in range(1, depth)]
    inner, _ = lax.optimization_barrier((inner, w))
    inner = jnp.concatenate(inner, axis=0)
    other_core = within(inner)
    halves = (depth * planes, HALO, columns)
    quarter = (depth * planes // 2, HALO, columns)
    core, to_core, near, far, near_edge, far_edge, scale, odd_rows = call(
        functools.partial(main_kernel, planes, view_rows),
        (shape(halves, F32), shape(halves, BF16)) + (shape(quarter, F32),) * 2 + (shape(quarter, BF16),) * 2
        + (shape((strip, LANES), F32), shape((HALO, LANES), jnp.int32)),
        1, 9,
        scratch=(
            pltpu.VMEM((span, columns), BF16),
            pltpu.VMEM((rows, columns + 2 * LANES), BF16),
            pltpu.VMEM((rows, columns + 2 * LANES), BF16),
            pltpu.VMEM((rows, columns), BF16),
        ),
        flops=2 * 10**9, moved=10 * 2**20,
    )(info, other_chip, outer, inner, other_core, views.reshape(rows, columns), w, wt, tf, tb)
    block = (planes, HALO, columns)

    def joined(core, other, first, earlier=()):
        core, _ = lax.optimization_barrier((core, earlier))
        steps = range(first, first + core.shape[0] // planes)
        totals = call(
            functools.partial(join_kernel, planes, planes if first == 0 else 0),
            tuple(shape(block, BF16 if step else F32) for step in steps),
            0, 2, flops=10**6, moved=3 * 2**20,
        )(core, other)
        return totals, [across(total, step) if step else total for step, total in zip(steps, totals)]

    far_edge = beside(far_edge, False)
    totals, sums = joined(core, within(to_core), 0)
    totals, far = joined(far, far_edge, depth // 2, [totals, sums[1]])
    sums += joined(near, beside(near_edge, False), 0, [totals, sums[2]])[1] + far
    return call(
        update_kernel,
        shape(estimate.shape, F32),
        0, 3 + 2 * depth, flops=10**6, moved=2**20,
    )(estimate, scale, odd_rows, *sums)


def solution(mesh):
    in_specs = (P("depth", "tile", None), P(None, "depth", "tile", None), P(), P(), P(), P())
    out_specs = P("depth", "tile", None)
    return jax.shard_map(shards, mesh=mesh, in_specs=in_specs, out_specs=out_specs, check_vma=False)
```

```python
import functools
import jax
import jax.numpy as jnp
from jax import lax
from jax.experimental import pallas as pl
from jax.experimental.pallas import tpu as pltpu
from jax.sharding import PartitionSpec as P

F32, BF16 = jnp.float32, jnp.bfloat16
HALO = 16
LANES = 128
WIDE = 256
INFO = 4
VMEM_LIMIT = 40 * 1024 * 1024


def select_taps(index, kernel):
    total = jnp.zeros((kernel.shape[0],) + index.shape[1:], F32)
    for tap in range(kernel.shape[1]):
        total = total + jnp.where(index == tap, kernel[:, tap : tap + 1], 0.0)
    return total


def slanted(row, rows):
    spread = jnp.broadcast_to(row, (rows, row.shape[1]))
    return pltpu.roll(spread, 0, 1, stride=1, stride_axis=0)


def matrices_kernel(planes, strip, device_ref, kernels_ref, w_ref, wt_ref, tf_ref, tb_ref):
    views, taps = kernels_ref.shape[1:]
    margin = taps // 2
    extent = strip + 2 * HALO
    kx, ky, kz = [kernels_ref[n] / jnp.sum(kernels_ref[n], axis=1, keepdims=True) for n in range(3)]
    lane = lax.broadcasted_iota(jnp.int32, (1, LANES), 1)
    x_row = select_taps(lane % extent - (HALO - margin), kx)
    near = jnp.where(lane < LANES // 2, lane, lane - LANES)
    forward_row = select_taps(margin - near, ky)
    backward_row = select_taps(margin + near, ky)
    column = lax.broadcasted_iota(jnp.int32, (1, w_ref.shape[1]), 1) // extent
    device, odd = device_ref[0], device_ref[1] == 1
    plane = (device ^ (column // planes)) * planes + column % planes
    spot = lax.broadcasted_iota(jnp.int32, (strip, LANES), 1) % extent
    z_rows = [select_taps(plane - (device * planes + own) + margin, kz) for own in range(planes)]
    for view in range(views):
        x_block = slanted(x_row[view : view + 1], strip)
        turned = x_block
        for quarter in range(extent // HALO):
            shift = extent - (2 * quarter + 1) * HALO
            moved = pltpu.roll(x_block, (LANES - shift) % LANES, 1)
            here = jnp.logical_and(spot // HALO == quarter, jnp.logical_not(odd))
            turned = jnp.where(here, moved, turned)
        x_block = turned
        x_block = jnp.concatenate([x_block] * (w_ref.shape[1] // LANES), axis=1)
        for own in range(planes):
            first = (view * planes + own) * strip
            block = x_block * z_rows[own][view : view + 1]
            w_ref[first : first + strip, :] = block.astype(BF16)
    wt_ref[...] = w_ref[...].astype(F32).T.astype(BF16)
    i = lax.broadcasted_iota(jnp.int32, (LANES, LANES), 0)
    j = lax.broadcasted_iota(jnp.int32, (LANES, LANES), 1)
    zeros = jnp.zeros((LANES, LANES), BF16)
    for view in range(views):
        for row, out in ((forward_row, tf_ref), (backward_row, tb_ref)):
            circle = slanted(row[view : view + 1], LANES)
            middle = jnp.where(jnp.abs(j - i) < LANES // 2, circle, 0.0).astype(BF16)
            earlier = jnp.where(i - j > LANES // 2, circle, 0.0).astype(BF16)
            later = jnp.where(j - i > LANES // 2, circle, 0.0).astype(BF16)
            grid = ((earlier, zeros), (middle, earlier), (later, middle), (zeros, later))
            for a, blocks in enumerate(grid):
                for b, block in enumerate(blocks):
                    out[view, a * LANES : (a + 1) * LANES, b * LANES : (b + 1) * LANES] = block


def write_coded(out_ref, where, values):
    pick = values.shape[-1] // 2 - LANES
    base = values[..., pick : pick + LANES].astype(BF16)
    wide = base.astype(F32)
    for first in range(0, values.shape[-1], LANES):
        part = values[..., first : first + LANES]
        part = base if first == pick else (part - wide).astype(BF16)
        out_ref[where + (slice(first, first + LANES),)] = part


def decoded(values, first):
    pick = values.shape[-1] // 2 - LANES
    base = values[..., pick : pick + LANES].astype(F32)
    if first == pick:
        return base
    return base + values[..., first : first + LANES].astype(F32)


def main_kernel(planes, view_rows, info_ref, *refs):
    quarters, (views_ref, w_ref, wt_ref, tf_ref, tb_ref) = refs[:4], refs[4:9]
    core_ref, inner_ref, *outer_refs, scale_ref, odd_ref = refs[9:17]
    ext_ref, pad_ref, back_ref, deep_ref = refs[17:]
    views = info_ref.shape[0] - INFO
    count = quarters[0].shape[0]
    extent = ext_ref.shape[0] // count
    strip = extent - 2 * HALO
    columns = ext_ref.shape[-1]
    group = planes * strip
    for p in range(count):
        for n, ref in enumerate(quarters[::-1]):
            ext_ref[p * extent + n * HALO : p * extent + (n + 1) * HALO, :] = ref[p]

    @pl.when(info_ref[2] == 0)
    def _():
        for p in range(count):
            ext_ref[(p + 1) * extent - HALO : (p + 1) * extent, :] = jnp.zeros((HALO, columns), BF16)

    for pad in (pad_ref, back_ref):
        pad[:, :LANES] = jnp.zeros((pad.shape[0], LANES), BF16)
        pad[:, LANES + columns :] = jnp.zeros((pad.shape[0], LANES), BF16)
    for first in range(0, columns, WIDE):
        block = jnp.dot(w_ref[...], ext_ref[:, first : first + WIDE], preferred_element_type=F32)
        pad_ref[:, LANES + first : LANES + first + WIDE] = block.astype(BF16)
    row = info_ref[3] + lax.broadcasted_iota(jnp.int32, (group, WIDE), 0) % strip
    coverage = jnp.zeros((strip, LANES), F32)
    starts = range(0, columns, WIDE)

    def windows(pad, rows):
        return jnp.concatenate([pad[rows, first : first + WIDE + 2 * LANES] for first in starts], axis=0)

    for view in range(views):
        rows = slice(view * group, (view + 1) * group)
        low = info_ref[INFO + view]
        inside = (row >= low) & (row < low + view_rows)
        coverage = coverage + jnp.where(inside[:strip, :LANES], 1.0, 0.0)
        blurred = jnp.dot(windows(pad_ref, rows), tf_ref[view], preferred_element_type=F32)
        for n, first in enumerate(starts):
            part = blurred[n * group : (n + 1) * group]
            seen = views_ref[rows, first : first + WIDE].astype(F32)
            inverse = pl.reciprocal(part, approx=True)
            inverse = inverse * (2.0 - part * inverse)
            correction = jnp.where(inside, seen * inverse - 1.0, 0.0)
            back_ref[rows, LANES + first : LANES + first + WIDE] = correction.astype(BF16)
        backward = jnp.dot(windows(back_ref, rows), tb_ref[view], preferred_element_type=F32)
        for n, first in enumerate(starts):
            deep_ref[rows, first : first + WIDE] = backward[n * group : (n + 1) * group].astype(BF16)
    for p in range(count):
        part = jnp.dot(wt_ref[p * extent : (p + 1) * extent], deep_ref[...], preferred_element_type=F32)
        write_coded(inner_ref, (p, slice(None)), part[:HALO])
        core_ref[p] = part[HALO : 2 * HALO]
        outer_refs[p // (count // 2)][p % (count // 2)] = part[2 * HALO : 3 * HALO]
        write_coded(outer_refs[2 + p // (count // 2)], (p % (count // 2), slice(None)), part[3 * HALO :])
    scale_ref[...] = 1.0 / jnp.maximum(coverage, 1.0)
    odd_ref[...] = jnp.full(odd_ref.shape, info_ref[1], jnp.int32)

    @pl.when(info_ref[2] == 0)
    def _():
        for ref in outer_refs[2:]:
            ref[...] = jnp.zeros(ref.shape, BF16)


def join_kernel(planes, kept, core_ref, other_ref, *outs):
    columns = core_ref.shape[2]
    for p in range(core_ref.shape[0]):
        other = other_ref[p]
        parts = []
        for first in range(0, columns, LANES):
            parts.append(core_ref[p, :, first : first + LANES] + decoded(other, first))
        whole = jnp.concatenate(parts, axis=1)
        if p < kept:
            outs[0][p] = whole
        else:
            write_coded(outs[p // planes], (p % planes, slice(None)), whole)


def update_kernel(estimate_ref, scale_ref, odd_ref, *refs):
    parts, out_ref = refs[:-1], refs[-1]
    planes, strip, columns = estimate_ref.shape
    half = len(parts) // 2
    odd = odd_ref[...] == 1
    for p in range(planes):
        for first in range(0, columns, LANES):
            lanes = slice(first, first + LANES)
            sums = []
            for own_ref, *others in (parts[:half], parts[half:]):
                total = own_ref[p, :, lanes]
                for ref in others:
                    total = total + decoded(ref[p], first)
                sums.append(total)
            inner, outer = sums
            for rows, total in (
                (slice(0, HALO), jnp.where(odd, inner, outer)),
                (slice(HALO, strip), jnp.where(odd, outer, inner)),
            ):
                out_ref[p, rows, lanes] = estimate_ref[p, rows, lanes] * (1.0 + total * scale_ref[rows, :])


def call(body, outs, scalars, arrays, scratch=(), flops=0, moved=0):
    return pl.pallas_call(
        body,
        out_shape=outs,
        in_specs=[pl.BlockSpec(memory_space=pltpu.SMEM)] * scalars
        + [pl.BlockSpec(memory_space=pltpu.VMEM)] * arrays,
        out_specs=jax.tree.map(lambda _: pl.BlockSpec(memory_space=pltpu.VMEM), outs),
        scratch_shapes=list(scratch),
        compiler_params=pltpu.CompilerParams(vmem_limit_bytes=VMEM_LIMIT),
        cost_estimate=pl.CostEstimate(flops=flops, bytes_accessed=moved, transcendentals=0),
    )


def shards(estimate, views, kernel_x, kernel_y, kernel_z, offsets):
    shape = jax.ShapeDtypeStruct
    depth, tiles = lax.axis_size("depth"), lax.axis_size("tile")
    planes, strip, columns = estimate.shape
    count = views.shape[0]
    extent = strip + 2 * HALO
    rows = count * planes * strip
    span = depth * planes * extent
    view_rows = 5 * strip * tiles // 8
    tile = lax.axis_index("tile").astype(jnp.int32)
    odd = tile % 2
    has_chip = ((tile > 0) & (tile < tiles - 1)).astype(jnp.int32)
    block_index = lax.axis_index("depth").astype(jnp.int32)
    info = jnp.concatenate([jnp.stack([block_index, odd, has_chip, tile * strip]), offsets])
    assert strip == 2 * HALO and tiles % 2 == 0

    def across(array, step):
        return lax.ppermute(array, "depth", [(i, i ^ step) for i in range(depth)])

    def beside(array, along_depth):
        pairs = []
        for d in range(depth):
            for i in range(tiles):
                j, e = (i - 1 + 2 * (i % 2)) % tiles, d
                if along_depth and i in (0, tiles - 1):
                    j, e = i, d ^ 1
                pairs.append((i * depth + d, j * depth + e))
        return lax.ppermute(array, ("tile", "depth"), pairs)

    def within(array):
        return lax.ppermute(array, "tile", [(i, i ^ 1) for i in range(tiles)])

    own = estimate.astype(BF16)
    early, late = own[:, :HALO], own[:, HALO:]
    outer_own, inner_own = jnp.where(odd == 1, late, early), jnp.where(odd == 1, early, late)
    outer = [outer_own] + [across(outer_own, step) for step in range(1, depth)]
    kernels = jnp.stack([kernel_x, kernel_y, kernel_z])
    outer, *_ = lax.optimization_barrier((outer, kernels, info))
    first, _ = lax.optimization_barrier((inner_own, outer[-1]))
    outer = jnp.concatenate(outer, axis=0)
    other_chip = beside(outer, True)
    second, _ = lax.optimization_barrier((first, outer))
    inner = [inner_own] + [across(second if step < depth - 1 else first, step) for step in range(1, depth)]
    kernels, _ = lax.optimization_barrier((kernels, outer))
    w, wt, tf, tb = call(
        functools.partial(matrices_kernel, planes, strip),
        (shape((rows, span), BF16), shape((span, rows), BF16))
        + (shape((count, WIDE + 2 * LANES, WIDE), BF16),) * 2,
        1, 1, flops=10**8, moved=5 * 2**20,
    )(info, kernels)
    inner, _ = lax.optimization_barrier((inner, (w, other_chip)))
    inner = jnp.concatenate(inner, axis=0)
    other_core = within(inner)
    halves = (depth * planes, HALO, columns)
    quarter = (depth * planes // 2, HALO, columns)
    core, to_core, near, far, near_edge, far_edge, scale, odd_rows = call(
        functools.partial(main_kernel, planes, view_rows),
        (shape(halves, F32), shape(halves, BF16)) + (shape(quarter, F32),) * 2 + (shape(quarter, BF16),) * 2
        + (shape((strip, LANES), F32), shape((HALO, LANES), jnp.int32)),
        1, 9,
        scratch=(
            pltpu.VMEM((span, columns), BF16),
            pltpu.VMEM((rows, columns + 2 * LANES), BF16),
            pltpu.VMEM((rows, columns + 2 * LANES), BF16),
            pltpu.VMEM((rows, columns), BF16),
        ),
        flops=2 * 10**9, moved=10 * 2**20,
    )(info, other_chip, outer, inner, other_core, views.reshape(rows, columns), w, wt, tf, tb)
    block = (planes, HALO, columns)

    def joined(core, other, first, earlier=()):
        core, _ = lax.optimization_barrier((core, earlier))
        steps = range(first, first + core.shape[0] // planes)
        totals = call(
            functools.partial(join_kernel, planes, planes if first == 0 else 0),
            tuple(shape(block, BF16 if step else F32) for step in steps),
            0, 2, flops=10**6, moved=3 * 2**20,
        )(core, other)
        return totals, [across(total, step) if step else total for step, total in zip(steps, totals)]

    far_edge = beside(far_edge, False)
    totals, sums = joined(core, within(to_core), 0)
    totals, far = joined(far, far_edge, depth // 2, [totals, sums[1]])
    sums += joined(near, beside(near_edge, False), 0, [totals, sums[2]])[1] + far
    return call(
        update_kernel,
        shape(estimate.shape, F32),
        0, 3 + 2 * depth, flops=10**6, moved=2**20,
    )(estimate, scale, odd_rows, *sums)


def solution(mesh):
    in_specs = (P("depth", "tile", None), P(None, "depth", "tile", None), P(), P(), P(), P())
    out_specs = P("depth", "tile", None)
    return jax.shard_map(shards, mesh=mesh, in_specs=in_specs, out_specs=out_specs, check_vma=False)
```

```python
import functools
import jax
import jax.numpy as jnp
from jax import lax
from jax.experimental import pallas as pl
from jax.experimental.pallas import tpu as pltpu
from jax.sharding import PartitionSpec as P

F32, BF16 = jnp.float32, jnp.bfloat16
HALO = 16
LANES = 128
WIDE = 256
INFO = 4
VMEM_LIMIT = 40 * 1024 * 1024


def select_taps(index, kernel):
    total = jnp.zeros((kernel.shape[0],) + index.shape[1:], F32)
    for tap in range(kernel.shape[1]):
        total = total + jnp.where(index == tap, kernel[:, tap : tap + 1], 0.0)
    return total


def slanted(row, rows):
    spread = jnp.broadcast_to(row, (rows, row.shape[1]))
    return pltpu.roll(spread, 0, 1, stride=1, stride_axis=0)


def matrices_kernel(planes, strip, device_ref, kernels_ref, w_ref, wt_ref, tf_ref, tb_ref):
    views, taps = kernels_ref.shape[1:]
    margin = taps // 2
    extent = strip + 2 * HALO
    kx, ky, kz = [kernels_ref[n] / jnp.sum(kernels_ref[n], axis=1, keepdims=True) for n in range(3)]
    lane = lax.broadcasted_iota(jnp.int32, (1, LANES), 1)
    x_row = select_taps(lane % extent - (HALO - margin), kx)
    near = jnp.where(lane < LANES // 2, lane, lane - LANES)
    forward_row = select_taps(margin - near, ky)
    backward_row = select_taps(margin + near, ky)
    column = lax.broadcasted_iota(jnp.int32, (1, w_ref.shape[1]), 1) // extent
    device, odd = device_ref[0], device_ref[1] == 1
    plane = (device ^ (column // planes)) * planes + column % planes
    spot = lax.broadcasted_iota(jnp.int32, (strip, LANES), 1) % extent
    z_rows = [select_taps(plane - (device * planes + own) + margin, kz) for own in range(planes)]
    for view in range(views):
        x_block = slanted(x_row[view : view + 1], strip)
        turned = x_block
        for quarter in range(extent // HALO):
            shift = extent - (2 * quarter + 1) * HALO
            moved = pltpu.roll(x_block, (LANES - shift) % LANES, 1)
            here = jnp.logical_and(spot // HALO == quarter, jnp.logical_not(odd))
            turned = jnp.where(here, moved, turned)
        x_block = turned
        x_block = jnp.concatenate([x_block] * (w_ref.shape[1] // LANES), axis=1)
        for own in range(planes):
            first = (view * planes + own) * strip
            block = x_block * z_rows[own][view : view + 1]
            w_ref[first : first + strip, :] = block.astype(BF16)
    wt_ref[...] = w_ref[...].astype(F32).T.astype(BF16)
    i = lax.broadcasted_iota(jnp.int32, (LANES, LANES), 0)
    j = lax.broadcasted_iota(jnp.int32, (LANES, LANES), 1)
    zeros = jnp.zeros((LANES, LANES), BF16)
    for view in range(views):
        for row, out in ((forward_row, tf_ref), (backward_row, tb_ref)):
            circle = slanted(row[view : view + 1], LANES)
            middle = jnp.where(jnp.abs(j - i) < LANES // 2, circle, 0.0).astype(BF16)
            earlier = jnp.where(i - j > LANES // 2, circle, 0.0).astype(BF16)
            later = jnp.where(j - i > LANES // 2, circle, 0.0).astype(BF16)
            grid = ((earlier, zeros), (middle, earlier), (later, middle), (zeros, later))
            for a, blocks in enumerate(grid):
                for b, block in enumerate(blocks):
                    out[view, a * LANES : (a + 1) * LANES, b * LANES : (b + 1) * LANES] = block


def write_coded(out_ref, where, values):
    pick = values.shape[-1] // 2 - LANES
    base = values[..., pick : pick + LANES].astype(BF16)
    wide = base.astype(F32)
    for first in range(0, values.shape[-1], LANES):
        part = values[..., first : first + LANES]
        part = base if first == pick else (part - wide).astype(BF16)
        out_ref[where + (slice(first, first + LANES),)] = part


def decoded(values, first):
    pick = values.shape[-1] // 2 - LANES
    base = values[..., pick : pick + LANES].astype(F32)
    if first == pick:
        return base
    return base + values[..., first : first + LANES].astype(F32)


def main_kernel(planes, view_rows, info_ref, *refs):
    quarters, (views_ref, w_ref, wt_ref, tf_ref, tb_ref) = refs[:4], refs[4:9]
    core_ref, inner_ref, *outer_refs, scale_ref, odd_ref = refs[9:17]
    ext_ref, pad_ref, back_ref, deep_ref = refs[17:]
    views = info_ref.shape[0] - INFO
    count = quarters[0].shape[0]
    extent = ext_ref.shape[0] // count
    strip = extent - 2 * HALO
    columns = ext_ref.shape[-1]
    group = planes * strip
    for p in range(count):
        for n, ref in enumerate(quarters[::-1]):
            ext_ref[p * extent + n * HALO : p * extent + (n + 1) * HALO, :] = ref[p]

    @pl.when(info_ref[2] == 0)
    def _():
        for p in range(count):
            ext_ref[(p + 1) * extent - HALO : (p + 1) * extent, :] = jnp.zeros((HALO, columns), BF16)

    for pad in (pad_ref, back_ref):
        pad[:, :LANES] = jnp.zeros((pad.shape[0], LANES), BF16)
        pad[:, LANES + columns :] = jnp.zeros((pad.shape[0], LANES), BF16)
    for first in range(0, columns, WIDE):
        block = jnp.dot(w_ref[...], ext_ref[:, first : first + WIDE], preferred_element_type=F32)
        pad_ref[:, LANES + first : LANES + first + WIDE] = block.astype(BF16)
    row = info_ref[3] + lax.broadcasted_iota(jnp.int32, (group, WIDE), 0) % strip
    coverage = jnp.zeros((strip, LANES), F32)
    starts = range(0, columns, WIDE)

    def windows(pad, rows):
        return jnp.concatenate([pad[rows, first : first + WIDE + 2 * LANES] for first in starts], axis=0)

    for view in range(views):
        rows = slice(view * group, (view + 1) * group)
        low = info_ref[INFO + view]
        inside = (row >= low) & (row < low + view_rows)
        coverage = coverage + jnp.where(inside[:strip, :LANES], 1.0, 0.0)
        blurred = jnp.dot(windows(pad_ref, rows), tf_ref[view], preferred_element_type=F32)
        for n, first in enumerate(starts):
            part = blurred[n * group : (n + 1) * group]
            seen = views_ref[rows, first : first + WIDE].astype(F32)
            inverse = pl.reciprocal(part, approx=True)
            inverse = inverse * (2.0 - part * inverse)
            correction = jnp.where(inside, seen * inverse - 1.0, 0.0)
            back_ref[rows, LANES + first : LANES + first + WIDE] = correction.astype(BF16)
    for view in range(views):
        rows = slice(view * group, (view + 1) * group)
        backward = jnp.dot(windows(back_ref, rows), tb_ref[view], preferred_element_type=F32)
        for n, first in enumerate(starts):
            deep_ref[rows, first : first + WIDE] = backward[n * group : (n + 1) * group].astype(BF16)
    for p in range(count):
        part = jnp.dot(wt_ref[p * extent : (p + 1) * extent], deep_ref[...], preferred_element_type=F32)
        write_coded(inner_ref, (p, slice(None)), part[:HALO])
        core_ref[p] = part[HALO : 2 * HALO]
        outer_refs[p // (count // 2)][p % (count // 2)] = part[2 * HALO : 3 * HALO]
        write_coded(outer_refs[2 + p // (count // 2)], (p % (count // 2), slice(None)), part[3 * HALO :])
    scale_ref[...] = 1.0 / jnp.maximum(coverage, 1.0)
    odd_ref[...] = jnp.full(odd_ref.shape, info_ref[1], jnp.int32)

    @pl.when(info_ref[2] == 0)
    def _():
        for ref in outer_refs[2:]:
            ref[...] = jnp.zeros(ref.shape, BF16)


def join_kernel(planes, kept, core_ref, other_ref, *outs):
    columns = core_ref.shape[2]
    for p in range(core_ref.shape[0]):
        other = other_ref[p]
        parts = []
        for first in range(0, columns, LANES):
            parts.append(core_ref[p, :, first : first + LANES] + decoded(other, first))
        whole = jnp.concatenate(parts, axis=1)
        if p < kept:
            outs[0][p] = whole
        else:
            write_coded(outs[p // planes], (p % planes, slice(None)), whole)


def update_kernel(estimate_ref, scale_ref, odd_ref, *refs):
    parts, out_ref = refs[:-1], refs[-1]
    planes, strip, columns = estimate_ref.shape
    half = len(parts) // 2
    odd = odd_ref[...] == 1
    for p in range(planes):
        for first in range(0, columns, LANES):
            lanes = slice(first, first + LANES)
            sums = []
            for own_ref, *others in (parts[:half], parts[half:]):
                total = own_ref[p, :, lanes]
                for ref in others:
                    total = total + decoded(ref[p], first)
                sums.append(total)
            inner, outer = sums
            for rows, total in (
                (slice(0, HALO), jnp.where(odd, inner, outer)),
                (slice(HALO, strip), jnp.where(odd, outer, inner)),
            ):
                out_ref[p, rows, lanes] = estimate_ref[p, rows, lanes] * (1.0 + total * scale_ref[rows, :])


def call(body, outs, scalars, arrays, scratch=(), flops=0, moved=0):
    return pl.pallas_call(
        body,
        out_shape=outs,
        in_specs=[pl.BlockSpec(memory_space=pltpu.SMEM)] * scalars
        + [pl.BlockSpec(memory_space=pltpu.VMEM)] * arrays,
        out_specs=jax.tree.map(lambda _: pl.BlockSpec(memory_space=pltpu.VMEM), outs),
        scratch_shapes=list(scratch),
        compiler_params=pltpu.CompilerParams(vmem_limit_bytes=VMEM_LIMIT),
        cost_estimate=pl.CostEstimate(flops=flops, bytes_accessed=moved, transcendentals=0),
    )


def shards(estimate, views, kernel_x, kernel_y, kernel_z, offsets):
    shape = jax.ShapeDtypeStruct
    depth, tiles = lax.axis_size("depth"), lax.axis_size("tile")
    planes, strip, columns = estimate.shape
    count = views.shape[0]
    extent = strip + 2 * HALO
    rows = count * planes * strip
    span = depth * planes * extent
    view_rows = 5 * strip * tiles // 8
    tile = lax.axis_index("tile").astype(jnp.int32)
    odd = tile % 2
    has_chip = ((tile > 0) & (tile < tiles - 1)).astype(jnp.int32)
    block_index = lax.axis_index("depth").astype(jnp.int32)
    info = jnp.concatenate([jnp.stack([block_index, odd, has_chip, tile * strip]), offsets])
    assert strip == 2 * HALO and tiles % 2 == 0

    def across(array, step):
        return lax.ppermute(array, "depth", [(i, i ^ step) for i in range(depth)])

    def beside(array, along_depth):
        pairs = []
        for d in range(depth):
            for i in range(tiles):
                j, e = (i - 1 + 2 * (i % 2)) % tiles, d
                if along_depth and i in (0, tiles - 1):
                    j, e = i, d ^ 1
                pairs.append((i * depth + d, j * depth + e))
        return lax.ppermute(array, ("tile", "depth"), pairs)

    def within(array):
        return lax.ppermute(array, "tile", [(i, i ^ 1) for i in range(tiles)])

    own = estimate.astype(BF16)
    early, late = own[:, :HALO], own[:, HALO:]
    outer_own, inner_own = jnp.where(odd == 1, late, early), jnp.where(odd == 1, early, late)
    outer = [outer_own] + [across(outer_own, step) for step in range(1, depth)]
    inner_own, _ = lax.optimization_barrier((inner_own, outer[-1]))
    outer = jnp.concatenate(outer, axis=0)
    other_chip = beside(outer, True)
    kernels, _ = lax.optimization_barrier((jnp.stack([kernel_x, kernel_y, kernel_z]), outer))
    w, wt, tf, tb = call(
        functools.partial(matrices_kernel, planes, strip),
        (shape((rows, span), BF16), shape((span, rows), BF16))
        + (shape((count, WIDE + 2 * LANES, WIDE), BF16),) * 2,
        1, 1, flops=10**8, moved=5 * 2**20,
    )(info, kernels)
    inner = [inner_own] + [across(inner_own, step) for step in range(1, depth)]
    inner, _ = lax.optimization_barrier((inner, w))
    inner = jnp.concatenate(inner, axis=0)
    other_core = within(inner)
    halves = (depth * planes, HALO, columns)
    quarter = (depth * planes // 2, HALO, columns)
    core, to_core, near, far, near_edge, far_edge, scale, odd_rows = call(
        functools.partial(main_kernel, planes, view_rows),
        (shape(halves, F32), shape(halves, BF16)) + (shape(quarter, F32),) * 2 + (shape(quarter, BF16),) * 2
        + (shape((strip, LANES), F32), shape((HALO, LANES), jnp.int32)),
        1, 9,
        scratch=(
            pltpu.VMEM((span, columns), BF16),
            pltpu.VMEM((rows, columns + 2 * LANES), BF16),
            pltpu.VMEM((rows, columns + 2 * LANES), BF16),
            pltpu.VMEM((rows, columns), BF16),
        ),
        flops=2 * 10**9, moved=10 * 2**20,
    )(info, other_chip, outer, inner, other_core, views.reshape(rows, columns), w, wt, tf, tb)
    block = (planes, HALO, columns)

    def joined(core, other, first, earlier=()):
        core, _ = lax.optimization_barrier((core, earlier))
        steps = range(first, first + core.shape[0] // planes)
        totals = call(
            functools.partial(join_kernel, planes, planes if first == 0 else 0),
            tuple(shape(block, BF16 if step else F32) for step in steps),
            0, 2, flops=10**6, moved=3 * 2**20,
        )(core, other)
        return totals, [across(total, step) if step else total for step, total in zip(steps, totals)]

    far_edge = beside(far_edge, False)
    totals, sums = joined(core, within(to_core), 0)
    totals, far = joined(far, far_edge, depth // 2, [totals, sums[1]])
    sums += joined(near, beside(near_edge, False), 0, [totals, sums[2]])[1] + far
    return call(
        update_kernel,
        shape(estimate.shape, F32),
        0, 3 + 2 * depth, flops=10**6, moved=2**20,
    )(estimate, scale, odd_rows, *sums)


def solution(mesh):
    in_specs = (P("depth", "tile", None), P(None, "depth", "tile", None), P(), P(), P(), P())
    out_specs = P("depth", "tile", None)
    return jax.shard_map(shards, mesh=mesh, in_specs=in_specs, out_specs=out_specs, check_vma=False)
```

```python
import functools
import jax
import jax.numpy as jnp
from jax import lax
from jax.experimental import pallas as pl
from jax.experimental.pallas import tpu as pltpu
from jax.sharding import PartitionSpec as P

F32, BF16 = jnp.float32, jnp.bfloat16
HALO = 16
LANES = 128
WIDE = 256
INFO = 4
VMEM_LIMIT = 40 * 1024 * 1024


def select_taps(index, kernel):
    total = jnp.zeros((kernel.shape[0],) + index.shape[1:], F32)
    for tap in range(kernel.shape[1]):
        total = total + jnp.where(index == tap, kernel[:, tap : tap + 1], 0.0)
    return total


def slanted(row, rows):
    spread = jnp.broadcast_to(row, (rows, row.shape[1]))
    return pltpu.roll(spread, 0, 1, stride=1, stride_axis=0)


def matrices_kernel(planes, strip, device_ref, kernels_ref, w_ref, wt_ref, tf_ref, tb_ref):
    views, taps = kernels_ref.shape[1:]
    margin = taps // 2
    extent = strip + 2 * HALO
    kx, ky, kz = [kernels_ref[n] / jnp.sum(kernels_ref[n], axis=1, keepdims=True) for n in range(3)]
    lane = lax.broadcasted_iota(jnp.int32, (1, LANES), 1)
    x_row = select_taps(lane % extent - (HALO - margin), kx)
    near = jnp.where(lane < LANES // 2, lane, lane - LANES)
    forward_row = select_taps(margin - near, ky)
    backward_row = select_taps(margin + near, ky)
    column = lax.broadcasted_iota(jnp.int32, (1, w_ref.shape[1]), 1) // extent
    device, odd = device_ref[0], device_ref[1] == 1
    plane = (device ^ (column // planes)) * planes + column % planes
    spot = lax.broadcasted_iota(jnp.int32, (strip, LANES), 1) % extent
    z_rows = [select_taps(plane - (device * planes + own) + margin, kz) for own in range(planes)]
    for view in range(views):
        x_block = slanted(x_row[view : view + 1], strip)
        turned = x_block
        for quarter in range(extent // HALO):
            shift = extent - (2 * quarter + 1) * HALO
            moved = pltpu.roll(x_block, (LANES - shift) % LANES, 1)
            here = jnp.logical_and(spot // HALO == quarter, jnp.logical_not(odd))
            turned = jnp.where(here, moved, turned)
        x_block = turned
        x_block = jnp.concatenate([x_block] * (w_ref.shape[1] // LANES), axis=1)
        for own in range(planes):
            first = (view * planes + own) * strip
            block = x_block * z_rows[own][view : view + 1]
            w_ref[first : first + strip, :] = block.astype(BF16)
    wt_ref[...] = w_ref[...].astype(F32).T.astype(BF16)
    i = lax.broadcasted_iota(jnp.int32, (LANES, LANES), 0)
    j = lax.broadcasted_iota(jnp.int32, (LANES, LANES), 1)
    zeros = jnp.zeros((LANES, LANES), BF16)
    for view in range(views):
        for row, out in ((forward_row, tf_ref), (backward_row, tb_ref)):
            circle = slanted(row[view : view + 1], LANES)
            middle = jnp.where(jnp.abs(j - i) < LANES // 2, circle, 0.0).astype(BF16)
            earlier = jnp.where(i - j > LANES // 2, circle, 0.0).astype(BF16)
            later = jnp.where(j - i > LANES // 2, circle, 0.0).astype(BF16)
            grid = ((earlier, zeros), (middle, earlier), (later, middle), (zeros, later))
            for a, blocks in enumerate(grid):
                for b, block in enumerate(blocks):
                    out[view, a * LANES : (a + 1) * LANES, b * LANES : (b + 1) * LANES] = block


def write_coded(out_ref, where, values):
    pick = coded_base(values.shape[-1])
    base = values[..., pick : pick + LANES].astype(BF16)
    wide = base.astype(F32)
    for first in range(0, values.shape[-1], LANES):
        part = values[..., first : first + LANES]
        part = base if first == pick else (part - wide).astype(BF16)
        out_ref[where + (slice(first, first + LANES),)] = part


def coded_base(columns):
    return columns // 2 - LANES


def write_coded_part(out_ref, plane, values, first):
    pick = coded_base(out_ref.shape[-1])
    begins = range(first, first + values.shape[-1], LANES)
    for begin in sorted(begins, key=lambda begin: begin != pick):
        part = values[:, begin - first : begin - first + LANES]
        if begin != pick:
            part = part - out_ref[plane, :, pick : pick + LANES].astype(F32)
        out_ref[plane, :, begin : begin + LANES] = part.astype(BF16)


def decoded(values, first):
    pick = coded_base(values.shape[-1])
    base = values[..., pick : pick + LANES].astype(F32)
    if first == pick:
        return base
    return base + values[..., first : first + LANES].astype(F32)


def main_kernel(planes, view_rows, info_ref, *refs):
    quarters, (views_ref, w_ref, wt_ref, tf_ref, tb_ref) = refs[:4], refs[4:9]
    core_ref, inner_ref, *outer_refs, scale_ref, odd_ref = refs[9:17]
    ext_ref, pad_ref, back_ref, deep_ref = refs[17:]
    views = info_ref.shape[0] - INFO
    count = quarters[0].shape[0]
    extent = ext_ref.shape[0] // count
    strip = extent - 2 * HALO
    columns = ext_ref.shape[-1]
    group = planes * strip
    for p in range(count):
        for n, ref in enumerate(quarters[::-1]):
            ext_ref[p * extent + n * HALO : p * extent + (n + 1) * HALO, :] = ref[p]

    @pl.when(info_ref[2] == 0)
    def _():
        for p in range(count):
            ext_ref[(p + 1) * extent - HALO : (p + 1) * extent, :] = jnp.zeros((HALO, columns), BF16)

    for pad in (pad_ref, back_ref):
        pad[:, :LANES] = jnp.zeros((pad.shape[0], LANES), BF16)
        pad[:, LANES + columns :] = jnp.zeros((pad.shape[0], LANES), BF16)
    for first in range(0, columns, WIDE):
        block = jnp.dot(w_ref[...], ext_ref[:, first : first + WIDE], preferred_element_type=F32)
        pad_ref[:, LANES + first : LANES + first + WIDE] = block.astype(BF16)
    row = info_ref[3] + lax.broadcasted_iota(jnp.int32, (group, WIDE), 0) % strip
    coverage = jnp.zeros((strip, LANES), F32)
    starts = range(0, columns, WIDE)

    def windows(pad, rows):
        return jnp.concatenate([pad[rows, first : first + WIDE + 2 * LANES] for first in starts], axis=0)

    for view in range(views):
        rows = slice(view * group, (view + 1) * group)
        low = info_ref[INFO + view]
        inside = (row >= low) & (row < low + view_rows)
        coverage = coverage + jnp.where(inside[:strip, :LANES], 1.0, 0.0)
        blurred = jnp.dot(windows(pad_ref, rows), tf_ref[view], preferred_element_type=F32)
        for n, first in enumerate(starts):
            part = blurred[n * group : (n + 1) * group]
            seen = views_ref[rows, first : first + WIDE].astype(F32)
            inverse = pl.reciprocal(part, approx=True)
            inverse = inverse * (2.0 - part * inverse)
            correction = jnp.where(inside, seen * inverse - 1.0, 0.0)
            back_ref[rows, LANES + first : LANES + first + WIDE] = correction.astype(BF16)
    for view in range(views):
        rows = slice(view * group, (view + 1) * group)
        backward = jnp.dot(windows(back_ref, rows), tb_ref[view], preferred_element_type=F32)
        for n, first in enumerate(starts):
            deep_ref[rows, first : first + WIDE] = backward[n * group : (n + 1) * group].astype(BF16)
    pick = coded_base(columns)
    for first in sorted(starts, key=lambda first: first // WIDE != pick // WIDE):
        block = jnp.dot(wt_ref[...], deep_ref[:, first : first + WIDE], preferred_element_type=F32)
        lanes = slice(first, first + WIDE)
        for p in range(count):
            half, slot = p // (count // 2), p % (count // 2)
            quarters = [block[p * extent + n * HALO : p * extent + (n + 1) * HALO] for n in range(4)]
            core_ref[p, :, lanes] = quarters[1]
            outer_refs[half][slot, :, lanes] = quarters[2]
            write_coded_part(inner_ref, p, quarters[0], first)
            write_coded_part(outer_refs[2 + half], slot, quarters[3], first)
    scale_ref[...] = 1.0 / jnp.maximum(coverage, 1.0)
    odd_ref[...] = jnp.full(odd_ref.shape, info_ref[1], jnp.int32)

    @pl.when(info_ref[2] == 0)
    def _():
        for ref in outer_refs[2:]:
            ref[...] = jnp.zeros(ref.shape, BF16)


def join_kernel(planes, kept, core_ref, other_ref, *outs):
    columns = core_ref.shape[2]
    for p in range(core_ref.shape[0]):
        other = other_ref[p]
        parts = []
        for first in range(0, columns, LANES):
            parts.append(core_ref[p, :, first : first + LANES] + decoded(other, first))
        whole = jnp.concatenate(parts, axis=1)
        if p < kept:
            outs[0][p] = whole
        else:
            write_coded(outs[p // planes], (p % planes, slice(None)), whole)


def update_kernel(estimate_ref, scale_ref, odd_ref, *refs):
    parts, out_ref = refs[:-1], refs[-1]
    planes, strip, columns = estimate_ref.shape
    half = len(parts) // 2
    odd = odd_ref[...] == 1
    for p in range(planes):
        for first in range(0, columns, LANES):
            lanes = slice(first, first + LANES)
            sums = []
            for own_ref, *others in (parts[:half], parts[half:]):
                total = own_ref[p, :, lanes]
                for ref in others:
                    total = total + decoded(ref[p], first)
                sums.append(total)
            inner, outer = sums
            for rows, total in (
                (slice(0, HALO), jnp.where(odd, inner, outer)),
                (slice(HALO, strip), jnp.where(odd, outer, inner)),
            ):
                out_ref[p, rows, lanes] = estimate_ref[p, rows, lanes] * (1.0 + total * scale_ref[rows, :])


def call(body, outs, scalars, arrays, scratch=(), flops=0, moved=0):
    return pl.pallas_call(
        body,
        out_shape=outs,
        in_specs=[pl.BlockSpec(memory_space=pltpu.SMEM)] * scalars
        + [pl.BlockSpec(memory_space=pltpu.VMEM)] * arrays,
        out_specs=jax.tree.map(lambda _: pl.BlockSpec(memory_space=pltpu.VMEM), outs),
        scratch_shapes=list(scratch),
        compiler_params=pltpu.CompilerParams(vmem_limit_bytes=VMEM_LIMIT),
        cost_estimate=pl.CostEstimate(flops=flops, bytes_accessed=moved, transcendentals=0),
    )


def shards(estimate, views, kernel_x, kernel_y, kernel_z, offsets):
    shape = jax.ShapeDtypeStruct
    depth, tiles = lax.axis_size("depth"), lax.axis_size("tile")
    planes, strip, columns = estimate.shape
    count = views.shape[0]
    extent = strip + 2 * HALO
    rows = count * planes * strip
    span = depth * planes * extent
    view_rows = 5 * strip * tiles // 8
    tile = lax.axis_index("tile").astype(jnp.int32)
    odd = tile % 2
    has_chip = ((tile > 0) & (tile < tiles - 1)).astype(jnp.int32)
    block_index = lax.axis_index("depth").astype(jnp.int32)
    info = jnp.concatenate([jnp.stack([block_index, odd, has_chip, tile * strip]), offsets])
    assert strip == 2 * HALO and tiles % 2 == 0

    def across(array, step):
        return lax.ppermute(array, "depth", [(i, i ^ step) for i in range(depth)])

    def beside(array, along_depth):
        pairs = []
        for d in range(depth):
            for i in range(tiles):
                j, e = (i - 1 + 2 * (i % 2)) % tiles, d
                if along_depth and i in (0, tiles - 1):
                    j, e = i, d ^ 1
                pairs.append((i * depth + d, j * depth + e))
        return lax.ppermute(array, ("tile", "depth"), pairs)

    def within(array):
        return lax.ppermute(array, "tile", [(i, i ^ 1) for i in range(tiles)])

    own = estimate.astype(BF16)
    early, late = own[:, :HALO], own[:, HALO:]
    outer_own, inner_own = jnp.where(odd == 1, late, early), jnp.where(odd == 1, early, late)
    outer = [outer_own] + [across(outer_own, step) for step in range(1, depth)]
    inner_own, _ = lax.optimization_barrier((inner_own, outer[-1]))
    outer = jnp.concatenate(outer, axis=0)
    other_chip = beside(outer, True)
    kernels, _ = lax.optimization_barrier((jnp.stack([kernel_x, kernel_y, kernel_z]), outer))
    w, wt, tf, tb = call(
        functools.partial(matrices_kernel, planes, strip),
        (shape((rows, span), BF16), shape((span, rows), BF16))
        + (shape((count, WIDE + 2 * LANES, WIDE), BF16),) * 2,
        1, 1, flops=10**8, moved=5 * 2**20,
    )(info, kernels)
    inner = [inner_own] + [across(inner_own, step) for step in range(1, depth)]
    inner, _ = lax.optimization_barrier((inner, w))
    inner = jnp.concatenate(inner, axis=0)
    other_core = within(inner)
    halves = (depth * planes, HALO, columns)
    quarter = (depth * planes // 2, HALO, columns)
    core, to_core, near, far, near_edge, far_edge, scale, odd_rows = call(
        functools.partial(main_kernel, planes, view_rows),
        (shape(halves, F32), shape(halves, BF16)) + (shape(quarter, F32),) * 2 + (shape(quarter, BF16),) * 2
        + (shape((strip, LANES), F32), shape((HALO, LANES), jnp.int32)),
        1, 9,
        scratch=(
            pltpu.VMEM((span, columns), BF16),
            pltpu.VMEM((rows, columns + 2 * LANES), BF16),
            pltpu.VMEM((rows, columns + 2 * LANES), BF16),
            pltpu.VMEM((rows, columns), BF16),
        ),
        flops=2 * 10**9, moved=10 * 2**20,
    )(info, other_chip, outer, inner, other_core, views.reshape(rows, columns), w, wt, tf, tb)
    block = (planes, HALO, columns)

    def joined(core, other, first, earlier=()):
        core, _ = lax.optimization_barrier((core, earlier))
        steps = range(first, first + core.shape[0] // planes)
        totals = call(
            functools.partial(join_kernel, planes, planes if first == 0 else 0),
            tuple(shape(block, BF16 if step else F32) for step in steps),
            0, 2, flops=10**6, moved=3 * 2**20,
        )(core, other)
        return totals, [across(total, step) if step else total for step, total in zip(steps, totals)]

    far_edge = beside(far_edge, False)
    totals, sums = joined(core, within(to_core), 0)
    totals, far = joined(far, far_edge, depth // 2, [totals, sums[1]])
    sums += joined(near, beside(near_edge, False), 0, [totals, sums[2]])[1] + far
    return call(
        update_kernel,
        shape(estimate.shape, F32),
        0, 3 + 2 * depth, flops=10**6, moved=2**20,
    )(estimate, scale, odd_rows, *sums)


def solution(mesh):
    in_specs = (P("depth", "tile", None), P(None, "depth", "tile", None), P(), P(), P(), P())
    out_specs = P("depth", "tile", None)
    return jax.shard_map(shards, mesh=mesh, in_specs=in_specs, out_specs=out_specs, check_vma=False)
```

```python
import functools
import jax
import jax.numpy as jnp
from jax import lax
from jax.experimental import pallas as pl
from jax.experimental.pallas import tpu as pltpu
from jax.sharding import PartitionSpec as P

F32, BF16 = jnp.float32, jnp.bfloat16
HALO = 16
LANES = 128
WIDE = 256
INFO = 4
VMEM_LIMIT = 40 * 1024 * 1024


def select_taps(index, kernel):
    total = jnp.zeros((kernel.shape[0],) + index.shape[1:], F32)
    for tap in range(kernel.shape[1]):
        total = total + jnp.where(index == tap, kernel[:, tap : tap + 1], 0.0)
    return total


def slanted(row, rows):
    spread = jnp.broadcast_to(row, (rows, row.shape[1]))
    return pltpu.roll(spread, 0, 1, stride=1, stride_axis=0)


def matrices_kernel(planes, strip, device_ref, kernels_ref, w_ref, wt_ref, tf_ref, tb_ref):
    views, taps = kernels_ref.shape[1:]
    margin = taps // 2
    extent = strip + 2 * HALO
    kx, ky, kz = [kernels_ref[n] / jnp.sum(kernels_ref[n], axis=1, keepdims=True) for n in range(3)]
    lane = lax.broadcasted_iota(jnp.int32, (1, LANES), 1)
    x_row = select_taps(lane % extent - (HALO - margin), kx)
    near = jnp.where(lane < LANES // 2, lane, lane - LANES)
    forward_row = select_taps(margin - near, ky)
    backward_row = select_taps(margin + near, ky)
    column = lax.broadcasted_iota(jnp.int32, (1, w_ref.shape[1]), 1) // extent
    device, odd = device_ref[0], device_ref[1] == 1
    plane = (device ^ (column // planes)) * planes + column % planes
    spot = lax.broadcasted_iota(jnp.int32, (strip, LANES), 1) % extent
    z_rows = [select_taps(plane - (device * planes + own) + margin, kz) for own in range(planes)]
    for view in range(views):
        x_block = slanted(x_row[view : view + 1], strip)
        turned = x_block
        for quarter in range(extent // HALO):
            shift = extent - (2 * quarter + 1) * HALO
            moved = pltpu.roll(x_block, (LANES - shift) % LANES, 1)
            here = jnp.logical_and(spot // HALO == quarter, jnp.logical_not(odd))
            turned = jnp.where(here, moved, turned)
        x_block = turned
        x_block = jnp.concatenate([x_block] * (w_ref.shape[1] // LANES), axis=1)
        for own in range(planes):
            first = (view * planes + own) * strip
            block = x_block * z_rows[own][view : view + 1]
            w_ref[first : first + strip, :] = block.astype(BF16)
    wt_ref[...] = w_ref[...].astype(F32).T.astype(BF16)
    i = lax.broadcasted_iota(jnp.int32, (LANES, LANES), 0)
    j = lax.broadcasted_iota(jnp.int32, (LANES, LANES), 1)
    zeros = jnp.zeros((LANES, LANES), BF16)
    for view in range(views):
        for row, out in ((forward_row, tf_ref), (backward_row, tb_ref)):
            circle = slanted(row[view : view + 1], LANES)
            middle = jnp.where(jnp.abs(j - i) < LANES // 2, circle, 0.0).astype(BF16)
            earlier = jnp.where(i - j > LANES // 2, circle, 0.0).astype(BF16)
            later = jnp.where(j - i > LANES // 2, circle, 0.0).astype(BF16)
            grid = ((earlier, zeros), (middle, earlier), (later, middle), (zeros, later))
            for a, blocks in enumerate(grid):
                for b, block in enumerate(blocks):
                    out[view, a * LANES : (a + 1) * LANES, b * LANES : (b + 1) * LANES] = block


def write_coded(out_ref, where, values):
    pick = coded_base(values.shape[-1])
    base = values[..., pick : pick + LANES].astype(BF16)
    wide = base.astype(F32)
    for first in range(0, values.shape[-1], LANES):
        part = values[..., first : first + LANES]
        part = base if first == pick else (part - wide).astype(BF16)
        out_ref[where + (slice(first, first + LANES),)] = part


def coded_base(columns):
    return columns // 2 - LANES


def write_coded_part(out_ref, plane, values, first):
    pick = coded_base(out_ref.shape[-1])
    begins = range(first, first + values.shape[-1], LANES)
    for begin in sorted(begins, key=lambda begin: begin != pick):
        part = values[:, begin - first : begin - first + LANES]
        if begin != pick:
            part = part - out_ref[plane, :, pick : pick + LANES].astype(F32)
        out_ref[plane, :, begin : begin + LANES] = part.astype(BF16)


def decoded(values, first):
    pick = coded_base(values.shape[-1])
    base = values[..., pick : pick + LANES].astype(F32)
    if first == pick:
        return base
    return base + values[..., first : first + LANES].astype(F32)


def main_kernel(planes, view_rows, info_ref, *refs):
    quarters, (views_ref, w_ref, wt_ref, tf_ref, tb_ref) = refs[:4], refs[4:9]
    core_ref, inner_ref, *outer_refs, scale_ref, odd_ref = refs[9:17]
    ext_ref, pad_ref, back_ref, deep_ref = refs[17:]
    views = info_ref.shape[0] - INFO
    count = quarters[0].shape[0]
    extent = ext_ref.shape[0] // count
    strip = extent - 2 * HALO
    columns = ext_ref.shape[-1]
    group = planes * strip
    for p in range(count):
        for n, ref in enumerate(quarters[::-1]):
            ext_ref[p * extent + n * HALO : p * extent + (n + 1) * HALO, :] = ref[p]

    @pl.when(info_ref[2] == 0)
    def _():
        for p in range(count):
            ext_ref[(p + 1) * extent - HALO : (p + 1) * extent, :] = jnp.zeros((HALO, columns), BF16)

    for pad in (pad_ref, back_ref):
        pad[:, :LANES] = jnp.zeros((pad.shape[0], LANES), BF16)
        pad[:, LANES + columns :] = jnp.zeros((pad.shape[0], LANES), BF16)
    for first in range(0, columns, WIDE):
        block = jnp.dot(w_ref[...], ext_ref[:, first : first + WIDE], preferred_element_type=F32)
        pad_ref[:, LANES + first : LANES + first + WIDE] = block.astype(BF16)
    row = info_ref[3] + lax.broadcasted_iota(jnp.int32, (group, WIDE), 0) % strip
    coverage = jnp.zeros((strip, LANES), F32)
    starts = range(0, columns, WIDE)

    def windows(pad, rows):
        return jnp.concatenate([pad[rows, first : first + WIDE + 2 * LANES] for first in starts], axis=0)

    for view in range(views):
        rows = slice(view * group, (view + 1) * group)
        low = info_ref[INFO + view]
        inside = (row >= low) & (row < low + view_rows)
        coverage = coverage + jnp.where(inside[:strip, :LANES], 1.0, 0.0)
        blurred = jnp.dot(windows(pad_ref, rows), tf_ref[view], preferred_element_type=F32)
        for n, first in enumerate(starts):
            part = blurred[n * group : (n + 1) * group]
            seen = views_ref[rows, first : first + WIDE].astype(F32)
            inverse = pl.reciprocal(part, approx=True)
            inverse = inverse * (2.0 - part * inverse)
            correction = jnp.where(inside, seen * inverse - 1.0, 0.0)
            back_ref[rows, LANES + first : LANES + first + WIDE] = correction.astype(BF16)
    for view in range(views):
        rows = slice(view * group, (view + 1) * group)
        backward = jnp.dot(windows(back_ref, rows), tb_ref[view], preferred_element_type=F32)
        for n, first in enumerate(starts):
            deep_ref[rows, first : first + WIDE] = backward[n * group : (n + 1) * group].astype(BF16)
    pick = coded_base(columns)
    for first in sorted(starts, key=lambda first: first // WIDE != pick // WIDE):
        block = jnp.dot(wt_ref[...], deep_ref[:, first : first + WIDE], preferred_element_type=F32)
        lanes = slice(first, first + WIDE)
        for p in range(count):
            half, slot = p // (count // 2), p % (count // 2)
            quarters = [block[p * extent + n * HALO : p * extent + (n + 1) * HALO] for n in range(4)]
            core_ref[p, :, lanes] = quarters[1]
            outer_refs[half][slot, :, lanes] = quarters[2]
            write_coded_part(inner_ref, p, quarters[0], first)
            write_coded_part(outer_refs[2 + half], slot, quarters[3], first)
    scale_ref[...] = 1.0 / jnp.maximum(coverage, 1.0)
    odd_ref[...] = jnp.full(odd_ref.shape, info_ref[1], jnp.int32)

    @pl.when(info_ref[2] == 0)
    def _():
        for ref in outer_refs[2:]:
            ref[...] = jnp.zeros(ref.shape, BF16)


def join_kernel(planes, kept, core_ref, other_ref, *outs):
    columns = core_ref.shape[2]
    for p in range(core_ref.shape[0]):
        other = other_ref[p]
        parts = []
        for first in range(0, columns, LANES):
            parts.append(core_ref[p, :, first : first + LANES] + decoded(other, first))
        whole = jnp.concatenate(parts, axis=1)
        if p < kept:
            outs[0][p] = whole
        else:
            write_coded(outs[p // planes], (p % planes, slice(None)), whole)


def update_kernel(estimate_ref, scale_ref, odd_ref, *refs):
    parts, out_ref = refs[:-1], refs[-1]
    planes, strip, columns = estimate_ref.shape
    half = len(parts) // 2
    odd = odd_ref[...] == 1
    for p in range(planes):
        for first in range(0, columns, LANES):
            lanes = slice(first, first + LANES)
            sums = []
            for own_ref, *others in (parts[:half], parts[half:]):
                total = own_ref[p, :, lanes]
                for ref in others:
                    total = total + decoded(ref[p], first)
                sums.append(total)
            inner, outer = sums
            for rows, total in (
                (slice(0, HALO), jnp.where(odd, inner, outer)),
                (slice(HALO, strip), jnp.where(odd, outer, inner)),
            ):
                out_ref[p, rows, lanes] = estimate_ref[p, rows, lanes] * (1.0 + total * scale_ref[rows, :])


def call(body, outs, scalars, arrays, scratch=(), flops=0, moved=0):
    return pl.pallas_call(
        body,
        out_shape=outs,
        in_specs=[pl.BlockSpec(memory_space=pltpu.SMEM)] * scalars
        + [pl.BlockSpec(memory_space=pltpu.VMEM)] * arrays,
        out_specs=jax.tree.map(lambda _: pl.BlockSpec(memory_space=pltpu.VMEM), outs),
        scratch_shapes=list(scratch),
        compiler_params=pltpu.CompilerParams(vmem_limit_bytes=VMEM_LIMIT),
        cost_estimate=pl.CostEstimate(flops=flops, bytes_accessed=moved, transcendentals=0),
    )


def shards(estimate, views, kernel_x, kernel_y, kernel_z, offsets):
    shape = jax.ShapeDtypeStruct
    depth, tiles = lax.axis_size("depth"), lax.axis_size("tile")
    planes, strip, columns = estimate.shape
    count = views.shape[0]
    extent = strip + 2 * HALO
    rows = count * planes * strip
    span = depth * planes * extent
    view_rows = 5 * strip * tiles // 8
    tile = lax.axis_index("tile").astype(jnp.int32)
    odd = tile % 2
    has_chip = ((tile > 0) & (tile < tiles - 1)).astype(jnp.int32)
    block_index = lax.axis_index("depth").astype(jnp.int32)
    info = jnp.concatenate([jnp.stack([block_index, odd, has_chip, tile * strip]), offsets])
    assert strip == 2 * HALO and tiles % 2 == 0

    def across(array, step):
        return lax.ppermute(array, "depth", [(i, i ^ step) for i in range(depth)])

    def beside(array, along_depth):
        pairs = []
        for d in range(depth):
            for i in range(tiles):
                j, e = (i - 1 + 2 * (i % 2)) % tiles, d
                if along_depth and i in (0, tiles - 1):
                    j, e = i, d ^ 1
                pairs.append((i * depth + d, j * depth + e))
        return lax.ppermute(array, ("tile", "depth"), pairs)

    def within(array):
        return lax.ppermute(array, "tile", [(i, i ^ 1) for i in range(tiles)])

    own = estimate.astype(BF16)
    early, late = own[:, :HALO], own[:, HALO:]
    outer_own, inner_own = jnp.where(odd == 1, late, early), jnp.where(odd == 1, early, late)
    outer = [outer_own] + [across(outer_own, step) for step in range(1, depth)]
    inner_own, _ = lax.optimization_barrier((inner_own, outer[-1]))
    outer = jnp.concatenate(outer, axis=0)
    other_chip = beside(outer, True)
    kernels, _ = lax.optimization_barrier((jnp.stack([kernel_x, kernel_y, kernel_z]), outer))
    w, wt, tf, tb = call(
        functools.partial(matrices_kernel, planes, strip),
        (shape((rows, span), BF16), shape((span, rows), BF16))
        + (shape((count, WIDE + 2 * LANES, WIDE), BF16),) * 2,
        1, 1, flops=10**8, moved=5 * 2**20,
    )(info, kernels)
    inner = [inner_own] + [across(inner_own, step) for step in range(1, depth)]
    inner, _ = lax.optimization_barrier((inner, w))
    inner = jnp.concatenate(inner, axis=0)
    other_core = within(inner)
    halves = (depth * planes, HALO, columns)
    quarter = (depth * planes // 2, HALO, columns)
    core, to_core, near, far, near_edge, far_edge, scale, odd_rows = call(
        functools.partial(main_kernel, planes, view_rows),
        (shape(halves, F32), shape(halves, BF16)) + (shape(quarter, F32),) * 2 + (shape(quarter, BF16),) * 2
        + (shape((strip, LANES), F32), shape((HALO, LANES), jnp.int32)),
        1, 9,
        scratch=(
            pltpu.VMEM((span, columns), BF16),
            pltpu.VMEM((rows, columns + 2 * LANES), BF16),
            pltpu.VMEM((rows, columns + 2 * LANES), BF16),
            pltpu.VMEM((rows, columns), BF16),
        ),
        flops=2 * 10**9, moved=10 * 2**20,
    )(info, other_chip, outer, inner, other_core, views.reshape(rows, columns), w, wt, tf, tb)
    block = (planes, HALO, columns)

    def joined(core, other, first, earlier=()):
        core, _ = lax.optimization_barrier((core, earlier))
        steps = range(first, first + core.shape[0] // planes)
        totals = call(
            functools.partial(join_kernel, planes, planes if first == 0 else 0),
            tuple(shape(block, BF16 if step else F32) for step in steps),
            0, 2, flops=10**6, moved=3 * 2**20,
        )(core, other)
        return totals, [across(total, step) if step else total for step, total in zip(steps, totals)]

    far_edge = beside(far_edge, False)
    totals, sums = joined(core, within(to_core), 0)
    totals, far = joined(far, far_edge, depth // 2, [totals, sums[depth - 1]])
    sums += joined(near, beside(near_edge, False), 0, [totals, sums[2]])[1] + far
    return call(
        update_kernel,
        shape(estimate.shape, F32),
        0, 3 + 2 * depth, flops=10**6, moved=2**20,
    )(estimate, scale, odd_rows, *sums)


def solution(mesh):
    in_specs = (P("depth", "tile", None), P(None, "depth", "tile", None), P(), P(), P(), P())
    out_specs = P("depth", "tile", None)
    return jax.shard_map(shards, mesh=mesh, in_specs=in_specs, out_specs=out_specs, check_vma=False)
```

```python
import functools
import jax
import jax.numpy as jnp
from jax import lax
from jax.experimental import pallas as pl
from jax.experimental.pallas import tpu as pltpu
from jax.sharding import PartitionSpec as P

F32, BF16 = jnp.float32, jnp.bfloat16
HALO = 16
LANES = 128
WIDE = 256
INFO = 4
VMEM_LIMIT = 40 * 1024 * 1024


def select_taps(index, kernel):
    total = jnp.zeros((kernel.shape[0],) + index.shape[1:], F32)
    for tap in range(kernel.shape[1]):
        total = total + jnp.where(index == tap, kernel[:, tap : tap + 1], 0.0)
    return total


def slanted(row, rows):
    spread = jnp.broadcast_to(row, (rows, row.shape[1]))
    return pltpu.roll(spread, 0, 1, stride=1, stride_axis=0)


def matrices_kernel(planes, strip, device_ref, kernels_ref, w_ref, wt_ref, tf_ref, tb_ref):
    views, taps = kernels_ref.shape[1:]
    margin = taps // 2
    extent = strip + 2 * HALO
    kx, ky, kz = [kernels_ref[n] / jnp.sum(kernels_ref[n], axis=1, keepdims=True) for n in range(3)]
    lane = lax.broadcasted_iota(jnp.int32, (1, LANES), 1)
    x_row = select_taps(lane % extent - (HALO - margin), kx)
    near = jnp.where(lane < LANES // 2, lane, lane - LANES)
    forward_row = select_taps(margin - near, ky)
    backward_row = select_taps(margin + near, ky)
    column = lax.broadcasted_iota(jnp.int32, (1, w_ref.shape[1]), 1) // extent
    device, odd = device_ref[0], device_ref[1] == 1
    plane = (device ^ (column // planes)) * planes + column % planes
    spot = lax.broadcasted_iota(jnp.int32, (strip, LANES), 1) % extent
    z_rows = [select_taps(plane - (device * planes + own) + margin, kz) for own in range(planes)]
    for view in range(views):
        x_block = slanted(x_row[view : view + 1], strip)
        turned = x_block
        for quarter in range(extent // HALO):
            shift = extent - (2 * quarter + 1) * HALO
            moved = pltpu.roll(x_block, (LANES - shift) % LANES, 1)
            here = jnp.logical_and(spot // HALO == quarter, jnp.logical_not(odd))
            turned = jnp.where(here, moved, turned)
        x_block = turned
        x_block = jnp.concatenate([x_block] * (w_ref.shape[1] // LANES), axis=1)
        for own in range(planes):
            first = (view * planes + own) * strip
            block = x_block * z_rows[own][view : view + 1]
            w_ref[first : first + strip, :] = block.astype(BF16)
    wt_ref[...] = w_ref[...].astype(F32).T.astype(BF16)
    i = lax.broadcasted_iota(jnp.int32, (LANES, LANES), 0)
    j = lax.broadcasted_iota(jnp.int32, (LANES, LANES), 1)
    zeros = jnp.zeros((LANES, LANES), BF16)
    for view in range(views):
        for row, out in ((forward_row, tf_ref), (backward_row, tb_ref)):
            circle = slanted(row[view : view + 1], LANES)
            middle = jnp.where(jnp.abs(j - i) < LANES // 2, circle, 0.0).astype(BF16)
            earlier = jnp.where(i - j > LANES // 2, circle, 0.0).astype(BF16)
            later = jnp.where(j - i > LANES // 2, circle, 0.0).astype(BF16)
            grid = ((earlier, zeros), (middle, earlier), (later, middle), (zeros, later))
            for a, blocks in enumerate(grid):
                for b, block in enumerate(blocks):
                    out[view, a * LANES : (a + 1) * LANES, b * LANES : (b + 1) * LANES] = block


def write_coded(out_ref, where, values):
    pick = coded_base(values.shape[-1])
    base = values[..., pick : pick + LANES].astype(BF16)
    wide = base.astype(F32)
    for first in range(0, values.shape[-1], LANES):
        part = values[..., first : first + LANES]
        part = base if first == pick else (part - wide).astype(BF16)
        out_ref[where + (slice(first, first + LANES),)] = part


def coded_base(columns):
    return columns // 2 - LANES


def write_coded_part(out_ref, plane, values, first):
    pick = coded_base(out_ref.shape[-1])
    begins = range(first, first + values.shape[-1], LANES)
    for begin in sorted(begins, key=lambda begin: begin != pick):
        part = values[:, begin - first : begin - first + LANES]
        if begin != pick:
            part = part - out_ref[plane, :, pick : pick + LANES].astype(F32)
        out_ref[plane, :, begin : begin + LANES] = part.astype(BF16)


def decoded(values, first):
    pick = coded_base(values.shape[-1])
    base = values[..., pick : pick + LANES].astype(F32)
    if first == pick:
        return base
    return base + values[..., first : first + LANES].astype(F32)


def main_kernel(planes, view_rows, info_ref, *refs):
    quarters, (views_ref, w_ref, wt_ref, tf_ref, tb_ref) = refs[:4], refs[4:9]
    core_ref, inner_ref, *outer_refs, scale_ref, odd_ref = refs[9:17]
    ext_ref, pad_ref, back_ref, deep_ref = refs[17:]
    views = info_ref.shape[0] - INFO
    count = quarters[0].shape[0]
    extent = ext_ref.shape[0] // count
    strip = extent - 2 * HALO
    columns = ext_ref.shape[-1]
    group = planes * strip
    for p in range(count):
        for n, ref in enumerate(quarters[::-1]):
            ext_ref[p * extent + n * HALO : p * extent + (n + 1) * HALO, :] = ref[p]

    @pl.when(info_ref[2] == 0)
    def _():
        for p in range(count):
            ext_ref[(p + 1) * extent - HALO : (p + 1) * extent, :] = jnp.zeros((HALO, columns), BF16)

    for pad in (pad_ref, back_ref):
        pad[:, :LANES] = jnp.zeros((pad.shape[0], LANES), BF16)
        pad[:, LANES + columns :] = jnp.zeros((pad.shape[0], LANES), BF16)
    for first in range(0, columns, WIDE):
        block = jnp.dot(w_ref[...], ext_ref[:, first : first + WIDE], preferred_element_type=F32)
        pad_ref[:, LANES + first : LANES + first + WIDE] = block.astype(BF16)
    row = info_ref[3] + lax.broadcasted_iota(jnp.int32, (group, WIDE), 0) % strip
    coverage = jnp.zeros((strip, LANES), F32)
    starts = range(0, columns, WIDE)

    def windows(pad, rows):
        return jnp.concatenate([pad[rows, first : first + WIDE + 2 * LANES] for first in starts], axis=0)

    for view in range(views):
        rows = slice(view * group, (view + 1) * group)
        low = info_ref[INFO + view]
        inside = (row >= low) & (row < low + view_rows)
        coverage = coverage + jnp.where(inside[:strip, :LANES], 1.0, 0.0)
        blurred = jnp.dot(windows(pad_ref, rows), tf_ref[view], preferred_element_type=F32)
        for n, first in enumerate(starts):
            part = blurred[n * group : (n + 1) * group]
            seen = views_ref[rows, first : first + WIDE].astype(F32)
            inverse = pl.reciprocal(part, approx=True)
            inverse = inverse * (2.0 - part * inverse)
            correction = jnp.where(inside, seen * inverse - 1.0, 0.0)
            back_ref[rows, LANES + first : LANES + first + WIDE] = correction.astype(BF16)
    for view in range(views):
        rows = slice(view * group, (view + 1) * group)
        backward = jnp.dot(windows(back_ref, rows), tb_ref[view], preferred_element_type=F32)
        for n, first in enumerate(starts):
            deep_ref[rows, first : first + WIDE] = backward[n * group : (n + 1) * group].astype(BF16)
    pick = coded_base(columns)
    for first in sorted(starts, key=lambda first: first // WIDE != pick // WIDE):
        block = jnp.dot(wt_ref[...], deep_ref[:, first : first + WIDE], preferred_element_type=F32)
        lanes = slice(first, first + WIDE)
        for p in range(count):
            half, slot = p // (count // 2), p % (count // 2)
            quarters = [block[p * extent + n * HALO : p * extent + (n + 1) * HALO] for n in range(4)]
            core_ref[p, :, lanes] = quarters[1]
            outer_refs[half][slot, :, lanes] = quarters[2]
            write_coded_part(inner_ref, p, quarters[0], first)
            write_coded_part(outer_refs[2 + half], slot, quarters[3], first)
    scale_ref[...] = 1.0 / jnp.maximum(coverage, 1.0)
    odd_ref[...] = jnp.full(odd_ref.shape, info_ref[1], jnp.int32)

    @pl.when(info_ref[2] == 0)
    def _():
        for ref in outer_refs[2:]:
            ref[...] = jnp.zeros(ref.shape, BF16)


def join_kernel(planes, kept, core_ref, other_ref, *outs):
    columns = core_ref.shape[2]
    for p in range(core_ref.shape[0]):
        other = other_ref[p]
        parts = []
        for first in range(0, columns, LANES):
            parts.append(core_ref[p, :, first : first + LANES] + decoded(other, first))
        whole = jnp.concatenate(parts, axis=1)
        if p < kept:
            outs[0][p] = whole
        else:
            write_coded(outs[p // planes], (p % planes, slice(None)), whole)


def update_kernel(estimate_ref, scale_ref, odd_ref, *refs):
    parts, out_ref = refs[:-1], refs[-1]
    planes, strip, columns = estimate_ref.shape
    half = len(parts) // 2
    odd = odd_ref[...] == 1
    for p in range(planes):
        for first in range(0, columns, LANES):
            lanes = slice(first, first + LANES)
            sums = []
            for own_ref, *others in (parts[:half], parts[half:]):
                total = own_ref[p, :, lanes]
                for ref in others:
                    total = total + decoded(ref[p], first)
                sums.append(total)
            inner, outer = sums
            for rows, total in (
                (slice(0, HALO), jnp.where(odd, inner, outer)),
                (slice(HALO, strip), jnp.where(odd, outer, inner)),
            ):
                out_ref[p, rows, lanes] = estimate_ref[p, rows, lanes] * (1.0 + total * scale_ref[rows, :])


def call(body, outs, scalars, arrays, scratch=(), flops=0, moved=0):
    return pl.pallas_call(
        body,
        out_shape=outs,
        in_specs=[pl.BlockSpec(memory_space=pltpu.SMEM)] * scalars
        + [pl.BlockSpec(memory_space=pltpu.VMEM)] * arrays,
        out_specs=jax.tree.map(lambda _: pl.BlockSpec(memory_space=pltpu.VMEM), outs),
        scratch_shapes=list(scratch),
        compiler_params=pltpu.CompilerParams(vmem_limit_bytes=VMEM_LIMIT),
        cost_estimate=pl.CostEstimate(flops=flops, bytes_accessed=moved, transcendentals=0),
    )


def shards(estimate, views, kernel_x, kernel_y, kernel_z, offsets):
    shape = jax.ShapeDtypeStruct
    depth, tiles = lax.axis_size("depth"), lax.axis_size("tile")
    planes, strip, columns = estimate.shape
    count = views.shape[0]
    extent = strip + 2 * HALO
    rows = count * planes * strip
    span = depth * planes * extent
    view_rows = 5 * strip * tiles // 8
    tile = lax.axis_index("tile").astype(jnp.int32)
    odd = tile % 2
    has_chip = ((tile > 0) & (tile < tiles - 1)).astype(jnp.int32)
    block_index = lax.axis_index("depth").astype(jnp.int32)
    info = jnp.concatenate([jnp.stack([block_index, odd, has_chip, tile * strip]), offsets])
    assert strip == 2 * HALO and tiles % 2 == 0

    def across(array, step):
        return lax.ppermute(array, "depth", [(i, i ^ step) for i in range(depth)])

    def beside(array, along_depth):
        pairs = []
        for d in range(depth):
            for i in range(tiles):
                j, e = (i - 1 + 2 * (i % 2)) % tiles, d
                if along_depth and i in (0, tiles - 1):
                    j, e = i, d ^ 1
                pairs.append((i * depth + d, j * depth + e))
        return lax.ppermute(array, ("tile", "depth"), pairs)

    def within(array):
        return lax.ppermute(array, "tile", [(i, i ^ 1) for i in range(tiles)])

    own = estimate.astype(BF16)
    early, late = own[:, :HALO], own[:, HALO:]
    outer_own, inner_own = jnp.where(odd == 1, late, early), jnp.where(odd == 1, early, late)
    outer = [outer_own] + [across(outer_own, step) for step in range(1, depth)]
    inner_own, _ = lax.optimization_barrier((inner_own, outer[-1]))
    outer = jnp.concatenate(outer, axis=0)
    other_chip = beside(outer, True)
    kernels, _ = lax.optimization_barrier((jnp.stack([kernel_x, kernel_y, kernel_z]), outer))
    w, wt, tf, tb = call(
        functools.partial(matrices_kernel, planes, strip),
        (shape((rows, span), BF16), shape((span, rows), BF16))
        + (shape((count, WIDE + 2 * LANES, WIDE), BF16),) * 2,
        1, 1, flops=10**8, moved=5 * 2**20,
    )(info, kernels)
    inner = [inner_own] + [across(inner_own, step) for step in range(1, depth)]
    inner, _ = lax.optimization_barrier((inner, w))
    inner = jnp.concatenate(inner, axis=0)
    other_core = within(inner)
    halves = (depth * planes, HALO, columns)
    quarter = (depth * planes // 2, HALO, columns)
    core, to_core, near, far, near_edge, far_edge, scale, odd_rows = call(
        functools.partial(main_kernel, planes, view_rows),
        (shape(halves, F32), shape(halves, BF16)) + (shape(quarter, F32),) * 2 + (shape(quarter, BF16),) * 2
        + (shape((strip, LANES), F32), shape((HALO, LANES), jnp.int32)),
        1, 9,
        scratch=(
            pltpu.VMEM((span, columns), BF16),
            pltpu.VMEM((rows, columns + 2 * LANES), BF16),
            pltpu.VMEM((rows, columns + 2 * LANES), BF16),
            pltpu.VMEM((rows, columns), BF16),
        ),
        flops=2 * 10**9, moved=10 * 2**20,
    )(info, other_chip, outer, inner, other_core, views.reshape(rows, columns), w, wt, tf, tb)
    block = (planes, HALO, columns)

    def joined(core, other, first, earlier=()):
        core, _ = lax.optimization_barrier((core, earlier))
        steps = range(first, first + core.shape[0] // planes)
        totals = call(
            functools.partial(join_kernel, planes, planes if first == 0 else 0),
            tuple(shape(block, BF16 if step else F32) for step in steps),
            0, 2, flops=10**6, moved=3 * 2**20,
        )(core, other)
        return totals, [across(total, step) if step else total for step, total in zip(steps, totals)]

    far_edge = beside(far_edge, False)
    totals, sums = joined(core, within(to_core), 0)
    totals, far = joined(far, far_edge, depth // 2, [totals, sums[1]])
    sums += joined(near, beside(near_edge, True), 0, [totals, sums[2]])[1] + far
    return call(
        update_kernel,
        shape(estimate.shape, F32),
        0, 3 + 2 * depth, flops=10**6, moved=2**20,
    )(estimate, scale, odd_rows, *sums)


def solution(mesh):
    in_specs = (P("depth", "tile", None), P(None, "depth", "tile", None), P(), P(), P(), P())
    out_specs = P("depth", "tile", None)
    return jax.shard_map(shards, mesh=mesh, in_specs=in_specs, out_specs=out_specs, check_vma=False)
```
